256 devices in a mesh: dp: 16 (over y, x_hi, core), tensor: 16 (over z, x_lo).
Axes of the slice: x: 4 (x_hi: 2, x_lo: 2; x = x_hi * 2 + x_lo), y: 4, z: 8, core: 2. Of those that a mesh axis runs over, the one named last changes fastest.
Arguments:
- hidden_in: bfloat16 [4096, 4096], P('dp'), may hold values from -6 to 6
- attn_gain: float32 [4096], replicated, may hold values from 0.5 to 1.5
- qkv_weight: bfloat16 [3, 4096, 4096], P(None, 'dp', 'tensor'), may hold values from -0.09375 to 0.09375
- mix_weight: bfloat16 [4096, 4096], P('tensor', 'dp'), may hold values from -0.09375 to 0.09375
- out_gain: float32 [4096], replicated, may hold values from 0.5 to 1.5
- depth_in_weight: bfloat16 [4096, 1024], P('tensor'), may hold values from -0.09375 to 0.09375
- text_table: bfloat16 [16000, 1024], P('tensor'), may hold values from -6 to 6
- code_tables: bfloat16 [7, 2048, 1024], P(None, 'tensor'), may hold values from -6 to 6
- depth_gain: float32 [1024], replicated, may hold values from 0.5 to 1.5
- depth_qkv: bfloat16 [3, 1024, 1024], P(None, 'dp'), may hold values from -0.1875 to 0.1875
- depth_mix: bfloat16 [1024, 1024], replicated, may hold values from -0.1875 to 0.1875
- final_gain: float32 [1024], replicated, may hold values from 0.5 to 1.5
- heads_weight: bfloat16 [8, 1024, 2048], P(None, None, 'tensor'), may hold values from -0.59765625 to 0.59765625
- text_ids: int32 [4096], P('dp'), may hold values from 0 to 15999
- codes: int32 [4096, 8], P('dp'), may hold values from 0 to 2047
Outputs:
- token_loss: float32 [4096, 8], P(('dp', 'tensor'))
The draws below stay inside these ranges and needn't reach their ends.
All inputs are finite; a program needn't handle non-finite values.
Results may differ from the reference program's by a relative error of at most 0.005.
Values may be sent and summed in bfloat16 or wider, within the bound.
A program may use at most 128 MiB of HBM per device.

```python
import math
import jax
import jax.numpy as jnp
from jax import lax

D = 4096
HEAD_DIM = 128
FRAMES = 256
DD = 1024
DHEADS = 16
DHEAD_DIM = 64
CODEBOOKS = 8
VOCAB = 2048
TEXT_VOCAB = 16000
ROWS = 4096


def touch_ends(drawn, key, smallest, high):
    place = [jax.random.randint(jax.random.fold_in(key, axis), (), 0, length) for axis, length in enumerate(drawn.shape)]
    main_axis = drawn.shape.index(max(drawn.shape))
    neighbour = place[:main_axis] + [(place[main_axis] + 1) % drawn.shape[main_axis]] + place[main_axis + 1:]
    return drawn.at[tuple(place)].set(smallest).at[tuple(neighbour)].set(high)


def steps_of(stream_key, dims, cuts, least, high):
    def one(position, shards_of):
        draws = jax.random.uniform(jax.random.fold_in(jax.random.fold_in(stream_key, 6), position), (shards_of,), jnp.float32, least / len(cuts), high / len(cuts))
        return jnp.repeat(jnp.exp(draws), dims[position] // shards_of).reshape((-1,) + (1,) * (len(dims) - position - 1))

    factor_of = one(*cuts[0])
    for cut in cuts[1:]:
        factor_of = factor_of * one(*cut)
    return factor_of


def bell_draw(stream_key, extent, deviation, most, cuts=(), kind=jnp.bfloat16):
    drawn = jax.random.normal(stream_key, extent, jnp.float32) * deviation
    if len(cuts) > 0:
        drawn = steps_of(stream_key, extent, cuts, -0.22, 0.18) * drawn
    return jnp.clip(drawn, min=-most, max=most).astype(kind)


def setup_inputs(seed: int = 0) -> dict:
    arg_keys = jax.random.split(jax.random.key(seed), 16)
    return {
        "hidden_in": bell_draw(arg_keys[0], (ROWS, D), 1.0, 6.0, ((0, 16),)),
        "attn_gain": jnp.clip(1.0 + 0.1 * jax.random.normal(arg_keys[1], (D,), jnp.float32), 0.5, 1.5),
        "qkv_weight": bell_draw(arg_keys[2], (3, D, D), D ** -0.5, 0.09375, ((1, 16), (2, 16))),
        "mix_weight": bell_draw(arg_keys[3], (D, D), D ** -0.5, 0.09375, ((0, 16), (1, 16))),
        "out_gain": jnp.clip(1.0 + 0.1 * jax.random.normal(arg_keys[4], (D,), jnp.float32), 0.5, 1.5),
        "depth_in_weight": bell_draw(arg_keys[5], (D, DD), D ** -0.5, 0.09375, ((0, 16),)),
        "text_table": bell_draw(arg_keys[6], (TEXT_VOCAB, DD), 1.0, 6.0, ((0, 16),)),
        "code_tables": bell_draw(arg_keys[7], (CODEBOOKS - 1, VOCAB, DD), 1.0, 6.0, ((1, 16),)),
        "depth_gain": jnp.clip(1.0 + 0.1 * jax.random.normal(arg_keys[8], (DD,), jnp.float32), 0.5, 1.5),
        "depth_qkv": bell_draw(arg_keys[9], (3, DD, DD), DD ** -0.5, 0.1875, ((1, 16),)),
        "depth_mix": bell_draw(arg_keys[10], (DD, DD), DD ** -0.5, 0.1875),
        "final_gain": jnp.clip(1.0 + 0.1 * jax.random.normal(arg_keys[11], (DD,), jnp.float32), 0.5, 1.5),
        "heads_weight": bell_draw(arg_keys[12], (CODEBOOKS, DD, VOCAB), 0.1, 0.59765625, ((2, 16),)),
        "text_ids": touch_ends(jax.random.randint(arg_keys[13], (ROWS,), 0, TEXT_VOCAB), jax.random.fold_in(arg_keys[13], 1), 0, TEXT_VOCAB - 1).astype(jnp.int32),
        "codes": touch_ends(jax.random.randint(arg_keys[14], (ROWS, CODEBOOKS), 0, VOCAB), jax.random.fold_in(arg_keys[14], 1), 0, VOCAB - 1).astype(jnp.int32),
    }


epsilon = 1e-05

def rms_factor(values):
    return lax.rsqrt(lax.optimization_barrier(jnp.mean(values * values, axis=-1, keepdims=True)) + epsilon)

def rotate_halves(tensor, positions):
    half_dim = tensor.shape[-1] // 2
    frequency = jnp.exp(jnp.arange(half_dim, dtype=jnp.float32) * (-math.log(10000.0) / half_dim))
    angles = positions[:, None] * frequency[None, :]
    cosine = jnp.cos(angles)[:, None, :]
    sine_part = jnp.sin(angles)[:, None, :]
    first_half = tensor[..., :half_dim]
    second_half = tensor[..., half_dim:]
    return jnp.concatenate([first_half * cosine - second_half * sine_part, second_half * cosine + first_half * sine_part], axis=-1)

def temporal_mix(normed, qkv_cols):
    row_count = normed.shape[0]
    col_width = qkv_cols.shape[2]
    seq_count = row_count // FRAMES
    head_count = col_width // HEAD_DIM
    projected = jnp.einsum('rd,idw->irw', normed.astype(jnp.float32), qkv_cols.astype(jnp.float32))
    projected = projected.reshape(3, seq_count, FRAMES, head_count, HEAD_DIM)
    positions = jnp.arange(FRAMES, dtype=jnp.float32)
    queries = rotate_halves(projected[0], positions).astype(jnp.bfloat16)
    keys_rot = rotate_halves(projected[1], positions).astype(jnp.bfloat16)
    values_all = projected[2].astype(jnp.bfloat16)
    scores = jnp.einsum('sqhd,skhd->shqk', queries.astype(jnp.float32), keys_rot.astype(jnp.float32)) * HEAD_DIM ** (-0.5)
    order = jnp.arange(FRAMES)
    causal = order[:, None] >= order[None, :]
    exp_scores = jnp.where(causal, jnp.exp(jnp.where(causal, scores, 0.0)), 0.0)
    weights = (exp_scores / lax.optimization_barrier(jnp.sum(exp_scores, axis=-1, keepdims=True))).astype(jnp.bfloat16)
    attended = jnp.einsum('shqk,skhd->sqhd', weights.astype(jnp.float32), values_all.astype(jnp.float32))
    return attended.astype(jnp.bfloat16).reshape(row_count, col_width)

def depth_mixer(projected, mix_weight):
    row_count = projected.shape[1]
    split = projected.reshape(3, row_count, CODEBOOKS, DHEADS, DHEAD_DIM).astype(jnp.float32)
    scores = jnp.einsum('rqhd,rkhd->rhqk', split[0], split[1]) * DHEAD_DIM ** (-0.5)
    order = jnp.arange(CODEBOOKS)
    causal = order[:, None] >= order[None, :]
    exp_scores = jnp.where(causal, jnp.exp(jnp.where(causal, scores, 0.0)), 0.0)
    weights = (exp_scores / lax.optimization_barrier(jnp.sum(exp_scores, axis=-1, keepdims=True))).astype(jnp.bfloat16)
    attended = jnp.einsum('rhqk,rkhd->rqhd', weights.astype(jnp.float32), split[2])
    attended = attended.astype(jnp.bfloat16).reshape(row_count, CODEBOOKS, DD)
    return jnp.einsum('rcd,de->rce', attended.astype(jnp.float32), mix_weight.astype(jnp.float32))

def reference(hidden_in, attn_gain, qkv_weight, mix_weight, out_gain, depth_in_weight, text_table, code_tables, depth_gain, depth_qkv, depth_mix, final_gain, heads_weight, text_ids, codes):
    hidden_f = hidden_in.astype(jnp.float32)
    normed = (hidden_f * rms_factor(hidden_f) * attn_gain).astype(jnp.bfloat16)
    attended = temporal_mix(normed, qkv_weight)
    resid = hidden_f + jnp.dot(attended, mix_weight, preferred_element_type=jnp.float32)
    scaled = (resid * out_gain).astype(jnp.bfloat16)
    context = jnp.dot(scaled, depth_in_weight, preferred_element_type=jnp.float32) * rms_factor(resid)
    text_embed = jnp.take(text_table, text_ids.astype(jnp.int32), axis=0).astype(jnp.float32)
    books = jnp.arange(CODEBOOKS - 1).astype(jnp.int32)[None, :]
    code_embed = code_tables[books, codes[:, :CODEBOOKS - 1].astype(jnp.int32)].astype(jnp.float32)
    embeds = jnp.concatenate([text_embed[:, None, :], code_embed], axis=1)
    depth_input = context[:, None, :] + embeds
    dnormed = (depth_input * rms_factor(depth_input) * depth_gain).astype(jnp.bfloat16)
    projected = jnp.einsum('rcd,ide->irce', dnormed.astype(jnp.float32), depth_qkv.astype(jnp.float32)).astype(jnp.bfloat16)
    depth_out = depth_input + depth_mixer(projected, depth_mix)
    final = (depth_out * rms_factor(depth_out) * final_gain).astype(jnp.bfloat16)
    logits = jnp.einsum('rcd,cdv->rcv', final.astype(jnp.float32), heads_weight.astype(jnp.float32))
    log_total = jnp.log(lax.optimization_barrier(jnp.sum(jnp.exp(logits), axis=-1)))
    target = jnp.take_along_axis(logits, codes.astype(jnp.int32)[:, :, None], axis=-1)[..., 0]
    return log_total - target
```

```python
import functools

import jax
import jax.numpy as jnp
import numpy as np
from jax import lax
from jax.experimental import pallas as pl
from jax.experimental.pallas import tpu as pltpu
from jax.sharding import PartitionSpec as P

D = 4096
HEAD_DIM = 128
FRAMES = 256
DD = 1024
DHEADS = 16
DHEAD_DIM = 64
CODEBOOKS = 8
DP = 16
TP = 16
NZ = 8
OWN = 16
F32 = jnp.float32
BF16 = jnp.bfloat16
MESH = pl.DeviceIdType.MESH

epsilon = 1e-05

X0, R1, L1, R2, L2, R3, L3, C0 = range(8)


def dot(a, b):
    return jnp.dot(a, b, preferred_element_type=F32)


def dot_t(a, b):
    return lax.dot_general(a, b, (((1,), (1,)), ((), ())), preferred_element_type=F32)


class Places:
    def __init__(self):
        d = lax.axis_index("dp")
        t = lax.axis_index("tensor")
        self.d, self.t = d, t
        self.core = lax.rem(d, 2)
        self.xh = lax.rem(d // 2, 2)
        self.xl = lax.rem(t, 2)
        self.z = t // 2
        self.up = lax.rem(d + 4, 16)
        self.down = lax.rem(d + 12, 16)
        self.far = lax.rem(d + 8, 16)
        self.xstep = 2 - 4 * self.xh
        self.xpeer = d + self.xstep
        self.cstep = 1 - 2 * self.core
        self.cpeer = d + self.cstep
        self.xsib = t + 1 - 2 * self.xl
        self.zup = lax.rem(t + 2, 16)
        self.zdown = lax.rem(t + 14, 16)
        self.blocks = [d, self.xpeer, self.down, self.up, self.down + self.xstep,
                       self.up + self.xstep, self.far, self.far + self.xstep]


class Flow:
    def __init__(self, pos, own, block, send_sem, recv_sem):
        self.pos, self.own, self.block = pos, own, block
        self.ss, self.rs = send_sem, recv_sem

    def copy(self, kind, idx, dev, own=False):
        src = self.own if own else self.block(idx)
        return pltpu.make_async_remote_copy(
            src_ref=src, dst_ref=self.block(idx), send_sem=self.ss(kind), recv_sem=self.rs(kind),
            device_id={"dp": dev}, device_id_type=MESH)

    def start0(self):
        p = self.pos
        for kind, dev in ((X0, p.xpeer), (R1, p.up), (L1, p.down), (C0, p.cpeer)):
            self.copy(kind, p.d, dev, own=True).start()

    def got(self, kind):
        p = self.pos
        self.copy(kind, p.blocks[kind + 1], p.cpeer).wait_recv()

    def forward(self, kind, idx, dev):
        self.copy(kind, idx, dev).start()

    def to_core(self, kind):
        p = self.pos
        self.forward(C0 + kind + 1, p.blocks[kind + 1], p.cpeer)

    def stage1(self):
        p = self.pos
        self.got(X0)
        self.forward(R2, p.xpeer, p.up)
        self.forward(L2, p.xpeer, p.down)
        self.to_core(X0)
        self.got(R1)
        self.forward(R3, p.down, p.up)
        self.to_core(R1)
        self.got(L1)
        self.to_core(L1)

    def stage2(self):
        p = self.pos
        self.got(R2)
        self.to_core(R2)
        self.got(L2)
        self.forward(L3, p.up + p.xstep, p.down)
        self.to_core(L2)

    def stage3(self):
        self.got(R3)
        self.to_core(R3)
        self.got(L3)
        self.to_core(L3)

    def stage4(self):
        p = self.pos
        for n in range(8):
            self.copy(C0 + n, p.blocks[n] + p.cstep, p.cpeer).wait_recv()

    def drain(self):
        p = self.pos
        for kind in range(15):
            self.copy(kind, p.d, p.cpeer).wait_send()


class Ring:
    def __init__(self, pos, own, right, left, out, inn, ss, rs, base):
        self.pos, self.own = pos, own
        self.right, self.left, self.out, self.inn = right, left, out, inn
        self.ss, self.rs, self.base = ss, rs, base

    def dest(self, right, s):
        z = self.pos.z
        return lax.rem(z + 4 - s, NZ) if right else lax.rem(z + 5 + s, NZ)

    def copy(self, right, s):
        slots = self.right if right else self.left
        k = self.base + s + (0 if right else 4)
        src = self.own(self.dest(right, s)) if s == 0 else slots.at[s - 1]
        return pltpu.make_async_remote_copy(
            src_ref=src, dst_ref=slots.at[s], send_sem=self.ss.at[k], recv_sem=self.rs.at[k],
            device_id={"tensor": self.pos.zup if right else self.pos.zdown}, device_id_type=MESH)

    def step(self, s):
        for right in (True, False):
            if s > (3 if right else 2):
                continue
            if s:
                self.copy(right, s - 1).wait_recv()
                slots = self.right if right else self.left
                mine = self.own(self.dest(right, s))
                for h in range(2):
                    slots[s - 1, h] = (slots[s - 1, h].astype(F32) + mine[h].astype(F32)).astype(BF16)
            self.copy(right, s).start()

    def total(self, h):
        mine = self.own(self.pos.z)
        return mine[h].astype(F32) + self.right[3, h].astype(F32) + self.left[2, h].astype(F32)

    def pair(self):
        return pltpu.make_async_remote_copy(
            src_ref=self.out, dst_ref=self.inn, send_sem=self.ss.at[self.base + 7],
            recv_sem=self.rs.at[self.base + 7], device_id={"tensor": self.pos.xsib}, device_id_type=MESH)

    def finish(self):
        self.copy(True, 3).wait_recv()
        self.copy(False, 2).wait_recv()
        self.out[...] = self.total(1 - self.pos.xl).astype(BF16)
        self.pair().start()

    def result(self):
        self.pair().wait_recv()
        return self.total(self.pos.xl) + self.inn[...].astype(F32)

    def drain(self):
        for s in range(4):
            self.copy(True, s).wait_send()
        for s in range(3):
            self.copy(False, s).wait_send()
        self.pair().wait_send()


def front(hid, gain, qkv, mix, ogain, din, text, tabs, tid, code, cosr, sinr, dqkv, heads,
          depth_in, dfull, hfull,
          wall, normed, acc, att, part, emb, er, el, eo, ei, pr, pl_, po, pi, ctxs, ctxr, sqs, sqr,
          wss, wrs, ess, ers, pss, prs, css, crs, hss, hrs, lsem):
    p = Places()
    d, t = p.d, p.t

    barrier = pltpu.get_barrier_semaphore()
    for dev in (p.xpeer, p.up, p.down, p.cpeer):
        pl.semaphore_signal(barrier, inc=1, device_id={"dp": dev}, device_id_type=MESH)
    for k in range(1, TP):
        pl.semaphore_signal(barrier, inc=1, device_id={"tensor": lax.rem(t + k, TP)}, device_id_type=MESH)
    pl.semaphore_wait(barrier, 4 + TP - 1)

    def flow(f):
        own = mix if f == 3 else qkv.at[f]
        return Flow(p, own, lambda i: wall.at[f, i], lambda k: wss.at[f, k], lambda k: wrs.at[f, k])

    flows = [flow(f) for f in range(4)]
    deep = Flow(p, dqkv, lambda i: dfull.at[:, pl.ds(pl.multiple_of(i * 64, 64), 64), :],
                lambda k: wss.at[4, k], lambda k: wrs.at[4, k])
    for f in flows:
        f.start0()
    own_deep = pltpu.make_async_copy(dqkv, dfull.at[:, pl.ds(pl.multiple_of(d * 64, 64), 64), :], lsem.at[0])
    own_heads = pltpu.make_async_copy(heads, hfull.at[p.xl], lsem.at[1])
    own_deep.start()
    own_heads.start()

    lanes = lax.broadcasted_iota(jnp.int32, (FRAMES, 128), 1)

    def place(c, found):
        emb[:, c] = found.astype(BF16).reshape(TP, OWN, DD)

    rows = text.shape[0]
    wide = lax.broadcasted_iota(jnp.int32, (FRAMES, rows), 1)
    place(0, dot((wide == tid[...]).astype(BF16), text[...]))
    for c in range(1, CODEBOOKS):
        place(c, dot((lanes == code[:, c - 1:c]).astype(BF16), tabs[c - 1]))
    eown = lambda z: emb.at[pl.ds(2 * z, 2)]
    ering = Ring(p, eown, er, el, eo, ei, ess, ers, 0)
    ering.step(0)

    for f in range(3):
        wall[f, d] = qkv[f]
    wall[3, d] = mix[...]

    def norm_rows(n, carry):
        r = pl.ds(pl.multiple_of(n * 32, 32), 32)
        h = hid[r, :].astype(F32)
        scale = lax.rsqrt(jnp.mean(h * h, axis=-1, keepdims=True) + epsilon)
        normed[r, :] = (h * scale * gain[...]).astype(BF16)
        return carry

    lax.fori_loop(0, FRAMES // 32, norm_rows, 0)

    for f in flows:
        f.stage1()
    for f in flows:
        f.stage2()
    ering.step(1)
    for f in flows:
        f.stage3()
    for f in flows[:3]:
        f.stage4()
    deep.start0()
    head_part = pl.ds(p.core * 4, 4)
    head_rest = pl.ds(4 - p.core * 4, 4)
    head_x = pltpu.make_async_remote_copy(
        src_ref=heads.at[head_part], dst_ref=hfull.at[p.xl, head_part], send_sem=hss.at[0],
        recv_sem=hrs.at[0], device_id={"tensor": p.xsib}, device_id_type=MESH)
    head_x.start()
    ering.step(2)

    acc[...] = jnp.zeros_like(acc)

    def project(b, carry):
        cols = normed[:, pl.ds(pl.multiple_of(b * 256, 256), 256)]
        for i in range(3):
            acc[i] += dot(cols, wall[i, b])
        return carry

    lax.fori_loop(0, DP, project, 0)

    order_q = lax.broadcasted_iota(jnp.int32, (FRAMES, FRAMES), 0)
    order_k = lax.broadcasted_iota(jnp.int32, (FRAMES, FRAMES), 1)
    causal = order_q >= order_k
    cosv, sinv = cosr[...], sinr[...]

    def rotate(v):
        half = HEAD_DIM // 2
        swapped = jnp.concatenate([v[:, half:], v[:, :half]], axis=1)
        return (v * cosv + swapped * sinv).astype(BF16)

    for h in range(2):
        cols = slice(h * HEAD_DIM, (h + 1) * HEAD_DIM)
        q = rotate(acc[0, :, cols])
        k = rotate(acc[1, :, cols])
        v = acc[2, :, cols].astype(BF16)
        scores = dot_t(q, k) * HEAD_DIM ** (-0.5)
        e = jnp.where(causal, jnp.exp(jnp.where(causal, scores, 0.0)), 0.0)
        w = (e / jnp.sum(e, axis=-1, keepdims=True)).astype(BF16)
        att[:, cols] = dot(w, v).astype(BF16)

    flows[3].stage4()
    ering.step(3)
    pown = lambda z: part.at[pl.ds(2 * z, 2)]
    pring = Ring(p, pown, pr, pl_, po, pi, pss, prs, 0)

    def mixed(offset):
        z = lax.rem(p.z + offset, NZ)
        for h in range(2):
            part[2 * z + h] = dot(att[...], wall[3, 2 * z + h]).astype(BF16)

    mixed(4)
    mixed(5)
    pring.step(0)
    mixed(3)
    mixed(6)
    deep.stage1()
    pring.step(1)
    mixed(2)
    mixed(7)
    deep.stage2()
    pring.step(2)
    mixed(1)
    mixed(0)
    deep.stage3()
    pring.step(3)
    head_x_in = pltpu.make_async_remote_copy(
        src_ref=hfull.at[1 - p.xl, head_part], dst_ref=hfull.at[1 - p.xl, head_part], send_sem=hss.at[1],
        recv_sem=hrs.at[0], device_id={"dp": p.cpeer}, device_id_type=MESH)
    head_x_in.wait_recv()
    head_c = pltpu.make_async_remote_copy(
        src_ref=hfull.at[1 - p.xl, head_part], dst_ref=hfull.at[1 - p.xl, head_part], send_sem=hss.at[1],
        recv_sem=hrs.at[1], device_id={"dp": p.cpeer}, device_id_type=MESH)
    head_c.start()
    pring.finish()
    ering.finish()

    cols = pl.ds(pl.multiple_of(t * 256, 256), 256)
    resid = pring.result() + hid[:, cols].astype(F32)
    square = jnp.sum(resid * resid, axis=-1, keepdims=True)
    sqs[...] = jnp.broadcast_to(square, (FRAMES, 128)).reshape(TP, OWN, 128)
    scaled = (resid * ogain[:, cols]).astype(BF16)
    ctxs[...] = dot(scaled, din[...]).astype(BF16).reshape(TP, OWN, DD)

    def share(k, which, sender):
        src, dst = (ctxs, ctxr) if which == 0 else (sqs, sqr)
        to = lax.rem(t + k, TP)
        return pltpu.make_async_remote_copy(
            src_ref=src.at[to], dst_ref=dst.at[sender], send_sem=css.at[which, k], recv_sem=crs.at[which, k],
            device_id={"tensor": to}, device_id_type=MESH)

    for k in range(1, TP):
        for which in range(2):
            share(k, which, t).start()
    ctxr[t] = ctxs[t]
    sqr[t] = sqs[t]
    embeds = ering.result().reshape(CODEBOOKS, OWN, DD)
    for k in range(1, TP):
        for which in range(2):
            share(k, which, lax.rem(t + TP - k, TP)).wait_recv()
    context = ctxr[0].astype(F32)
    squares = sqr[0]
    for n in range(1, TP):
        context = context + ctxr[n].astype(F32)
        squares = squares + sqr[n]
    context = context * lax.rsqrt(squares[:, :1] / D + epsilon)
    depth_in[...] = context[None] + embeds

    deep.stage4()
    head_rest_in = pltpu.make_async_remote_copy(
        src_ref=hfull.at[1 - p.xl, head_rest], dst_ref=hfull.at[1 - p.xl, head_rest], send_sem=hss.at[1],
        recv_sem=hrs.at[1], device_id={"dp": p.cpeer}, device_id_type=MESH)
    head_rest_in.wait_recv()
    own_deep.wait()
    own_heads.wait()
    for f in flows:
        f.drain()
    deep.drain()
    ering.drain()
    pring.drain()
    for k in range(1, TP):
        for which in range(2):
            share(k, which, t).wait_send()
    head_x.wait_send()
    head_c.wait_send()


def back(depth_in, dfull, dgain, dmix, fgain, hfull, target,
         loss,
         wq, wm, wh, proj, att, fin, sums, got, lsem, ss, rs, tss, trs):
    t = lax.axis_index("tensor")
    z = t // 2
    xl = lax.rem(t, 2)
    zup, zdown = lax.rem(t + 2, 16), lax.rem(t + 14, 16)

    loads = [pltpu.make_async_copy(dfull.at[i], wq.at[i], lsem.at[i]) for i in range(3)]
    loads.append(pltpu.make_async_copy(dmix, wm, lsem.at[3]))
    for h in range(2):
        loads.append(pltpu.make_async_copy(hfull.at[h], wh.at[:, :, pl.ds(h * 128, 128)], lsem.at[4 + h]))
    for one in loads:
        one.start()

    barrier = pltpu.get_barrier_semaphore()
    for k in range(1, NZ):
        pl.semaphore_signal(barrier, inc=1, device_id={"tensor": lax.rem(t + 2 * k, TP)}, device_id_type=MESH)
    pl.semaphore_wait(barrier, NZ - 1)

    rows = CODEBOOKS * OWN
    x = depth_in[...].reshape(rows, DD)
    dn = (x * lax.rsqrt(jnp.mean(x * x, axis=-1, keepdims=True) + epsilon) * dgain[...]).astype(BF16)
    for i in range(3):
        loads[i].wait()
        proj[i] = dot(dn, wq[i]).astype(BF16)

    rq = lax.broadcasted_iota(jnp.int32, (rows, rows), 0)
    rk = lax.broadcasted_iota(jnp.int32, (rows, rows), 1)
    seen = (lax.rem(rq, OWN) == lax.rem(rk, OWN)) & (rq >= rk)
    low = lax.broadcasted_iota(jnp.int32, (rows, 128), 1) < DHEAD_DIM
    for j in range(DHEADS // 2):
        cols = slice(j * 128, (j + 1) * 128)
        q, k, v = proj[0, :, cols], proj[1, :, cols], proj[2, :, cols]
        parts = []
        for half in (low, jnp.logical_not(low)):
            scores = dot_t(jnp.where(half, q, jnp.zeros_like(q)), k) * DHEAD_DIM ** (-0.5)
            e = jnp.where(seen, jnp.exp(jnp.where(seen, scores, 0.0)), 0.0)
            w = (e / jnp.sum(e, axis=-1, keepdims=True)).astype(BF16)
            parts.append(dot(w, v))
        att[:, cols] = jnp.where(low, parts[0], parts[1]).astype(BF16)
    loads[3].wait()
    out = x + dot(att[...], wm[...])
    final = (out * lax.rsqrt(jnp.mean(out * out, axis=-1, keepdims=True) + epsilon) * fgain[...]).astype(BF16)
    fin[:, z] = final.reshape(CODEBOOKS, OWN, DD)

    def ring(right, s, block):
        books = pl.ds(0, CODEBOOKS) if s < 3 else (pl.ds(0, 4) if right else pl.ds(4, 4))
        view = fin.at[books, block]
        k = s + (0 if right else 4)
        return pltpu.make_async_remote_copy(
            src_ref=view, dst_ref=view, send_sem=ss.at[k], recv_sem=rs.at[k],
            device_id={"tensor": zup if right else zdown}, device_id_type=MESH)

    for s in range(4):
        if s:
            ring(True, s - 1, lax.rem(z + NZ - s, NZ)).wait_recv()
        ring(True, s, lax.rem(z + NZ - s, NZ)).start()
        if s:
            ring(False, s - 1, lax.rem(z + s, NZ)).wait_recv()
        ring(False, s, lax.rem(z + s, NZ)).start()
    far = lax.rem(z + 4, NZ)
    ring(True, 3, far).wait_recv()
    ring(False, 3, far).wait_recv()

    loads[4].wait()
    loads[5].wait()
    shared = OWN * NZ
    lanes = lax.broadcasted_iota(jnp.int32, (shared, 256), 1)
    spots = lax.broadcasted_iota(jnp.int32, (shared, 128), 1)
    total = jnp.zeros((shared, 128), F32)
    for c in range(CODEBOOKS):
        logits = dot(fin[c].reshape(shared, DD), wh[c])
        e = jnp.sum(jnp.exp(logits), axis=-1, keepdims=True)
        hit = jnp.sum(jnp.where(lanes == target[:, c:c + 1], logits, 0.0), axis=-1, keepdims=True)
        total = jnp.where(spots == c, e, total)
        total = jnp.where(spots == CODEBOOKS + c, hit, total)
    sums[...] = total.reshape(NZ, OWN, 128)

    def share(k, sender):
        to = lax.rem(z + k, NZ)
        return pltpu.make_async_remote_copy(
            src_ref=sums.at[to], dst_ref=got.at[sender], send_sem=tss.at[k], recv_sem=trs.at[k],
            device_id={"tensor": 2 * to + xl}, device_id_type=MESH)

    for k in range(1, NZ):
        share(k, z).start()
    got[z] = sums[z]
    for k in range(1, NZ):
        share(k, lax.rem(z + NZ - k, NZ)).wait_recv()
    both = got[0]
    for n in range(1, NZ):
        both = both + got[n]
    loss[...] = jnp.log(both[:, :CODEBOOKS]) - both[:, CODEBOOKS:2 * CODEBOOKS]
    for k in range(1, NZ):
        share(k, z).wait_send()
    for s in range(4):
        ring(True, s, z).wait_send()
        ring(False, s, z).wait_send()


def shards(hidden_in, attn_gain, qkv_weight, mix_weight, out_gain, depth_in_weight, text_table, code_tables,
           depth_gain, depth_qkv, depth_mix, final_gain, heads_weight, text_ids, codes):
    t = lax.axis_index("tensor")
    half = HEAD_DIM // 2
    angles = np.arange(FRAMES)[:, None] * 10000.0 ** (-np.arange(half) / half)[None, :]
    cosv = np.concatenate([np.cos(angles)] * 2, axis=1).astype(np.float32)
    sinv = np.concatenate([-np.sin(angles), np.sin(angles)], axis=1).astype(np.float32)
    count = text_table.shape[0]
    text = jnp.pad(text_table, ((0, -count % 128), (0, 0)))
    text_local = text_ids - t * count
    text_local = jnp.where((text_local >= 0) & (text_local < count), text_local, -1)[:, None]
    code_local = codes - t * code_tables.shape[1]

    vmem = pl.BlockSpec(memory_space=pltpu.VMEM)
    anym = pl.BlockSpec(memory_space=pl.ANY)
    dma = pltpu.SemaphoreType.DMA
    depth_in, dfull, hfull = pl.pallas_call(
        front,
        out_shape=(
            jax.ShapeDtypeStruct((CODEBOOKS, OWN, DD), F32),
            jax.ShapeDtypeStruct((3, DD, DD), BF16),
            jax.ShapeDtypeStruct((2, CODEBOOKS, DD, 128), BF16),
        ),
        in_specs=[vmem] * 12 + [anym] * 2,
        out_specs=(vmem, anym, anym),
        scratch_shapes=[
            pltpu.VMEM((4, DP, 256, 256), BF16),
            pltpu.VMEM((FRAMES, D), BF16),
            pltpu.VMEM((3, FRAMES, 256), F32),
            pltpu.VMEM((FRAMES, 256), BF16),
            pltpu.VMEM((TP, FRAMES, 256), BF16),
            pltpu.VMEM((TP, CODEBOOKS, OWN, DD), BF16),
            pltpu.VMEM((4, 2, CODEBOOKS, OWN, DD), BF16),
            pltpu.VMEM((3, 2, CODEBOOKS, OWN, DD), BF16),
            pltpu.VMEM((CODEBOOKS, OWN, DD), BF16),
            pltpu.VMEM((CODEBOOKS, OWN, DD), BF16),
            pltpu.VMEM((4, 2, FRAMES, 256), BF16),
            pltpu.VMEM((3, 2, FRAMES, 256), BF16),
            pltpu.VMEM((FRAMES, 256), BF16),
            pltpu.VMEM((FRAMES, 256), BF16),
            pltpu.VMEM((TP, OWN, DD), BF16),
            pltpu.VMEM((TP, OWN, DD), BF16),
            pltpu.VMEM((TP, OWN, 128), F32),
            pltpu.VMEM((TP, OWN, 128), F32),
            dma((5, 15)), dma((5, 15)),
            dma((8,)), dma((8,)),
            dma((8,)), dma((8,)),
            dma((2, TP)), dma((2, TP)),
            dma((2,)), dma((2,)),
            dma((2,)),
        ],
        compiler_params=pltpu.CompilerParams(
            collective_id=0, has_side_effects=True, vmem_limit_bytes=56 * 2**20),
        name="front",
    )(hidden_in, attn_gain[None], qkv_weight, mix_weight, out_gain[None], depth_in_weight, text, code_tables,
      text_local, code_local, cosv, sinv, depth_qkv, heads_weight)

    z, xl = t // 2, lax.rem(t, 2)
    target = lax.dynamic_index_in_dim(codes.reshape(NZ, 2, OWN, CODEBOOKS), xl, 1, keepdims=False)
    target = target.reshape(NZ * OWN, CODEBOOKS) - z * 256
    return pl.pallas_call(
        back,
        out_shape=jax.ShapeDtypeStruct((OWN, CODEBOOKS), F32),
        in_specs=[vmem, anym, vmem, anym, vmem, anym, vmem],
        out_specs=vmem,
        scratch_shapes=[
            pltpu.VMEM((3, DD, DD), BF16),
            pltpu.VMEM((DD, DD), BF16),
            pltpu.VMEM((CODEBOOKS, DD, 256), BF16),
            pltpu.VMEM((3, CODEBOOKS * OWN, DD), BF16),
            pltpu.VMEM((CODEBOOKS * OWN, DD), BF16),
            pltpu.VMEM((CODEBOOKS, NZ, OWN, DD), BF16),
            pltpu.VMEM((NZ, OWN, 128), F32),
            pltpu.VMEM((NZ, OWN, 128), F32),
            dma((6,)),
            dma((8,)), dma((8,)),
            dma((NZ,)), dma((NZ,)),
        ],
        compiler_params=pltpu.CompilerParams(
            collective_id=1, has_side_effects=True, vmem_limit_bytes=48 * 2**20),
        name="back",
    )(depth_in, dfull, depth_gain[None], depth_mix, final_gain[None], hfull, target)


def solution(mesh):
    in_specs = (
        P("dp", None),
        P(),
        P(None, "dp", "tensor"),
        P("tensor", "dp"),
        P(),
        P("tensor", None),
        P("tensor", None),
        P(None, "tensor", None),
        P(),
        P(None, "dp", None),
        P(),
        P(),
        P(None, None, "tensor"),
        P("dp"),
        P("dp", None),
    )
    out_specs = P(("dp", "tensor"), None)
    return jax.shard_map(shards, mesh=mesh, in_specs=in_specs, out_specs=out_specs, check_vma=False)
```

```python
import functools

import jax
import jax.numpy as jnp
import numpy as np
from jax import lax
from jax.experimental import pallas as pl
from jax.experimental.pallas import tpu as pltpu
from jax.sharding import PartitionSpec as P

D = 4096
HEAD_DIM = 128
FRAMES = 256
DD = 1024
DHEADS = 16
DHEAD_DIM = 64
CODEBOOKS = 8
DP = 16
TP = 16
NZ = 8
OWN = 16
F32 = jnp.float32
BF16 = jnp.bfloat16
MESH = pl.DeviceIdType.MESH

epsilon = 1e-05

X0, R1, L1, R2, L2, R3, L3, C0 = range(8)


def dot(a, b):
    return jnp.dot(a, b, preferred_element_type=F32)


def dot_t(a, b):
    return lax.dot_general(a, b, (((1,), (1,)), ((), ())), preferred_element_type=F32)


class Places:
    def __init__(self):
        d = lax.axis_index("dp")
        t = lax.axis_index("tensor")
        self.d, self.t = d, t
        self.core = lax.rem(d, 2)
        self.xh = lax.rem(d // 2, 2)
        self.xl = lax.rem(t, 2)
        self.z = t // 2
        self.up = lax.rem(d + 4, 16)
        self.down = lax.rem(d + 12, 16)
        self.far = lax.rem(d + 8, 16)
        self.xstep = 2 - 4 * self.xh
        self.xpeer = d + self.xstep
        self.cstep = 1 - 2 * self.core
        self.cpeer = d + self.cstep
        self.xsib = t + 1 - 2 * self.xl
        self.zup = lax.rem(t + 2, 16)
        self.zdown = lax.rem(t + 14, 16)
        self.blocks = [d, self.xpeer, self.down, self.up, self.down + self.xstep,
                       self.up + self.xstep, self.far, self.far + self.xstep]


class Flow:
    def __init__(self, pos, own, block, send_sem, recv_sem):
        self.pos, self.own, self.block = pos, own, block
        self.ss, self.rs = send_sem, recv_sem

    def copy(self, kind, idx, dev, own=False):
        src = self.own if own else self.block(idx)
        return pltpu.make_async_remote_copy(
            src_ref=src, dst_ref=self.block(idx), send_sem=self.ss(kind), recv_sem=self.rs(kind),
            device_id={"dp": dev}, device_id_type=MESH)

    def start0(self):
        p = self.pos
        for kind, dev in ((X0, p.xpeer), (R1, p.up), (L1, p.down), (C0, p.cpeer)):
            self.copy(kind, p.d, dev, own=True).start()

    def core_in(self, n):
        p = self.pos
        self.copy(C0 + n, p.blocks[n] + p.cstep, p.cpeer).wait_recv()

    def got(self, kind):
        p = self.pos
        self.copy(kind, p.blocks[kind + 1], p.cpeer).wait_recv()

    def forward(self, kind, idx, dev):
        self.copy(kind, idx, dev).start()

    def to_core(self, kind):
        p = self.pos
        self.forward(C0 + kind + 1, p.blocks[kind + 1], p.cpeer)

    def stage1(self):
        p = self.pos
        self.got(X0)
        self.forward(R2, p.xpeer, p.up)
        self.forward(L2, p.xpeer, p.down)
        self.to_core(X0)
        self.got(R1)
        self.forward(R3, p.down, p.up)
        self.to_core(R1)
        self.got(L1)
        self.to_core(L1)

    def stage2(self):
        p = self.pos
        self.got(R2)
        self.to_core(R2)
        self.got(L2)
        self.forward(L3, p.up + p.xstep, p.down)
        self.to_core(L2)

    def stage3(self):
        self.got(R3)
        self.to_core(R3)
        self.got(L3)
        self.to_core(L3)

    def stage4(self):
        p = self.pos
        for n in range(8):
            self.core_in(n)

    def drain(self):
        p = self.pos
        for kind in range(15):
            self.copy(kind, p.d, p.cpeer).wait_send()


class Ring:
    def __init__(self, pos, own, slots, half, add, ss, rs):
        self.pos, self.own, self.slots, self.half, self.add = pos, own, slots, half, add
        self.ss, self.rs = ss, rs

    def dest(self, way, s):
        return lax.rem(self.pos.z + (4 - s if way == 0 else 4 + s), NZ)

    def copy(self, way, s):
        slots = self.slots[way]
        if s == 0:
            part = pl.ds(way * self.half, self.half)
            src, dst = self.own(self.dest(way, 0)).at[:, part], slots.at[0, :, part]
        else:
            src, dst = slots.at[s - 1], slots.at[s]
        k = 4 * way + s
        return pltpu.make_async_remote_copy(
            src_ref=src, dst_ref=dst, send_sem=self.ss.at[k], recv_sem=self.rs.at[k],
            device_id={"tensor": self.pos.zdown if way else self.pos.zup}, device_id_type=MESH)

    def clear(self):
        for way in range(2):
            rest = pl.ds((1 - way) * self.half, self.half)
            self.slots[way][0, :, rest] = jnp.zeros_like(self.slots[way][0, :, rest])

    def step(self, s):
        for way in range(2):
            if s:
                self.copy(way, s - 1).wait_recv()
                self.add(self.slots[way].at[s - 1], self.own(self.dest(way, s)))
            self.copy(way, s).start()

    def arrive(self):
        for way in range(2):
            self.copy(way, 3).wait_recv()

    def drain(self):
        for way in range(2):
            for s in range(4):
                self.copy(way, s).wait_send()


def layer(gain, ogain, text, ids, cosr, sinr, dgain, fgain, target,
          hid_h, qkv_h, mix_h, din_h, tabs_h, dqkv, dmix_h, heads,
          loss,
          hid, din, tabs, wall, normed, acc, att, part, emb, er, el, eo, ei, pr, pe, po, pi, bs, br,
          cs, cx, cr, wq, wm, wh, proj, datt, fin, sums, got,
          lsem, wss, wrs, ess, ers, pss, prs, bss, brs, xss, xrs, css, crs, hss, hrs, fss, frs, tss, trs):
    p = Places()
    d, t, z, xl = p.d, p.t, p.z, p.xl

    def block_of(f):
        return lambda i: wall.at[f, i]

    deep_block = lambda i: wq.at[:, pl.ds(pl.multiple_of(i * 64, 64), 64), :]
    own_lanes = pl.ds(pl.multiple_of(xl * 128, 128), 128)
    sib_lanes = pl.ds(pl.multiple_of((1 - xl) * 128, 128), 128)
    loads = [(qkv_h.at[0], wall.at[0, d]), (qkv_h.at[1], wall.at[1, d]), (qkv_h.at[2], wall.at[2, d]),
             (mix_h, wall.at[3, d]), (tabs_h, tabs), (hid_h, hid), (din_h, din), (dqkv, deep_block(d)),
             (dmix_h, wm), (heads, wh.at[:, :, own_lanes])]
    loads = [pltpu.make_async_copy(src, dst, lsem.at[n]) for n, (src, dst) in enumerate(loads)]
    for one in loads:
        one.start()

    def add_books(a, b):
        def one(n, carry):
            h, c = n // CODEBOOKS, lax.rem(n, CODEBOOKS)
            a[h, c] = a[h, c] + b[h, c]
            return carry

        lax.fori_loop(0, 2 * CODEBOOKS, one, 0)

    def add_rows(a, b):
        def one(n, carry):
            a[n] = (a[n].astype(F32) + b[n].astype(F32)).astype(BF16)
            return carry

        lax.fori_loop(0, 3, one, 0)

    ering = Ring(p, lambda i: emb.at[pl.ds(2 * i, 2)], (er, el), CODEBOOKS // 2, add_books, ess, ers)
    pring = Ring(p, lambda i: part.at[i], (pr, pe), 64, add_rows, pss, prs)
    ering.clear()
    pring.clear()

    barrier = pltpu.get_barrier_semaphore()
    for dev in (p.xpeer, p.up, p.down, p.cpeer):
        pl.semaphore_signal(barrier, inc=1, device_id={"dp": dev}, device_id_type=MESH)

    def greet(k, carry):
        pl.semaphore_signal(barrier, inc=1, device_id={"tensor": lax.rem(t + 2 * k, TP)}, device_id_type=MESH)
        return carry

    lax.fori_loop(1, NZ, greet, 0)
    pl.semaphore_signal(barrier, inc=1, device_id={"tensor": p.xsib}, device_id_type=MESH)
    pl.semaphore_wait(barrier, 4 + NZ)

    def flow(f):
        return Flow(p, wall.at[f, d], block_of(f), lambda k: wss.at[f, k], lambda k: wrs.at[f, k])

    def qkv_flows(act):
        def one(f, carry):
            act(flow(f))
            return carry

        lax.fori_loop(0, 3, one, 0)

    mixer = flow(3)
    deep = Flow(p, dqkv, deep_block, lambda k: wss.at[4, k], lambda k: wrs.at[4, k])
    for n in range(3):
        loads[n].wait()
    qkv_flows(lambda f: f.start0())

    idv = ids[...].astype(F32)
    pick = lax.broadcasted_iota(jnp.int32, idv.shape, 1)
    count = text.shape[0]
    whole = count // 128 * 128

    def named(c, start, width):
        want = jnp.sum(jnp.where(pick == c, idv, 0.0), axis=1, keepdims=True)
        lanes = lax.broadcasted_iota(jnp.int32, (FRAMES, width), 1).astype(F32) + start
        return (lanes == want).astype(BF16)

    found = dot(named(0, 0, whole), text[:whole])
    if count > whole:
        found = found + dot(named(0, whole, count - whole), text[whole:])
    emb[:, 0] = found.astype(BF16).reshape(TP, OWN, DD)
    loads[4].wait()

    def lookup(c, carry):
        emb[:, c] = dot(named(c, 0, 128), tabs[c - 1]).astype(BF16).reshape(TP, OWN, DD)
        return carry

    lax.fori_loop(1, CODEBOOKS, lookup, 0)
    ering.step(0)
    loads[5].wait()

    def norm_rows(n, carry):
        r = pl.ds(pl.multiple_of(n * 32, 32), 32)
        h = hid[r, :].astype(F32)
        scale = lax.rsqrt(jnp.mean(h * h, axis=-1, keepdims=True) + epsilon)
        normed[r, :] = (h * scale * gain[...]).astype(BF16)
        return carry

    lax.fori_loop(0, FRAMES // 32, norm_rows, 0)
    acc[...] = jnp.zeros_like(acc)

    def project(ns):
        for n in ns:
            def side(c, carry):
                @pl.when(c == 1)
                def _():
                    qkv_flows(lambda f: f.core_in(n))

                b = p.blocks[n] + c * p.cstep
                cols = normed[:, pl.ds(pl.multiple_of(b * 256, 256), 256)]

                def one(i, carry):
                    acc[i] += dot(cols, wall[i, b])
                    return carry

                return lax.fori_loop(0, 3, one, carry)

            lax.fori_loop(0, 2, side, 0)

    qkv_flows(lambda f: f.stage1())
    loads[3].wait()
    mixer.start0()
    project((0, 1, 2, 3))
    ering.step(1)
    qkv_flows(lambda f: f.stage2())
    mixer.stage1()
    loads[7].wait()
    deep.start0()
    project((4, 5))
    qkv_flows(lambda f: f.stage3())
    mixer.stage2()
    project((6, 7))
    ering.step(2)

    order_q = lax.broadcasted_iota(jnp.int32, (FRAMES, FRAMES), 0)
    order_k = lax.broadcasted_iota(jnp.int32, (FRAMES, FRAMES), 1)
    causal = order_q >= order_k

    def rotate(v):
        half = HEAD_DIM // 2
        swapped = jnp.concatenate([v[:, half:], v[:, :half]], axis=1)
        return (v * cosr[...] + swapped * sinr[...]).astype(BF16)

    def attend(h, carry):
        cols = pl.ds(pl.multiple_of(h * HEAD_DIM, HEAD_DIM), HEAD_DIM)
        q = rotate(acc[0, :, cols])
        k = rotate(acc[1, :, cols])
        v = acc[2, :, cols].astype(BF16)
        scores = dot_t(q, k) * HEAD_DIM ** (-0.5)
        e = jnp.where(causal, jnp.exp(jnp.where(causal, scores, 0.0)), 0.0)
        w = (e / jnp.sum(e, axis=-1, keepdims=True)).astype(BF16)
        att[:, cols] = dot(w, v).astype(BF16)
        return carry

    lax.fori_loop(0, 2, attend, 0)
    mixer.stage3()
    mixer.stage4()

    def cross(zz):
        return pltpu.make_async_remote_copy(
            src_ref=bs.at[zz], dst_ref=br.at[zz], send_sem=bss.at[zz], recv_sem=brs.at[zz],
            device_id={"tensor": p.xsib}, device_id_type=MESH)

    def near_far(n):
        step = (n + 1) // 2
        return lax.rem(z + 4 + jnp.where(lax.rem(n, 2) == 1, -step, step), NZ)

    def mixed(n, carry):
        zz = near_far(n)
        sib = dot(att[...], wall[3, 2 * zz + 1 - xl]).astype(BF16)
        bs[zz] = sib[128:]
        cross(zz).start()
        part[zz, 1 - xl] = sib[:128]
        mine = dot(att[...], wall[3, 2 * zz + xl]).astype(BF16)
        part[zz, xl] = mine[:128]
        part[zz, 2] = mine[128:]
        return carry

    lax.fori_loop(0, NZ, mixed, 0)
    ering.step(3)

    def crossed(n, carry):
        zz = near_far(n)
        cross(zz).wait_recv()
        part[zz, 2] = (part[zz, 2].astype(F32) + br[zz].astype(F32)).astype(BF16)
        return carry

    crossed(0, 0)
    pring.step(0)
    deep.stage1()
    lax.fori_loop(1, NZ, crossed, 0)
    pring.step(1)
    head_part = pl.ds(p.core * 4, 4)
    head_rest = pl.ds(4 - p.core * 4, 4)
    head_x = pltpu.make_async_remote_copy(
        src_ref=heads.at[head_part], dst_ref=wh.at[head_part, :, own_lanes], send_sem=hss.at[0],
        recv_sem=hrs.at[0], device_id={"tensor": p.xsib}, device_id_type=MESH)
    head_x.start()
    pring.step(2)
    deep.stage2()

    def swap(src, dst, k):
        return pltpu.make_async_remote_copy(
            src_ref=src, dst_ref=dst, send_sem=xss.at[k], recv_sem=xrs.at[k],
            device_id={"tensor": p.xsib}, device_id_type=MESH)

    ering.arrive()
    eo[...] = emb[2 * z + 1 - xl] + er[3, 1 - xl] + el[3, 1 - xl]
    swap(eo, ei, 0).start()
    pring.step(3)
    deep.stage3()
    pring.arrive()

    def total(h):
        return part[z, h].astype(F32) + pr[3, h].astype(F32) + pe[3, h].astype(F32)

    po[...] = total(1 - xl).astype(BF16)
    swap(po, pi, 1).start()
    loads[6].wait()
    cols = pl.ds(pl.multiple_of(t * 256, 256), 256)

    def context_part(rows, resid):
        at = slice(rows * 128, rows * 128 + 128)
        resid = resid + hid[at, cols].astype(F32)
        square = jnp.sum(resid * resid, axis=-1, keepdims=True)
        scaled = (resid * ogain[:, cols]).astype(BF16)
        at = slice(rows * 8, rows * 8 + 8)
        cs[at, :, :DD] = dot(scaled, din[...]).astype(BF16).reshape(8, OWN, DD)
        high = square.astype(BF16)
        low = (square - high.astype(F32)).astype(BF16)
        first = lax.broadcasted_iota(jnp.int32, (128, 128), 1) < 64
        both = jnp.where(first, high.astype(F32), low.astype(F32)).astype(BF16)
        cs[at, :, DD:] = both.reshape(8, OWN, 128)

    context_part(1, total(2))
    swap(po, pi, 1).wait_recv()
    context_part(0, total(xl) + pi[...].astype(F32))

    def over(zz):
        return pltpu.make_async_remote_copy(
            src_ref=cs.at[2 * zz + 1 - xl], dst_ref=cx.at[zz], send_sem=css.at[0, zz], recv_sem=crs.at[0, zz],
            device_id={"tensor": p.xsib}, device_id_type=MESH)

    def share(k, sender):
        to = lax.rem(z + k, NZ)
        return pltpu.make_async_remote_copy(
            src_ref=cs.at[2 * to + xl], dst_ref=cr.at[sender], send_sem=css.at[1, k], recv_sem=crs.at[1, k],
            device_id={"tensor": 2 * to + xl}, device_id_type=MESH)

    def start_over(n, carry):
        over(near_far(n)).start()
        return carry

    lax.fori_loop(0, NZ, start_over, 0)

    def squares(v):
        hl = v[:, DD:].astype(F32)
        return hl[:, :1] + hl[:, 64:65]

    def pair_sum(n, carry):
        zz = near_far(n)
        over(zz).wait_recv()
        mine, theirs = cs[2 * zz + xl], cx[zz]
        cs[2 * zz + xl, :, :DD] = (mine[:, :DD].astype(F32) + theirs[:, :DD].astype(F32)).astype(BF16)
        square = squares(mine) + squares(theirs)
        high = square.astype(BF16)
        low = (square - high.astype(F32)).astype(BF16)
        first = lax.broadcasted_iota(jnp.int32, (OWN, 128), 1) < 64
        cs[2 * zz + xl, :, DD:] = jnp.where(first, high.astype(F32), low.astype(F32)).astype(BF16)
        return carry

    def pass_on(n, carry):
        pair_sum(n, 0)
        share(lax.rem(near_far(n) - z + NZ, NZ), z).start()
        return carry

    lax.fori_loop(0, NZ - 1, pass_on, 0)
    pair_sum(NZ - 1, 0)
    swap(eo, ei, 0).wait_recv()
    cr[z] = cs[2 * z + xl]

    def take(k, carry):
        share(k, lax.rem(z + NZ - k, NZ)).wait_recv()
        return carry

    lax.fori_loop(1, NZ, take, 0)

    def gathered(n, carry):
        context, square = carry
        v = cr[n]
        return context + v[:, :DD].astype(F32), square + squares(v)

    context, square = lax.fori_loop(0, NZ, gathered, (jnp.zeros((OWN, DD), F32), jnp.zeros((OWN, 1), F32)))
    context = context * lax.rsqrt(square / D + epsilon)
    embeds = emb[2 * z + xl].astype(F32) + er[3, xl].astype(F32) + el[3, xl].astype(F32) + ei[...].astype(F32)

    rows = CODEBOOKS * OWN
    x = (context[None] + embeds).reshape(rows, DD)
    dn = (x * lax.rsqrt(jnp.mean(x * x, axis=-1, keepdims=True) + epsilon) * dgain[...]).astype(BF16)
    deep.stage4()

    def dproject(i, carry):
        proj[i] = dot(dn, wq[i]).astype(BF16)
        return carry

    lax.fori_loop(0, 3, dproject, 0)
    head_x_in = pltpu.make_async_remote_copy(
        src_ref=wh.at[head_part, :, sib_lanes], dst_ref=wh.at[head_part, :, sib_lanes], send_sem=hss.at[1],
        recv_sem=hrs.at[0], device_id={"dp": p.cpeer}, device_id_type=MESH)
    head_x_in.wait_recv()
    head_c = pltpu.make_async_remote_copy(
        src_ref=wh.at[head_part, :, sib_lanes], dst_ref=wh.at[head_part, :, sib_lanes], send_sem=hss.at[1],
        recv_sem=hrs.at[1], device_id={"dp": p.cpeer}, device_id_type=MESH)
    head_c.start()

    rq = lax.broadcasted_iota(jnp.int32, (rows, rows), 0)
    rk = lax.broadcasted_iota(jnp.int32, (rows, rows), 1)
    seen = (lax.rem(rq, OWN) == lax.rem(rk, OWN)) & (rq >= rk)
    low_half = lax.broadcasted_iota(jnp.int32, (rows, 128), 1) < DHEAD_DIM

    def dattend(j, carry):
        cols = pl.ds(pl.multiple_of(j * 128, 128), 128)
        q, k, v = proj[0, :, cols], proj[1, :, cols], proj[2, :, cols]
        parts = []
        for half in (low_half, jnp.logical_not(low_half)):
            scores = dot_t(jnp.where(half, q, jnp.zeros_like(q)), k) * DHEAD_DIM ** (-0.5)
            e = jnp.where(seen, jnp.exp(jnp.where(seen, scores, 0.0)), 0.0)
            w = (e / jnp.sum(e, axis=-1, keepdims=True)).astype(BF16)
            parts.append(dot(w, v))
        datt[:, cols] = jnp.where(low_half, parts[0], parts[1]).astype(BF16)
        return carry

    lax.fori_loop(0, DHEADS // 2, dattend, 0)
    loads[8].wait()
    out = x + dot(datt[...], wm[...])
    final = (out * lax.rsqrt(jnp.mean(out * out, axis=-1, keepdims=True) + epsilon) * fgain[...]).astype(BF16)
    fin[:, z] = final.reshape(CODEBOOKS, OWN, DD)

    def ring(way, s, block):
        books = pl.ds(0, CODEBOOKS) if s < 3 else pl.ds(4 * way, 4)
        view = fin.at[books, block]
        return pltpu.make_async_remote_copy(
            src_ref=view, dst_ref=view, send_sem=fss.at[4 * way + s], recv_sem=frs.at[4 * way + s],
            device_id={"tensor": p.zdown if way else p.zup}, device_id_type=MESH)

    for s in range(4):
        for way in range(2):
            block = lax.rem(z + (s if way else NZ - s), NZ)
            if s:
                ring(way, s - 1, block).wait_recv()
            ring(way, s, block).start()
    far = lax.rem(z + 4, NZ)
    ring(0, 3, far).wait_recv()
    ring(1, 3, far).wait_recv()

    loads[9].wait()
    pltpu.make_async_remote_copy(
        src_ref=wh.at[head_rest, :, sib_lanes], dst_ref=wh.at[head_rest, :, sib_lanes], send_sem=hss.at[1],
        recv_sem=hrs.at[1], device_id={"dp": p.cpeer}, device_id_type=MESH).wait_recv()
    shared = OWN * NZ
    lanes = lax.broadcasted_iota(jnp.int32, (shared, 256), 1).astype(F32)
    spots = lax.broadcasted_iota(jnp.int32, (shared, 128), 1)
    goal = target[...].astype(F32)
    books = lax.broadcasted_iota(jnp.int32, goal.shape, 1)

    def book(c, total):
        logits = dot(fin[c].reshape(shared, DD), wh[c])
        e = jnp.sum(jnp.exp(logits), axis=-1, keepdims=True)
        want = jnp.sum(jnp.where(books == c, goal, 0.0), axis=1, keepdims=True)
        hit = jnp.sum(jnp.where(lanes == want, logits, 0.0), axis=-1, keepdims=True)
        total = jnp.where(spots == c, e, total)
        return jnp.where(spots == CODEBOOKS + c, hit, total)

    sums[...] = lax.fori_loop(0, CODEBOOKS, book, jnp.zeros((shared, 128), F32)).reshape(NZ, OWN, 128)

    def reply(k, sender):
        to = lax.rem(z + k, NZ)
        return pltpu.make_async_remote_copy(
            src_ref=sums.at[to], dst_ref=got.at[sender], send_sem=tss.at[k], recv_sem=trs.at[k],
            device_id={"tensor": 2 * to + xl}, device_id_type=MESH)

    def start_reply(k, carry):
        reply(k, z).start()
        return carry

    def take_reply(k, carry):
        reply(k, lax.rem(z + NZ - k, NZ)).wait_recv()
        return carry

    lax.fori_loop(1, NZ, start_reply, 0)
    got[z] = sums[z]
    lax.fori_loop(1, NZ, take_reply, 0)
    both = got[0]
    for n in range(1, NZ):
        both = both + got[n]
    loss[...] = jnp.log(both[:, :CODEBOOKS]) - both[:, CODEBOOKS:2 * CODEBOOKS]

    qkv_flows(lambda f: f.drain())
    mixer.drain()
    deep.drain()
    ering.drain()
    pring.drain()
    swap(eo, ei, 0).wait_send()
    swap(po, pi, 1).wait_send()
    head_x.wait_send()
    head_c.wait_send()

    def sent(k, carry):
        cross(k).wait_send()
        over(k).wait_send()
        return carry

    def sent_far(k, carry):
        share(k, z).wait_send()
        reply(k, z).wait_send()
        return carry

    lax.fori_loop(0, NZ, sent, 0)
    lax.fori_loop(1, NZ, sent_far, 0)
    for s in range(4):
        for way in range(2):
            ring(way, s, z).wait_send()


def shards(hidden_in, attn_gain, qkv_weight, mix_weight, out_gain, depth_in_weight, text_table, code_tables,
           depth_gain, depth_qkv, depth_mix, final_gain, heads_weight, text_ids, codes):
    t = lax.axis_index("tensor")
    half = HEAD_DIM // 2
    angles = np.arange(FRAMES)[:, None] * 10000.0 ** (-np.arange(half) / half)[None, :]
    cosv = np.concatenate([np.cos(angles)] * 2, axis=1).astype(np.float32)
    sinv = np.concatenate([-np.sin(angles), np.sin(angles)], axis=1).astype(np.float32)
    ids = jnp.concatenate(
        [text_ids[:, None] - t * text_table.shape[0], codes[:, :CODEBOOKS - 1] - t * code_tables.shape[1]], axis=1)
    z, xl = t // 2, lax.rem(t, 2)
    target = lax.dynamic_index_in_dim(codes.reshape(NZ, 2, OWN, CODEBOOKS), xl, 1, keepdims=False)
    target = target.reshape(NZ * OWN, CODEBOOKS) - z * 256

    vmem = pl.BlockSpec(memory_space=pltpu.VMEM)
    anym = pl.BlockSpec(memory_space=pl.ANY)
    dma = pltpu.SemaphoreType.DMA
    b16 = lambda *shape: pltpu.VMEM(shape, BF16)
    f32 = lambda *shape: pltpu.VMEM(shape, F32)
    wide = DD + 128
    return pl.pallas_call(
        layer,
        out_shape=jax.ShapeDtypeStruct((OWN, CODEBOOKS), F32),
        in_specs=[vmem] * 9 + [anym] * 8,
        out_specs=vmem,
        scratch_shapes=[
            b16(FRAMES, D), b16(256, DD), b16(CODEBOOKS - 1, 128, DD),
            b16(4, DP, 256, 256), b16(FRAMES, D), f32(3, FRAMES, 256), b16(FRAMES, 256),
            b16(NZ, 3, 128, 256),
            b16(TP, CODEBOOKS, OWN, DD),
            b16(4, 2, CODEBOOKS, OWN, DD), b16(4, 2, CODEBOOKS, OWN, DD),
            b16(CODEBOOKS, OWN, DD), b16(CODEBOOKS, OWN, DD),
            b16(4, 3, 128, 256), b16(4, 3, 128, 256), b16(128, 256), b16(128, 256),
            b16(NZ, 128, 256), b16(NZ, 128, 256),
            b16(TP, OWN, wide), b16(NZ, OWN, wide), b16(NZ, OWN, wide),
            b16(3, DD, DD), b16(DD, DD), b16(CODEBOOKS, DD, 256),
            b16(3, CODEBOOKS * OWN, DD), b16(CODEBOOKS * OWN, DD),
            b16(CODEBOOKS, NZ, OWN, DD), f32(NZ, OWN, 128), f32(NZ, OWN, 128),
            dma((10,)),
            dma((5, 15)), dma((5, 15)),
            dma((8,)), dma((8,)),
            dma((8,)), dma((8,)),
            dma((NZ,)), dma((NZ,)),
            dma((2,)), dma((2,)),
            dma((2, NZ)), dma((2, NZ)),
            dma((2,)), dma((2,)),
            dma((8,)), dma((8,)),
            dma((NZ,)), dma((NZ,)),
        ],
        compiler_params=pltpu.CompilerParams(
            collective_id=0, has_side_effects=True, vmem_limit_bytes=60 * 2**20),
        name="layer",
    )(attn_gain[None], out_gain[None], text_table, ids, cosv, sinv, depth_gain[None], final_gain[None], target,
      hidden_in, qkv_weight, mix_weight, depth_in_weight, code_tables, depth_qkv, depth_mix, heads_weight)


def solution(mesh):
    in_specs = (
        P("dp", None),
        P(),
        P(None, "dp", "tensor"),
        P("tensor", "dp"),
        P(),
        P("tensor", None),
        P("tensor", None),
        P(None, "tensor", None),
        P(),
        P(None, "dp", None),
        P(),
        P(),
        P(None, None, "tensor"),
        P("dp"),
        P("dp", None),
    )
    out_specs = P(("dp", "tensor"), None)
    return jax.shard_map(shards, mesh=mesh, in_specs=in_specs, out_specs=out_specs, check_vma=False)
```

```python
import functools

import jax
import jax.numpy as jnp
import numpy as np
from jax import lax
from jax.experimental import pallas as pl
from jax.experimental.pallas import tpu as pltpu
from jax.sharding import PartitionSpec as P

D = 4096
HEAD_DIM = 128
FRAMES = 256
DD = 1024
DHEADS = 16
DHEAD_DIM = 64
CODEBOOKS = 8
DP = 16
TP = 16
NZ = 8
OWN = 16
F32 = jnp.float32
BF16 = jnp.bfloat16
MESH = pl.DeviceIdType.MESH

epsilon = 1e-05

X0, R1, L1, R2, L2, R3, L3, C0 = range(8)


def dot(a, b):
    return jnp.dot(a, b, preferred_element_type=F32)


def dot_t(a, b):
    return lax.dot_general(a, b, (((1,), (1,)), ((), ())), preferred_element_type=F32)


class Places:
    def __init__(self):
        d = lax.axis_index("dp")
        t = lax.axis_index("tensor")
        self.d, self.t = d, t
        self.core = lax.rem(d, 2)
        self.xh = lax.rem(d // 2, 2)
        self.xl = lax.rem(t, 2)
        self.z = t // 2
        self.up = lax.rem(d + 4, 16)
        self.down = lax.rem(d + 12, 16)
        self.far = lax.rem(d + 8, 16)
        self.xstep = 2 - 4 * self.xh
        self.xpeer = d + self.xstep
        self.cstep = 1 - 2 * self.core
        self.cpeer = d + self.cstep
        self.xsib = t + 1 - 2 * self.xl
        self.zup = lax.rem(t + 2, 16)
        self.zdown = lax.rem(t + 14, 16)
        self.blocks = [d, self.xpeer, self.down, self.up, self.down + self.xstep,
                       self.up + self.xstep, self.far, self.far + self.xstep]


class Flow:
    def __init__(self, pos, own, block, send_sem, recv_sem):
        self.pos, self.own, self.block = pos, own, block
        self.ss, self.rs = send_sem, recv_sem

    def copy(self, kind, idx, dev, own=False):
        src = self.own if own else self.block(idx)
        return pltpu.make_async_remote_copy(
            src_ref=src, dst_ref=self.block(idx), send_sem=self.ss(kind), recv_sem=self.rs(kind),
            device_id={"dp": dev}, device_id_type=MESH)

    def start0(self):
        p = self.pos
        for kind, dev in ((X0, p.xpeer), (R1, p.up), (L1, p.down), (C0, p.cpeer)):
            self.copy(kind, p.d, dev, own=True).start()

    def core_in(self, n):
        p = self.pos
        self.copy(C0 + n, p.blocks[n] + p.cstep, p.cpeer).wait_recv()

    def got(self, kind):
        p = self.pos
        self.copy(kind, p.blocks[kind + 1], p.cpeer).wait_recv()

    def forward(self, kind, idx, dev):
        self.copy(kind, idx, dev).start()

    def to_core(self, kind):
        p = self.pos
        self.forward(C0 + kind + 1, p.blocks[kind + 1], p.cpeer)

    def stage1(self):
        p = self.pos
        self.got(X0)
        self.forward(R2, p.xpeer, p.up)
        self.forward(L2, p.xpeer, p.down)
        self.to_core(X0)
        self.got(R1)
        self.forward(R3, p.down, p.up)
        self.to_core(R1)
        self.got(L1)
        self.to_core(L1)

    def stage2(self):
        p = self.pos
        self.got(R2)
        self.to_core(R2)
        self.got(L2)
        self.forward(L3, p.up + p.xstep, p.down)
        self.to_core(L2)

    def stage3(self):
        self.got(R3)
        self.to_core(R3)
        self.got(L3)
        self.to_core(L3)

    def stage4(self):
        p = self.pos
        for n in range(8):
            self.core_in(n)

    def drain(self):
        p = self.pos
        for kind in range(15):
            self.copy(kind, p.d, p.cpeer).wait_send()


class Ring:
    def __init__(self, pos, own, slots, half, add, ss, rs):
        self.pos, self.own, self.slots, self.half, self.add = pos, own, slots, half, add
        self.ss, self.rs = ss, rs

    def dest(self, way, s):
        return lax.rem(self.pos.z + (4 - s if way == 0 else 4 + s), NZ)

    def copy(self, way, s):
        slots = self.slots[way]
        if s == 0:
            part = pl.ds(way * self.half, self.half)
            src, dst = self.own(self.dest(way, 0)).at[:, part], slots.at[0, :, part]
        else:
            src, dst = slots.at[s - 1], slots.at[s]
        k = 4 * way + s
        return pltpu.make_async_remote_copy(
            src_ref=src, dst_ref=dst, send_sem=self.ss.at[k], recv_sem=self.rs.at[k],
            device_id={"tensor": self.pos.zdown if way else self.pos.zup}, device_id_type=MESH)

    def clear(self):
        for way in range(2):
            rest = pl.ds((1 - way) * self.half, self.half)
            self.slots[way][0, :, rest] = jnp.zeros_like(self.slots[way][0, :, rest])

    def step(self, s):
        for way in range(2):
            if s:
                self.copy(way, s - 1).wait_recv()
                self.add(self.slots[way].at[s - 1], self.own(self.dest(way, s)))
            self.copy(way, s).start()

    def arrive(self):
        for way in range(2):
            self.copy(way, 3).wait_recv()

    def drain(self):
        for way in range(2):
            for s in range(4):
                self.copy(way, s).wait_send()


def layer(gain, ogain, text, tid, code, cosr, sinr, dgain, fgain,
          hid_h, qkv_h, mix_h, din_h, tabs_h, dqkv, dmix_h, heads,
          loss,
          hid, hown, din, tabs, goal, wall, normed, acc, att, part, emb, er, el, eo, ei, pr, pe, po, pi, bs, br,
          cs, cr, xin, wq, wm, wh, proj, datt, fin, sums, got,
          lsem, wss, wrs, ess, ers, pss, prs, bss, brs, xss, xrs, css, crs, hss, hrs, fss, frs, tss, trs):
    p = Places()
    d, t, z, xl = p.d, p.t, p.z, p.xl

    def block_of(f):
        return lambda i: wall.at[f, i]

    deep_block = lambda i: wq.at[:, pl.ds(pl.multiple_of(i * 64, 64), 64), :]
    own_lanes = pl.ds(pl.multiple_of(xl * 128, 128), 128)
    sib_lanes = pl.ds(pl.multiple_of((1 - xl) * 128, 128), 128)
    loads = [(qkv_h.at[0], wall.at[0, d]), (qkv_h.at[1], wall.at[1, d]), (qkv_h.at[2], wall.at[2, d]),
             (mix_h, wall.at[3, d]), (tabs_h, tabs), (hid_h, hid), (din_h, din.at[xl]), (dqkv, deep_block(d)),
             (dmix_h, wm), (heads, wh.at[:, :, own_lanes])]
    loads = [pltpu.make_async_copy(src, dst, lsem.at[n]) for n, (src, dst) in enumerate(loads)]
    for one in loads:
        one.start()

    def add_books(a, b):
        def one(n, carry):
            h, c = n // 4, lax.rem(n, 4)
            a[h, c] = a[h, c] + b[h, c]
            return carry

        lax.fori_loop(0, 8, one, 0)

    def add_rows(a, b):
        def one(n, carry):
            a[n] = (a[n].astype(F32) + b[n].astype(F32)).astype(BF16)
            return carry

        lax.fori_loop(0, 3, one, 0)

    def ering_of(n):
        books = pl.ds(4 * n, 4)
        return Ring(p, lambda i: emb.at[pl.ds(2 * i, 2), books], (er.at[n], el.at[n]), 2, add_books, ess.at[n], ers.at[n])

    erings = [ering_of(n) for n in range(2)]
    pring = Ring(p, lambda i: part.at[i], (pr, pe), 64, add_rows, pss, prs)
    erings[0].clear()
    erings[1].clear()
    pring.clear()

    barrier = pltpu.get_barrier_semaphore()
    for dev in (p.xpeer, p.up, p.down, p.cpeer):
        pl.semaphore_signal(barrier, inc=1, device_id={"dp": dev}, device_id_type=MESH)

    def greet(k, carry):
        pl.semaphore_signal(barrier, inc=1, device_id={"tensor": lax.rem(t + 2 * k, TP)}, device_id_type=MESH)
        return carry

    lax.fori_loop(1, NZ, greet, 0)
    pl.semaphore_signal(barrier, inc=1, device_id={"tensor": p.xsib}, device_id_type=MESH)
    pl.semaphore_wait(barrier, 4 + NZ)

    def flow(f):
        return Flow(p, wall.at[f, d], block_of(f), lambda k: wss.at[f, k], lambda k: wrs.at[f, k])

    def qkv_flows(act):
        def one(f, carry):
            act(flow(f))
            return carry

        lax.fori_loop(0, 3, one, 0)

    mixer = flow(3)
    deep = Flow(p, dqkv, deep_block, lambda k: wss.at[4, k], lambda k: wrs.at[4, k])
    for n in range(3):
        loads[n].wait()
    qkv_flows(lambda f: f.start0())

    codev = code[...].astype(F32)
    pick = lax.broadcasted_iota(jnp.int32, codev.shape, 1)
    count = text.shape[0]
    whole = count // 128 * 128
    square_r = lax.broadcasted_iota(jnp.int32, (128, 128), 0)
    square_c = lax.broadcasted_iota(jnp.int32, (128, 128), 1)
    halves = [jnp.sum(jnp.where(square_r == square_c, jnp.broadcast_to(tid[h:h + 1].astype(F32), (128, 128)), 0.0),
                      axis=1, keepdims=True) for h in range(2)]
    text_want = jnp.concatenate(halves, axis=0) - (t * count).astype(F32)

    def named(want, start, width):
        lanes = lax.broadcasted_iota(jnp.int32, (FRAMES, width), 1).astype(F32) + start
        return (lanes == want).astype(BF16)

    found = dot(named(text_want, 0, whole), text[:whole])
    if count > whole:
        found = found + dot(named(text_want, whole, count - whole), text[whole:])
    emb[:, 0] = found.astype(BF16).reshape(TP, OWN, DD)
    loads[4].wait()

    def lookup(c, carry):
        want = jnp.sum(jnp.where(pick == c - 1, codev, 0.0), axis=1, keepdims=True) - (t * 128).astype(F32)
        emb[:, c] = dot(named(want, 0, 128), tabs[c - 1]).astype(BF16).reshape(TP, OWN, DD)
        return carry

    lax.fori_loop(1, 4, lookup, 0)
    erings[0].step(0)
    lax.fori_loop(4, CODEBOOKS, lookup, 0)
    erings[1].step(0)
    loads[5].wait()

    def norm_rows(n, carry):
        r = pl.ds(pl.multiple_of(n * 32, 32), 32)
        h = hid[r, :].astype(F32)
        scale = lax.rsqrt(jnp.mean(h * h, axis=-1, keepdims=True) + epsilon)
        normed[r, :] = (h * scale * gain[...]).astype(BF16)
        return carry

    lax.fori_loop(0, FRAMES // 32, norm_rows, 0)

    def side_rows(n, carry):
        frames = pl.ds(pl.multiple_of(n * 32 + xl * 16, 16), OWN)
        to = pl.ds(pl.multiple_of(n * 16, 16), OWN)
        hown[to, :] = hid[frames, pl.ds(pl.multiple_of(z * 512, 512), 512)]
        goal[to, :] = code[frames, :]
        return carry

    lax.fori_loop(0, NZ, side_rows, 0)
    def project(ns, first=False):
        for n in ns:
            for f in range(3):
                flow(f).core_in(n)
        y = p.blocks[ns[0]] // 4
        cols = normed[:, pl.ds(pl.multiple_of(y * 1024, 1024), 1024)]

        def one(i, carry):
            got_one = dot(cols, wall[i, pl.ds(4 * y, 4)].reshape(1024, 256))
            acc[i] = got_one if first else acc[i] + got_one
            return carry

        lax.fori_loop(0, 3, one, 0)

    flow(0).stage1()
    erings[0].step(1)
    flow(1).stage1()
    erings[1].step(1)
    flow(2).stage1()
    loads[3].wait()
    mixer.start0()
    din_x = pltpu.make_async_remote_copy(
        src_ref=din_h, dst_ref=din.at[xl], send_sem=hss.at[2], recv_sem=hrs.at[2],
        device_id={"tensor": p.xsib}, device_id_type=MESH)
    din_x.start()
    head_part = pl.ds(p.core * 4, 4)
    head_rest = pl.ds(4 - p.core * 4, 4)
    head_x = pltpu.make_async_remote_copy(
        src_ref=heads.at[head_part], dst_ref=wh.at[head_part, :, own_lanes], send_sem=hss.at[0],
        recv_sem=hrs.at[0], device_id={"tensor": p.xsib}, device_id_type=MESH)
    project((0, 1), True)
    flow(0).stage2()
    erings[0].step(2)
    flow(1).stage2()
    flow(2).stage2()
    mixer.stage1()
    erings[1].step(2)
    project((2, 4))
    project((3, 5))
    for f in range(3):
        flow(f).stage3()
    mixer.stage2()
    loads[7].wait()
    deep.start0()
    erings[0].step(3)
    project((6, 7))

    order_q = lax.broadcasted_iota(jnp.int32, (FRAMES, FRAMES), 0)
    order_k = lax.broadcasted_iota(jnp.int32, (FRAMES, FRAMES), 1)
    causal = order_q >= order_k

    def rotate(v):
        half = HEAD_DIM // 2
        swapped = jnp.concatenate([v[:, half:], v[:, :half]], axis=1)
        return (v * cosr[...] + swapped * sinr[...]).astype(BF16)

    def attend(h, carry):
        cols = pl.ds(pl.multiple_of(h * HEAD_DIM, HEAD_DIM), HEAD_DIM)
        q = rotate(acc[0, :, cols])
        k = rotate(acc[1, :, cols])
        v = acc[2, :, cols].astype(BF16)
        scores = dot_t(q, k) * HEAD_DIM ** (-0.5)
        e = jnp.where(causal, jnp.exp(jnp.where(causal, scores, 0.0)), 0.0)
        w = (e / jnp.sum(e, axis=-1, keepdims=True)).astype(BF16)
        mixed_rows = dot(w, v).astype(BF16).reshape(NZ, 2, OWN, HEAD_DIM)
        for side in range(2):
            att[side * 128:side * 128 + 128, cols] = mixed_rows[:, side].reshape(128, HEAD_DIM)
        return carry

    lax.fori_loop(0, 2, attend, 0)
    erings[1].step(3)
    mixer.stage3()
    mixer.stage4()

    def cross(zz):
        return pltpu.make_async_remote_copy(
            src_ref=bs.at[zz], dst_ref=br.at[zz], send_sem=bss.at[zz], recv_sem=brs.at[zz],
            device_id={"tensor": p.xsib}, device_id_type=MESH)

    def near_far(n):
        step = (n + 1) // 2
        return lax.rem(z + 4 + jnp.where(lax.rem(n, 2) == 1, -step, step), NZ)

    def mixed(n, carry):
        zz = near_far(n)
        second = wall[3, 2 * zz + 1]
        bs[zz] = dot(att[pl.ds(pl.multiple_of(128 - 128 * xl, 128), 128), :], second).astype(BF16)
        cross(zz).start()
        part[zz, 2] = dot(att[pl.ds(pl.multiple_of(128 * xl, 128), 128), :], second).astype(BF16)
        one = dot(att[...], wall[3, 2 * zz]).astype(BF16)
        part[zz, 0] = one[:128]
        part[zz, 1] = one[128:]
        return carry

    lax.fori_loop(0, NZ, mixed, 0)
    head_x.start()

    def crossed(n, carry):
        zz = near_far(n)
        cross(zz).wait_recv()
        part[zz, 2] = (part[zz, 2].astype(F32) + br[zz].astype(F32)).astype(BF16)
        return carry

    crossed(0, 0)
    pring.step(0)
    lax.fori_loop(1, NZ, crossed, 0)
    pring.step(1)
    pring.step(2)
    deep.stage1()

    def swap(src, dst, k):
        return pltpu.make_async_remote_copy(
            src_ref=src, dst_ref=dst, send_sem=xss.at[k], recv_sem=xrs.at[k],
            device_id={"tensor": p.xsib}, device_id_type=MESH)

    pring.step(3)
    for n in range(2):
        erings[n].arrive()
        mine = pl.ds(4 * n, 4)
        eo[mine] = emb[2 * z + 1 - xl, mine] + er[n, 3, 1 - xl] + el[n, 3, 1 - xl]
    swap(eo, ei, 0).start()
    pring.arrive()

    def total(h):
        return part[z, h].astype(F32) + pr[3, h].astype(F32) + pe[3, h].astype(F32)

    po[...] = total(1 - xl).astype(BF16)
    swap(po, pi, 1).start()
    loads[6].wait()
    din_x.wait_recv()

    def scale_cols(b, summed):
        resid = summed + hown[:, b * 256:b * 256 + 256].astype(F32)
        gains = ogain[:, pl.ds(pl.multiple_of(z * 512 + b * 256, 256), 256)]
        return jnp.sum(resid * resid, axis=-1, keepdims=True), dot((resid * gains).astype(BF16), din[b])

    square, context = scale_cols(1, total(2))
    swap(po, pi, 1).wait_recv()
    square_b, context_b = scale_cols(0, total(xl) + pi[...].astype(F32))
    square = square + square_b
    cs[:, :, :DD] = (context + context_b).astype(BF16).reshape(NZ, OWN, DD)
    high = square.astype(BF16)
    low = (square - high.astype(F32)).astype(BF16)
    first = lax.broadcasted_iota(jnp.int32, (128, 128), 1) < 64
    both = jnp.where(first, high.astype(F32), low.astype(F32)).astype(BF16)
    cs[:, :, DD:] = both.reshape(NZ, OWN, 128)

    def share(k, sender):
        to = lax.rem(z + k, NZ)
        return pltpu.make_async_remote_copy(
            src_ref=cs.at[to], dst_ref=cr.at[sender], send_sem=css.at[k], recv_sem=crs.at[k],
            device_id={"tensor": 2 * to + xl}, device_id_type=MESH)

    def give(n, carry):
        share(lax.rem(near_far(n) - z + NZ, NZ), z).start()
        return carry

    lax.fori_loop(0, NZ - 1, give, 0)
    deep.stage2()
    cr[z] = cs[z]
    swap(eo, ei, 0).wait_recv()
    embeds = [emb[2 * z + xl, pl.ds(4 * n, 4)].astype(F32) + er[n, 3, xl].astype(F32) + el[n, 3, xl].astype(F32)
              + ei[pl.ds(4 * n, 4)].astype(F32) for n in range(2)]
    xin[...] = jnp.concatenate(embeds, axis=0).reshape(CODEBOOKS * OWN, DD)

    def take(k, carry):
        share(k, lax.rem(z + NZ - k, NZ)).wait_recv()
        return carry

    lax.fori_loop(1, NZ, take, 0)

    def gathered(n, carry):
        context, square = carry
        v = cr[n]
        hl = v[:, DD:].astype(F32)
        return context + v[:, :DD].astype(F32), square + hl[:, :1] + hl[:, 64:65]

    context, square = lax.fori_loop(0, NZ, gathered, (jnp.zeros((OWN, DD), F32), jnp.zeros((OWN, 1), F32)))
    context = context * lax.rsqrt(square / D + epsilon)
    deep.stage3()

    rows = CODEBOOKS * OWN
    x = (context[None] + xin[...].reshape(CODEBOOKS, OWN, DD)).reshape(rows, DD)
    dn = (x * lax.rsqrt(jnp.mean(x * x, axis=-1, keepdims=True) + epsilon) * dgain[...]).astype(BF16)
    deep.stage4()

    def dproject(i, carry):
        proj[i] = dot(dn, wq[i]).astype(BF16)
        return carry

    lax.fori_loop(0, 3, dproject, 0)
    head_x_in = pltpu.make_async_remote_copy(
        src_ref=wh.at[head_part, :, sib_lanes], dst_ref=wh.at[head_part, :, sib_lanes], send_sem=hss.at[1],
        recv_sem=hrs.at[0], device_id={"dp": p.cpeer}, device_id_type=MESH)
    head_x_in.wait_recv()
    head_c = pltpu.make_async_remote_copy(
        src_ref=wh.at[head_part, :, sib_lanes], dst_ref=wh.at[head_part, :, sib_lanes], send_sem=hss.at[1],
        recv_sem=hrs.at[1], device_id={"dp": p.cpeer}, device_id_type=MESH)
    head_c.start()

    rq = lax.broadcasted_iota(jnp.int32, (rows, rows), 0)
    rk = lax.broadcasted_iota(jnp.int32, (rows, rows), 1)
    seen = (lax.rem(rq, OWN) == lax.rem(rk, OWN)) & (rq >= rk)
    low_half = lax.broadcasted_iota(jnp.int32, (rows, 128), 1) < DHEAD_DIM

    def dattend(j, carry):
        cols = pl.ds(pl.multiple_of(j * 128, 128), 128)
        q, k, v = proj[0, :, cols], proj[1, :, cols], proj[2, :, cols]
        parts = []
        for half in (low_half, jnp.logical_not(low_half)):
            scores = dot_t(jnp.where(half, q, jnp.zeros_like(q)), k) * DHEAD_DIM ** (-0.5)
            e = jnp.where(seen, jnp.exp(jnp.where(seen, scores, 0.0)), 0.0)
            w = (e / jnp.sum(e, axis=-1, keepdims=True)).astype(BF16)
            parts.append(dot(w, v))
        datt[:, cols] = jnp.where(low_half, parts[0], parts[1]).astype(BF16)
        return carry

    lax.fori_loop(0, DHEADS // 2, dattend, 0, unroll=4)
    loads[8].wait()
    out = x + dot(datt[...], wm[...])
    final = (out * lax.rsqrt(jnp.mean(out * out, axis=-1, keepdims=True) + epsilon) * fgain[...]).astype(BF16)
    fin[:, z] = final.reshape(CODEBOOKS, OWN, DD)

    def ring(way, s, block):
        books = pl.ds(0, CODEBOOKS) if s < 3 else pl.ds(4 * way, 4)
        view = fin.at[books, block]
        return pltpu.make_async_remote_copy(
            src_ref=view, dst_ref=view, send_sem=fss.at[4 * way + s], recv_sem=frs.at[4 * way + s],
            device_id={"tensor": p.zdown if way else p.zup}, device_id_type=MESH)

    for s in range(4):
        for way in range(2):
            block = lax.rem(z + (s if way else NZ - s), NZ)
            if s:
                ring(way, s - 1, block).wait_recv()
            ring(way, s, block).start()
    far = lax.rem(z + 4, NZ)
    ring(0, 3, far).wait_recv()
    ring(1, 3, far).wait_recv()

    loads[9].wait()
    pltpu.make_async_remote_copy(
        src_ref=wh.at[head_rest, :, sib_lanes], dst_ref=wh.at[head_rest, :, sib_lanes], send_sem=hss.at[1],
        recv_sem=hrs.at[1], device_id={"dp": p.cpeer}, device_id_type=MESH).wait_recv()
    shared = OWN * NZ
    lanes = lax.broadcasted_iota(jnp.int32, (shared, 256), 1).astype(F32)
    spots = lax.broadcasted_iota(jnp.int32, (shared, 128), 1)
    goals = goal[...].astype(F32) - (z * 256).astype(F32)
    books = lax.broadcasted_iota(jnp.int32, goals.shape, 1)

    def book(c, total):
        logits = dot(fin[c].reshape(shared, DD), wh[c])
        e = jnp.sum(jnp.exp(logits), axis=-1, keepdims=True)
        want = jnp.sum(jnp.where(books == c, goals, 0.0), axis=1, keepdims=True)
        hit = jnp.sum(jnp.where(lanes == want, logits, 0.0), axis=-1, keepdims=True)
        total = jnp.where(spots == c, e, total)
        return jnp.where(spots == CODEBOOKS + c, hit, total)

    sums[...] = lax.fori_loop(0, CODEBOOKS, book, jnp.zeros((shared, 128), F32)).reshape(NZ, OWN, 128)

    def reply(k, sender):
        to = lax.rem(z + k, NZ)
        return pltpu.make_async_remote_copy(
            src_ref=sums.at[to], dst_ref=got.at[sender], send_sem=tss.at[k], recv_sem=trs.at[k],
            device_id={"tensor": 2 * to + xl}, device_id_type=MESH)

    def start_reply(k, carry):
        reply(k, z).start()
        return carry

    def take_reply(k, carry):
        reply(k, lax.rem(z + NZ - k, NZ)).wait_recv()
        return carry

    lax.fori_loop(1, NZ, start_reply, 0)
    got[z] = sums[z]
    lax.fori_loop(1, NZ, take_reply, 0)
    both = got[0]
    for n in range(1, NZ):
        both = both + got[n]
    loss[...] = jnp.log(both[:, :CODEBOOKS]) - both[:, CODEBOOKS:2 * CODEBOOKS]

    qkv_flows(lambda f: f.drain())
    mixer.drain()
    deep.drain()
    erings[0].drain()
    erings[1].drain()
    din_x.wait_send()
    pring.drain()
    swap(eo, ei, 0).wait_send()
    swap(po, pi, 1).wait_send()
    head_x.wait_send()
    head_c.wait_send()

    def sent(k, carry):
        cross(k).wait_send()
        return carry

    def sent_far(k, carry):
        share(k, z).wait_send()
        reply(k, z).wait_send()
        return carry

    lax.fori_loop(0, NZ, sent, 0)
    lax.fori_loop(1, NZ, sent_far, 0)
    for s in range(4):
        for way in range(2):
            ring(way, s, z).wait_send()


def shards(hidden_in, attn_gain, qkv_weight, mix_weight, out_gain, depth_in_weight, text_table, code_tables,
           depth_gain, depth_qkv, depth_mix, final_gain, heads_weight, text_ids, codes):
    half = HEAD_DIM // 2
    angles = np.arange(FRAMES)[:, None] * 10000.0 ** (-np.arange(half) / half)[None, :]
    cosv = np.concatenate([np.cos(angles)] * 2, axis=1).astype(np.float32)
    sinv = np.concatenate([-np.sin(angles), np.sin(angles)], axis=1).astype(np.float32)
    vmem = pl.BlockSpec(memory_space=pltpu.VMEM)
    anym = pl.BlockSpec(memory_space=pl.ANY)
    dma = pltpu.SemaphoreType.DMA
    b16 = lambda *shape: pltpu.VMEM(shape, BF16)
    f32 = lambda *shape: pltpu.VMEM(shape, F32)
    wide = DD + 128
    return pl.pallas_call(
        layer,
        out_shape=jax.ShapeDtypeStruct((OWN, CODEBOOKS), F32),
        in_specs=[vmem] * 9 + [anym] * 8,
        out_specs=vmem,
        scratch_shapes=[
            b16(FRAMES, D), b16(128, 512), b16(2, 256, DD), b16(CODEBOOKS - 1, 128, DD),
            pltpu.VMEM((128, CODEBOOKS), jnp.int32),
            b16(4, DP, 256, 256), b16(FRAMES, D), f32(3, FRAMES, 256), b16(FRAMES, 256),
            b16(NZ, 3, 128, 256),
            b16(TP, CODEBOOKS, OWN, DD),
            b16(2, 4, 2, 4, OWN, DD), b16(2, 4, 2, 4, OWN, DD),
            b16(CODEBOOKS, OWN, DD), b16(CODEBOOKS, OWN, DD),
            b16(4, 3, 128, 256), b16(4, 3, 128, 256), b16(128, 256), b16(128, 256),
            b16(NZ, 128, 256), b16(NZ, 128, 256),
            b16(NZ, OWN, wide), b16(NZ, OWN, wide), f32(CODEBOOKS * OWN, DD),
            b16(3, DD, DD), b16(DD, DD), b16(CODEBOOKS, DD, 256),
            b16(3, CODEBOOKS * OWN, DD), b16(CODEBOOKS * OWN, DD),
            b16(CODEBOOKS, NZ, OWN, DD), f32(NZ, OWN, 128), f32(NZ, OWN, 128),
            dma((10,)),
            dma((5, 15)), dma((5, 15)),
            dma((2, 8)), dma((2, 8)),
            dma((8,)), dma((8,)),
            dma((NZ,)), dma((NZ,)),
            dma((2,)), dma((2,)),
            dma((NZ,)), dma((NZ,)),
            dma((3,)), dma((3,)),
            dma((8,)), dma((8,)),
            dma((NZ,)), dma((NZ,)),
        ],
        compiler_params=pltpu.CompilerParams(
            collective_id=0, has_side_effects=True, vmem_limit_bytes=60 * 2**20),
        name="layer",
    )(attn_gain[None], out_gain[None], text_table, text_ids.reshape(2, 128), codes, cosv, sinv, depth_gain[None],
      final_gain[None],
      hidden_in, qkv_weight, mix_weight, depth_in_weight, code_tables, depth_qkv, depth_mix, heads_weight)


def solution(mesh):
    in_specs = (
        P("dp", None),
        P(),
        P(None, "dp", "tensor"),
        P("tensor", "dp"),
        P(),
        P("tensor", None),
        P("tensor", None),
        P(None, "tensor", None),
        P(),
        P(None, "dp", None),
        P(),
        P(),
        P(None, None, "tensor"),
        P("dp"),
        P("dp", None),
    )
    out_specs = P(("dp", "tensor"), None)
    return jax.shard_map(shards, mesh=mesh, in_specs=in_specs, out_specs=out_specs, check_vma=False)
```

```python
import functools

import jax
import jax.numpy as jnp
import numpy as np
from jax import lax
from jax.experimental import pallas as pl
from jax.experimental.pallas import tpu as pltpu
from jax.sharding import PartitionSpec as P

D = 4096
HEAD_DIM = 128
FRAMES = 256
DD = 1024
DHEADS = 16
DHEAD_DIM = 64
CODEBOOKS = 8
DP = 16
TP = 16
NZ = 8
OWN = 16
F32 = jnp.float32
BF16 = jnp.bfloat16
MESH = pl.DeviceIdType.MESH

epsilon = 1e-05

X0, R1, L1, R2, L2, R3, L3, C0 = range(8)


def dot(a, b):
    return jnp.dot(a, b, preferred_element_type=F32)


def dot_t(a, b):
    return lax.dot_general(a, b, (((1,), (1,)), ((), ())), preferred_element_type=F32)


class Places:
    def __init__(self):
        d = lax.axis_index("dp")
        t = lax.axis_index("tensor")
        self.d, self.t = d, t
        self.core = lax.rem(d, 2)
        self.xh = lax.rem(d // 2, 2)
        self.xl = lax.rem(t, 2)
        self.z = t // 2
        self.up = lax.rem(d + 4, 16)
        self.down = lax.rem(d + 12, 16)
        self.far = lax.rem(d + 8, 16)
        self.xstep = 2 - 4 * self.xh
        self.xpeer = d + self.xstep
        self.cstep = 1 - 2 * self.core
        self.cpeer = d + self.cstep
        self.xsib = t + 1 - 2 * self.xl
        self.zup = lax.rem(t + 2, 16)
        self.zdown = lax.rem(t + 14, 16)
        self.blocks = [d, self.xpeer, self.down, self.up, self.down + self.xstep,
                       self.up + self.xstep, self.far, self.far + self.xstep]


class Flow:
    def __init__(self, pos, own, block, send_sem, recv_sem):
        self.pos, self.own, self.block = pos, own, block
        self.ss, self.rs = send_sem, recv_sem

    def copy(self, kind, idx, dev, own=False):
        src = self.own if own else self.block(idx)
        return pltpu.make_async_remote_copy(
            src_ref=src, dst_ref=self.block(idx), send_sem=self.ss(kind), recv_sem=self.rs(kind),
            device_id={"dp": dev}, device_id_type=MESH)

    def start0(self):
        p = self.pos
        for kind, dev in ((X0, p.xpeer), (R1, p.up), (L1, p.down), (C0, p.cpeer)):
            self.copy(kind, p.d, dev, own=True).start()

    def core_in(self, n):
        p = self.pos
        self.copy(C0 + n, p.blocks[n] + p.cstep, p.cpeer).wait_recv()

    def got(self, kind):
        p = self.pos
        self.copy(kind, p.blocks[kind + 1], p.cpeer).wait_recv()

    def forward(self, kind, idx, dev):
        self.copy(kind, idx, dev).start()

    def to_core(self, kind):
        p = self.pos
        self.forward(C0 + kind + 1, p.blocks[kind + 1], p.cpeer)

    def stage1(self):
        p = self.pos
        self.got(X0)
        self.forward(R2, p.xpeer, p.up)
        self.forward(L2, p.xpeer, p.down)
        self.to_core(X0)
        self.got(R1)
        self.forward(R3, p.down, p.up)
        self.to_core(R1)
        self.got(L1)
        self.to_core(L1)

    def stage2(self):
        p = self.pos
        self.got(R2)
        self.to_core(R2)
        self.got(L2)
        self.forward(L3, p.up + p.xstep, p.down)
        self.to_core(L2)

    def stage3(self):
        self.got(R3)
        self.to_core(R3)
        self.got(L3)
        self.to_core(L3)

    def stage4(self):
        p = self.pos
        for n in range(8):
            self.core_in(n)

    def drain(self):
        p = self.pos
        for kind in range(15):
            self.copy(kind, p.d, p.cpeer).wait_send()


class FlowDeep(Flow):
    def start0(self):
        p = self.pos
        pltpu.make_async_remote_copy(
            src_ref=self.own, dst_ref=self.block(p.d), send_sem=self.ss(X0), recv_sem=self.rs(X0),
            device_id={"dp": p.xpeer, "tensor": p.xsib}, device_id_type=MESH).start()
        for kind, dev in ((R1, p.up), (L1, p.down), (C0, p.cpeer)):
            self.copy(kind, p.d, dev, own=True).start()


class FlowY(Flow):
    def half(self, kind, idx, dev, which):
        view = self.block(idx).at[pl.ds(which * 128, 128)]
        return pltpu.make_async_remote_copy(
            src_ref=view, dst_ref=view, send_sem=self.ss(kind), recv_sem=self.rs(kind),
            device_id={"dp": dev}, device_id_type=MESH)

    def start0(self):
        p = self.pos
        for kind, dev in ((R1, p.up), (L1, p.down), (X0, p.xpeer), (C0, p.cpeer)):
            self.copy(kind, p.d, dev, own=True).start()

    def across(self, kind, idx):
        self.forward(kind, idx, self.pos.xpeer)

    def stage1(self):
        p = self.pos
        self.got(R1)
        self.half(L3, p.down, p.up, 0).start()
        self.across(R2, p.down)
        self.forward(C0 + 2, p.down, p.cpeer)
        self.got(L1)
        self.half(15, p.up, p.down, 1).start()
        self.across(L2, p.up)
        self.forward(C0 + 3, p.up, p.cpeer)
        self.got(X0)
        self.forward(C0 + 1, p.xpeer, p.cpeer)

    def stage2(self):
        p = self.pos
        self.half(L3, p.far, p.up, 0).wait_recv()
        self.half(15, p.far, p.down, 1).wait_recv()
        self.across(R3, p.far)
        self.forward(C0 + 6, p.far, p.cpeer)
        self.got(R2)
        self.forward(C0 + 4, p.blocks[4], p.cpeer)
        self.got(L2)
        self.forward(C0 + 5, p.blocks[5], p.cpeer)

    def stage3(self):
        p = self.pos
        self.got(R3)
        self.forward(C0 + 7, p.blocks[7], p.cpeer)

    def drain(self):
        p = self.pos
        for kind in range(16):
            if kind in (L3, 15):
                self.half(kind, p.d, p.up, 0).wait_send()
            else:
                self.copy(kind, p.d, p.cpeer).wait_send()


class Ring:
    def __init__(self, pos, own, slots, long, add, ss, rs):
        self.pos, self.own, self.slots, self.long, self.add = pos, own, slots, long, add
        self.ss, self.rs = ss, rs

    def first(self, way):
        return 0 if way == self.long else 1

    def dest(self, way, s):
        return lax.rem(self.pos.z + (4 - s if way == 0 else 4 + s), NZ)

    def copy(self, way, s):
        slots = self.slots[way]
        src = self.own(self.dest(way, s)) if s == self.first(way) else slots.at[s - 1]
        k = 4 * way + s
        return pltpu.make_async_remote_copy(
            src_ref=src, dst_ref=slots.at[s], send_sem=self.ss.at[k], recv_sem=self.rs.at[k],
            device_id={"tensor": self.pos.zdown if way else self.pos.zup}, device_id_type=MESH)

    def step(self, s):
        for way in range(2):
            if s < self.first(way):
                continue
            if s > self.first(way):
                self.copy(way, s - 1).wait_recv()
                self.add(self.slots[way].at[s - 1], self.own(self.dest(way, s)))
            self.copy(way, s).start()

    def arrive(self):
        for way in range(2):
            self.copy(way, 3).wait_recv()

    def drain(self):
        for way in range(2):
            for s in range(self.first(way), 4):
                self.copy(way, s).wait_send()


def layer(gain, ogain, tid, code, cosr, sinr, dgain, fgain,
          hid_h, text_h, qkv_h, mix_h, din_h, tabs_h, dqkv, dmix_h, heads,
          loss,
          hid, text, hown, din, tabs, goal, wall, normed, acc, att, part, emb, er, el, eo, ei, pr, pe, po, pi, bs, br,
          cs, cr, xin, wq, wm, wh, hx, proj, datt, fin, sums, got,
          lsem, wss, wrs, ess, ers, pss, prs, bss, brs, xss, xrs, css, crs, hss, hrs, fss, frs, tss, trs):
    p = Places()
    d, t, z, xl = p.d, p.t, p.z, p.xl

    def block_of(f):
        return lambda i: wall.at[f, i]

    deep_block = lambda i: wq.at[:, pl.ds(pl.multiple_of(i * 64, 64), 64), :]
    own_lanes = pl.ds(pl.multiple_of(xl * 128, 128), 128)
    sib_lanes = pl.ds(pl.multiple_of((1 - xl) * 128, 128), 128)
    loads = [(qkv_h.at[0], wall.at[0, d]), (qkv_h.at[1], wall.at[1, d]), (qkv_h.at[2], wall.at[2, d]),
             (mix_h, wall.at[3, d]), (tabs_h, tabs), (hid_h, hid), (din_h, din.at[xl]), (dqkv, deep_block(d)),
             (dmix_h, wm), (heads, wh.at[:, :, own_lanes]), (text_h, text)]
    loads = [pltpu.make_async_copy(src, dst, lsem.at[n]) for n, (src, dst) in enumerate(loads)]
    for one in loads:
        one.start()

    def add_books(a, b):
        def one(n, carry):
            h, c = n // 4, lax.rem(n, 4)
            a[h, c] = a[h, c] + b[h, c]
            return carry

        lax.fori_loop(0, 8, one, 0)

    def add_rows(a, b):
        def one(n, carry):
            a[n] = (a[n].astype(F32) + b[n].astype(F32)).astype(BF16)
            return carry

        lax.fori_loop(0, 3, one, 0)

    def ering_of(n):
        books = pl.ds(4 * n, 4)
        return Ring(p, lambda i: emb.at[pl.ds(2 * i, 2), books], (er.at[n], el.at[n]), n, add_books, ess.at[n], ers.at[n])

    erings = [ering_of(n) for n in range(2)]

    def pring_of(n):
        rows = pl.ds(64 * n, 64)
        return Ring(p, lambda i: part.at[i, :, rows], (pr.at[n], pe.at[n]), n, add_rows, pss.at[n], prs.at[n])

    prings = [pring_of(n) for n in range(2)]

    barrier = pltpu.get_barrier_semaphore()
    for dev in (p.xpeer, p.up, p.down, p.cpeer):
        pl.semaphore_signal(barrier, inc=1, device_id={"dp": dev}, device_id_type=MESH)

    def greet(k, carry):
        pl.semaphore_signal(barrier, inc=1, device_id={"tensor": lax.rem(t + 2 * k, TP)}, device_id_type=MESH)
        return carry

    lax.fori_loop(1, NZ, greet, 0)
    pl.semaphore_signal(barrier, inc=1, device_id={"tensor": p.xsib}, device_id_type=MESH)
    pl.semaphore_signal(barrier, inc=1, device_id={"dp": p.xpeer, "tensor": p.xsib}, device_id_type=MESH)
    pl.semaphore_wait(barrier, 5 + NZ)

    def flow(f):
        kind = FlowY if f == 2 else Flow
        return kind(p, wall.at[f, d], block_of(f), lambda k: wss.at[f, k], lambda k: wrs.at[f, k])

    mixer = flow(3)
    deep = FlowDeep(p, dqkv, deep_block, lambda k: wss.at[4, k], lambda k: wrs.at[4, k])
    for n in range(3):
        loads[n].wait()
    for f in range(3):
        flow(f).start0()

    codev = code[...].astype(F32)
    pick = lax.broadcasted_iota(jnp.int32, codev.shape, 1)
    count = text.shape[0]
    whole = count // 128 * 128
    square_r = lax.broadcasted_iota(jnp.int32, (128, 128), 0)
    square_c = lax.broadcasted_iota(jnp.int32, (128, 128), 1)
    halves = [jnp.sum(jnp.where(square_r == square_c, jnp.broadcast_to(tid[h:h + 1].astype(F32), (128, 128)), 0.0),
                      axis=1, keepdims=True) for h in range(2)]
    text_want = jnp.concatenate(halves, axis=0) - (t * count).astype(F32)

    def named(want, start, width):
        lanes = lax.broadcasted_iota(jnp.int32, (FRAMES, width), 1).astype(F32) + start
        return (lanes == want).astype(BF16)

    loads[10].wait()
    found = dot(named(text_want, 0, whole), text[:whole])
    if count > whole:
        found = found + dot(named(text_want, whole, count - whole), text[whole:])
    emb[:, 0] = found.astype(BF16).reshape(TP, OWN, DD)
    loads[4].wait()

    def lookup(c, carry):
        want = jnp.sum(jnp.where(pick == c - 1, codev, 0.0), axis=1, keepdims=True) - (t * 128).astype(F32)
        emb[:, c] = dot(named(want, 0, 128), tabs[c - 1]).astype(BF16).reshape(TP, OWN, DD)
        return carry

    lax.fori_loop(1, 4, lookup, 0)
    erings[0].step(0)
    lax.fori_loop(4, CODEBOOKS, lookup, 0)
    erings[1].step(0)
    loads[5].wait()

    def norm_rows(n, carry):
        r = pl.ds(pl.multiple_of(n * 32, 32), 32)
        h = hid[r, :].astype(F32)
        scale = lax.rsqrt(jnp.mean(h * h, axis=-1, keepdims=True) + epsilon)
        normed[r, :] = (h * scale * gain[...]).astype(BF16)
        return carry

    lax.fori_loop(0, FRAMES // 32, norm_rows, 0)

    def side_rows(n, carry):
        frames = pl.ds(pl.multiple_of(n * 32 + xl * 16, 16), OWN)
        to = pl.ds(pl.multiple_of(n * 16, 16), OWN)
        hown[to, :] = hid[frames, pl.ds(pl.multiple_of(z * 512, 512), 512)]
        goal[to, :] = code[frames, :]
        return carry

    lax.fori_loop(0, NZ, side_rows, 0)
    def project(ns, first=False):
        for n in ns:
            for f in range(3):
                flow(f).core_in(n)
        y = p.blocks[ns[0]] // 4
        cols = normed[:, pl.ds(pl.multiple_of(y * 1024, 1024), 1024)]

        def one(i, carry):
            got_one = dot(cols, wall[i, pl.ds(4 * y, 4)].reshape(1024, 256))
            acc[i] = got_one if first else acc[i] + got_one
            return carry

        lax.fori_loop(0, 3, one, 0, unroll=3)

    flow(0).stage1()
    erings[0].step(1)
    flow(1).stage1()
    erings[1].step(1)
    flow(2).stage1()
    loads[3].wait()
    mixer.start0()
    project((0, 1), True)
    flow(0).stage2()
    erings[0].step(2)
    flow(1).stage2()
    flow(2).stage2()
    mixer.stage1()
    erings[1].step(2)
    project((2, 4))
    for f in range(3):
        flow(f).stage3()
    mixer.stage2()
    loads[7].wait()
    deep.start0()
    din_part = pl.ds(pl.multiple_of(128 * p.core, 128), 128)
    din_rest = pl.ds(pl.multiple_of(128 - 128 * p.core, 128), 128)
    din_x = pltpu.make_async_remote_copy(
        src_ref=din_h.at[din_part], dst_ref=din.at[xl, din_part], send_sem=hss.at[2], recv_sem=hrs.at[2],
        device_id={"tensor": p.xsib}, device_id_type=MESH)
    din_x.start()

    def din_core(some):
        view = din.at[1 - xl, some]
        return pltpu.make_async_remote_copy(
            src_ref=view, dst_ref=view, send_sem=hss.at[3], recv_sem=hrs.at[3],
            device_id={"dp": p.cpeer}, device_id_type=MESH)

    project((3, 5))
    erings[0].step(3)
    project((6, 7))

    order_q = lax.broadcasted_iota(jnp.int32, (FRAMES, FRAMES), 0)
    order_k = lax.broadcasted_iota(jnp.int32, (FRAMES, FRAMES), 1)
    causal = order_q >= order_k

    def rotate(v):
        half = HEAD_DIM // 2
        swapped = jnp.concatenate([v[:, half:], v[:, :half]], axis=1)
        return (v * cosr[...] + swapped * sinr[...]).astype(BF16)

    def attend(h, carry):
        cols = pl.ds(pl.multiple_of(h * HEAD_DIM, HEAD_DIM), HEAD_DIM)
        q = rotate(acc[0, :, cols])
        k = rotate(acc[1, :, cols])
        v = acc[2, :, cols].astype(BF16)
        scores = dot_t(q, k) * HEAD_DIM ** (-0.5)
        e = jnp.where(causal, jnp.exp(jnp.where(causal, scores, 0.0)), 0.0)
        w = (e / jnp.sum(e, axis=-1, keepdims=True)).astype(BF16)
        mixed_rows = dot(w, v).astype(BF16).reshape(NZ, 2, OWN, HEAD_DIM)
        for side in range(2):
            att[side * 128:side * 128 + 128, cols] = mixed_rows[:, side].reshape(128, HEAD_DIM)
        return carry

    lax.fori_loop(0, 2, attend, 0, unroll=2)
    erings[1].step(3)
    mixer.stage3()
    mixer.stage4()

    def cross(zz):
        return pltpu.make_async_remote_copy(
            src_ref=bs.at[zz], dst_ref=br.at[zz], send_sem=bss.at[zz], recv_sem=brs.at[zz],
            device_id={"tensor": p.xsib}, device_id_type=MESH)

    def near_far(n):
        step = (n + 1) // 2
        return lax.rem(z + 4 + jnp.where(lax.rem(n, 2) == 1, -step, step), NZ)

    def mixed(n, carry):
        zz = near_far(n)
        second = wall[3, 2 * zz + 1]
        bs[zz] = dot(att[pl.ds(pl.multiple_of(128 - 128 * xl, 128), 128), :], second).astype(BF16)
        cross(zz).start()
        part[zz, 2] = dot(att[pl.ds(pl.multiple_of(128 * xl, 128), 128), :], second).astype(BF16)
        one = dot(att[...], wall[3, 2 * zz]).astype(BF16)
        part[zz, 0] = one[:128]
        part[zz, 1] = one[128:]
        return carry

    lax.fori_loop(0, NZ, mixed, 0, unroll=2)

    def crossed(n, carry):
        zz = near_far(n)
        cross(zz).wait_recv()
        part[zz, 2] = (part[zz, 2].astype(F32) + br[zz].astype(F32)).astype(BF16)
        return carry

    crossed(0, 0)
    for n in range(2):
        prings[n].step(0)
    lax.fori_loop(1, NZ, crossed, 0)
    for n in range(2):
        prings[n].step(1)
    din_x.wait_recv()
    din_core(din_part).start()
    for n in range(2):
        prings[n].step(2)
    deep.stage1()

    def swap(src, dst, k):
        return pltpu.make_async_remote_copy(
            src_ref=src, dst_ref=dst, send_sem=xss.at[k], recv_sem=xrs.at[k],
            device_id={"tensor": p.xsib}, device_id_type=MESH)

    for n in range(2):
        prings[n].step(3)
    deep.stage2()
    for n in range(2):
        erings[n].arrive()
        mine = pl.ds(4 * n, 4)
        eo[mine] = emb[2 * z + 1 - xl, mine] + er[n, 3, 1 - xl] + el[n, 3, 1 - xl]
    swap(eo, ei, 0).start()
    for n in range(2):
        prings[n].arrive()

    def total(h):
        sides = [pr[n, 3, h].astype(F32) + pe[n, 3, h].astype(F32) for n in range(2)]
        return part[z, h].astype(F32) + jnp.concatenate(sides, axis=0)

    po[...] = total(1 - xl).astype(BF16)
    swap(po, pi, 1).start()
    head_part = pl.ds(p.core * 4, 4)
    head_rest = pl.ds(4 - p.core * 4, 4)
    head_x = pltpu.make_async_remote_copy(
        src_ref=heads.at[head_part], dst_ref=hx.at[head_part], send_sem=hss.at[0],
        recv_sem=hrs.at[0], device_id={"tensor": p.xsib}, device_id_type=MESH)
    head_x.start()
    deep.stage3()
    loads[6].wait()
    din_core(din_rest).wait_recv()

    def scale_cols(b, summed):
        resid = summed + hown[:, b * 256:b * 256 + 256].astype(F32)
        gains = ogain[:, pl.ds(pl.multiple_of(z * 512 + b * 256, 256), 256)]
        return jnp.sum(resid * resid, axis=-1, keepdims=True), dot((resid * gains).astype(BF16), din[b])

    square, context = scale_cols(1, total(2))
    swap(po, pi, 1).wait_recv()
    square_b, context_b = scale_cols(0, total(xl) + pi[...].astype(F32))
    square = square + square_b
    cs[:, :, :DD] = (context + context_b).astype(BF16).reshape(NZ, OWN, DD)
    high = square.astype(BF16)
    low = (square - high.astype(F32)).astype(BF16)
    first = lax.broadcasted_iota(jnp.int32, (128, 128), 1) < 64
    both = jnp.where(first, high.astype(F32), low.astype(F32)).astype(BF16)
    cs[:, :, DD:] = both.reshape(NZ, OWN, 128)

    def share(k, sender):
        to = lax.rem(z + k, NZ)
        return pltpu.make_async_remote_copy(
            src_ref=cs.at[to], dst_ref=cr.at[sender], send_sem=css.at[k], recv_sem=crs.at[k],
            device_id={"tensor": 2 * to + xl}, device_id_type=MESH)

    def give(n, carry):
        share(lax.rem(near_far(n) - z + NZ, NZ), z).start()
        return carry

    lax.fori_loop(0, NZ - 1, give, 0)
    cr[z] = cs[z]
    swap(eo, ei, 0).wait_recv()
    embeds = [emb[2 * z + xl, pl.ds(4 * n, 4)].astype(F32) + er[n, 3, xl].astype(F32) + el[n, 3, xl].astype(F32)
              + ei[pl.ds(4 * n, 4)].astype(F32) for n in range(2)]
    xin[...] = jnp.concatenate(embeds, axis=0).reshape(CODEBOOKS * OWN, DD)

    def take(k, carry):
        share(k, lax.rem(z + NZ - k, NZ)).wait_recv()
        return carry

    lax.fori_loop(1, NZ, take, 0)

    def gathered(n, carry):
        context, square = carry
        v = cr[n]
        hl = v[:, DD:].astype(F32)
        return context + v[:, :DD].astype(F32), square + hl[:, :1] + hl[:, 64:65]

    context, square = lax.fori_loop(0, NZ, gathered, (jnp.zeros((OWN, DD), F32), jnp.zeros((OWN, 1), F32)))
    context = context * lax.rsqrt(square / D + epsilon)

    rows = CODEBOOKS * OWN
    x = (context[None] + xin[...].reshape(CODEBOOKS, OWN, DD)).reshape(rows, DD)
    dn = (x * lax.rsqrt(jnp.mean(x * x, axis=-1, keepdims=True) + epsilon) * dgain[...]).astype(BF16)
    deep.stage4()

    def dproject(i, carry):
        proj[i] = dot(dn, wq[i]).astype(BF16)
        return carry

    lax.fori_loop(0, 3, dproject, 0, unroll=3)

    rq = lax.broadcasted_iota(jnp.int32, (rows, rows), 0)
    rk = lax.broadcasted_iota(jnp.int32, (rows, rows), 1)
    seen = (lax.rem(rq, OWN) == lax.rem(rk, OWN)) & (rq >= rk)
    low_half = lax.broadcasted_iota(jnp.int32, (rows, 128), 1) < DHEAD_DIM

    def dattend(j, carry):
        cols = pl.ds(pl.multiple_of(j * 128, 128), 128)
        q, k, v = proj[0, :, cols], proj[1, :, cols], proj[2, :, cols]
        parts = []
        for half in (low_half, jnp.logical_not(low_half)):
            scores = dot_t(jnp.where(half, q, jnp.zeros_like(q)), k) * DHEAD_DIM ** (-0.5)
            e = jnp.where(seen, jnp.exp(jnp.where(seen, scores, 0.0)), 0.0)
            w = (e / jnp.sum(e, axis=-1, keepdims=True)).astype(BF16)
            parts.append(dot(w, v))
        datt[:, cols] = jnp.where(low_half, parts[0], parts[1]).astype(BF16)
        return carry

    lax.fori_loop(0, DHEADS // 2, dattend, 0, unroll=4)
    loads[8].wait()
    out = x + dot(datt[...], wm[...])
    final = (out * lax.rsqrt(jnp.mean(out * out, axis=-1, keepdims=True) + epsilon) * fgain[...]).astype(BF16)
    fin[:, z] = final.reshape(CODEBOOKS, OWN, DD)

    head_x_in = pltpu.make_async_remote_copy(
        src_ref=hx.at[head_part], dst_ref=hx.at[head_part], send_sem=hss.at[1],
        recv_sem=hrs.at[0], device_id={"dp": p.cpeer}, device_id_type=MESH)
    head_c = pltpu.make_async_remote_copy(
        src_ref=hx.at[head_part], dst_ref=hx.at[head_part], send_sem=hss.at[1],
        recv_sem=hrs.at[1], device_id={"dp": p.cpeer}, device_id_type=MESH)
    head_c_in = pltpu.make_async_remote_copy(
        src_ref=hx.at[head_rest], dst_ref=hx.at[head_rest], send_sem=hss.at[1],
        recv_sem=hrs.at[1], device_id={"dp": p.cpeer}, device_id_type=MESH)
    placed = [pltpu.make_async_copy(hx.at[some], wh.at[some, :, sib_lanes], lsem.at[11 + n])
              for n, some in enumerate((head_part, head_rest))]

    def ring(n, way, s, block):
        view = fin.at[pl.ds(4 * n, 4), block]
        return pltpu.make_async_remote_copy(
            src_ref=view, dst_ref=view, send_sem=fss.at[n, 4 * way + s], recv_sem=frs.at[n, 4 * way + s],
            device_id={"tensor": p.zdown if way else p.zup}, device_id_type=MESH)

    for s in range(4):
        for n in range(2):
            for way in range(2):
                block = lax.rem(z + (s if way else NZ - s), NZ)
                if s:
                    ring(n, way, s - 1, block).wait_recv()
                if s < 3 or way == n:
                    ring(n, way, s, block).start()
        if s == 2:
            head_x_in.wait_recv()
            head_c.start()
            placed[0].start()
        if s == 3:
            head_c_in.wait_recv()
            placed[1].start()
    for n in range(2):
        ring(n, n, 3, lax.rem(z + 4, NZ)).wait_recv()

    loads[9].wait()
    placed[0].wait()
    placed[1].wait()
    shared = OWN * NZ
    lanes = lax.broadcasted_iota(jnp.int32, (shared, 256), 1).astype(F32)
    spots = lax.broadcasted_iota(jnp.int32, (shared, 128), 1)
    goals = goal[...].astype(F32) - (z * 256).astype(F32)
    books = lax.broadcasted_iota(jnp.int32, goals.shape, 1)

    def book(c, total):
        logits = dot(fin[c].reshape(shared, DD), wh[c])
        e = jnp.sum(jnp.exp(logits), axis=-1, keepdims=True)
        want = jnp.sum(jnp.where(books == c, goals, 0.0), axis=1, keepdims=True)
        hit = jnp.sum(jnp.where(lanes == want, logits, 0.0), axis=-1, keepdims=True)
        total = jnp.where(spots == c, e, total)
        return jnp.where(spots == CODEBOOKS + c, hit, total)

    sums[...] = lax.fori_loop(0, CODEBOOKS, book, jnp.zeros((shared, 128), F32), unroll=4).reshape(NZ, OWN, 128)

    def reply(k, sender):
        to = lax.rem(z + k, NZ)
        return pltpu.make_async_remote_copy(
            src_ref=sums.at[to], dst_ref=got.at[sender], send_sem=tss.at[k], recv_sem=trs.at[k],
            device_id={"tensor": 2 * to + xl}, device_id_type=MESH)

    def start_reply(k, carry):
        reply(k, z).start()
        return carry

    def take_reply(k, carry):
        reply(k, lax.rem(z + NZ - k, NZ)).wait_recv()
        return carry

    lax.fori_loop(1, NZ, start_reply, 0)
    got[z] = sums[z]
    lax.fori_loop(1, NZ, take_reply, 0)
    both = got[0]
    for n in range(1, NZ):
        both = both + got[n]
    loss[...] = jnp.log(both[:, :CODEBOOKS]) - both[:, CODEBOOKS:2 * CODEBOOKS]

    for f in range(3):
        flow(f).drain()
    mixer.drain()
    deep.drain()
    erings[0].drain()
    erings[1].drain()
    din_x.wait_send()
    din_core(din_part).wait_send()
    prings[0].drain()
    prings[1].drain()
    swap(eo, ei, 0).wait_send()
    swap(po, pi, 1).wait_send()
    head_x.wait_send()
    head_c.wait_send()

    def sent(k, carry):
        cross(k).wait_send()
        return carry

    def sent_far(k, carry):
        share(k, z).wait_send()
        reply(k, z).wait_send()
        return carry

    lax.fori_loop(0, NZ, sent, 0)
    lax.fori_loop(1, NZ, sent_far, 0)
    for n in range(2):
        for way in range(2):
            for s in range(4 if way == n else 3):
                ring(n, way, s, z).wait_send()


def shards(hidden_in, attn_gain, qkv_weight, mix_weight, out_gain, depth_in_weight, text_table, code_tables,
           depth_gain, depth_qkv, depth_mix, final_gain, heads_weight, text_ids, codes):
    half = HEAD_DIM // 2
    angles = np.arange(FRAMES)[:, None] * 10000.0 ** (-np.arange(half) / half)[None, :]
    cosv = np.concatenate([np.cos(angles)] * 2, axis=1).astype(np.float32)
    sinv = np.concatenate([-np.sin(angles), np.sin(angles)], axis=1).astype(np.float32)
    vmem = pl.BlockSpec(memory_space=pltpu.VMEM)
    anym = pl.BlockSpec(memory_space=pl.ANY)
    dma = pltpu.SemaphoreType.DMA
    b16 = lambda *shape: pltpu.VMEM(shape, BF16)
    f32 = lambda *shape: pltpu.VMEM(shape, F32)
    wide = DD + 128
    return pl.pallas_call(
        layer,
        out_shape=jax.ShapeDtypeStruct((OWN, CODEBOOKS), F32),
        in_specs=[vmem] * 8 + [anym] * 9,
        out_specs=vmem,
        scratch_shapes=[
            b16(FRAMES, D), b16(*text_table.shape), b16(128, 512), b16(2, 256, DD), b16(CODEBOOKS - 1, 128, DD),
            pltpu.VMEM((128, CODEBOOKS), jnp.int32),
            b16(4, DP, 256, 256), b16(FRAMES, D), f32(3, FRAMES, 256), b16(FRAMES, 256),
            b16(NZ, 3, 128, 256),
            b16(TP, CODEBOOKS, OWN, DD),
            b16(2, 4, 2, 4, OWN, DD), b16(2, 4, 2, 4, OWN, DD),
            b16(CODEBOOKS, OWN, DD), b16(CODEBOOKS, OWN, DD),
            b16(2, 4, 3, 64, 256), b16(2, 4, 3, 64, 256), b16(128, 256), b16(128, 256),
            b16(NZ, 128, 256), b16(NZ, 128, 256),
            b16(NZ, OWN, wide), b16(NZ, OWN, wide), f32(CODEBOOKS * OWN, DD),
            b16(3, DD, DD), b16(DD, DD), b16(CODEBOOKS, DD, 256), b16(CODEBOOKS, DD, 128),
            b16(3, CODEBOOKS * OWN, DD), b16(CODEBOOKS * OWN, DD),
            b16(CODEBOOKS, NZ, OWN, DD), f32(NZ, OWN, 128), f32(NZ, OWN, 128),
            dma((13,)),
            dma((5, 16)), dma((5, 16)),
            dma((2, 8)), dma((2, 8)),
            dma((2, 8)), dma((2, 8)),
            dma((NZ,)), dma((NZ,)),
            dma((2,)), dma((2,)),
            dma((NZ,)), dma((NZ,)),
            dma((4,)), dma((4,)),
            dma((2, 8)), dma((2, 8)),
            dma((NZ,)), dma((NZ,)),
        ],
        compiler_params=pltpu.CompilerParams(
            collective_id=0, has_side_effects=True, vmem_limit_bytes=60 * 2**20),
        name="layer",
    )(attn_gain[None], out_gain[None], text_ids.reshape(2, 128), codes, cosv, sinv, depth_gain[None],
      final_gain[None],
      hidden_in, text_table, qkv_weight, mix_weight, depth_in_weight, code_tables, depth_qkv, depth_mix, heads_weight)


def solution(mesh):
    in_specs = (
        P("dp", None),
        P(),
        P(None, "dp", "tensor"),
        P("tensor", "dp"),
        P(),
        P("tensor", None),
        P("tensor", None),
        P(None, "tensor", None),
        P(),
        P(None, "dp", None),
        P(),
        P(),
        P(None, None, "tensor"),
        P("dp"),
        P("dp", None),
    )
    out_specs = P(("dp", "tensor"), None)
    return jax.shard_map(shards, mesh=mesh, in_specs=in_specs, out_specs=out_specs, check_vma=False)
```

```python
import functools

import jax
import jax.numpy as jnp
import numpy as np
from jax import lax
from jax.experimental import pallas as pl
from jax.experimental.pallas import tpu as pltpu
from jax.sharding import PartitionSpec as P

D = 4096
HEAD_DIM = 128
FRAMES = 256
DD = 1024
DHEADS = 16
DHEAD_DIM = 64
CODEBOOKS = 8
DP = 16
TP = 16
NZ = 8
OWN = 16
F32 = jnp.float32
BF16 = jnp.bfloat16
MESH = pl.DeviceIdType.MESH

epsilon = 1e-05

X0, R1, L1, R2, L2, R3, L3, C0 = range(8)


def dot(a, b):
    return jnp.dot(a, b, preferred_element_type=F32)


def dot_t(a, b):
    return lax.dot_general(a, b, (((1,), (1,)), ((), ())), preferred_element_type=F32)


class Places:
    def __init__(self):
        d = lax.axis_index("dp")
        t = lax.axis_index("tensor")
        self.d, self.t = d, t
        self.core = lax.rem(d, 2)
        self.xh = lax.rem(d // 2, 2)
        self.xl = lax.rem(t, 2)
        self.z = t // 2
        self.up = lax.rem(d + 4, 16)
        self.down = lax.rem(d + 12, 16)
        self.far = lax.rem(d + 8, 16)
        self.xstep = 2 - 4 * self.xh
        self.xpeer = d + self.xstep
        self.cstep = 1 - 2 * self.core
        self.cpeer = d + self.cstep
        self.xsib = t + 1 - 2 * self.xl
        self.zup = lax.rem(t + 2, 16)
        self.zdown = lax.rem(t + 14, 16)
        self.blocks = [d, self.xpeer, self.down, self.up, self.down + self.xstep,
                       self.up + self.xstep, self.far, self.far + self.xstep]


class Flow:
    def __init__(self, pos, own, block, send_sem, recv_sem):
        self.pos, self.own, self.block = pos, own, block
        self.ss, self.rs = send_sem, recv_sem

    def copy(self, kind, idx, dev, own=False):
        src = self.own if own else self.block(idx)
        return pltpu.make_async_remote_copy(
            src_ref=src, dst_ref=self.block(idx), send_sem=self.ss(kind), recv_sem=self.rs(kind),
            device_id={"dp": dev}, device_id_type=MESH)

    def start0(self):
        p = self.pos
        for kind, dev in ((X0, p.xpeer), (R1, p.up), (L1, p.down), (C0, p.cpeer)):
            self.copy(kind, p.d, dev, own=True).start()

    def core_in(self, n):
        p = self.pos
        self.copy(C0 + n, p.blocks[n] + p.cstep, p.cpeer).wait_recv()

    def got(self, kind):
        p = self.pos
        self.copy(kind, p.blocks[kind + 1], p.cpeer).wait_recv()

    def forward(self, kind, idx, dev):
        self.copy(kind, idx, dev).start()

    def to_core(self, kind):
        p = self.pos
        self.forward(C0 + kind + 1, p.blocks[kind + 1], p.cpeer)

    def stage1(self):
        p = self.pos
        self.got(X0)
        self.forward(R2, p.xpeer, p.up)
        self.forward(L2, p.xpeer, p.down)
        self.to_core(X0)
        self.got(R1)
        self.forward(R3, p.down, p.up)
        self.to_core(R1)
        self.got(L1)
        self.to_core(L1)

    def stage2(self):
        p = self.pos
        self.got(R2)
        self.to_core(R2)
        self.got(L2)
        self.forward(L3, p.up + p.xstep, p.down)
        self.to_core(L2)

    def stage3(self):
        self.got(R3)
        self.to_core(R3)
        self.got(L3)
        self.to_core(L3)

    def stage4(self):
        p = self.pos
        for n in range(8):
            self.core_in(n)

    def drain(self):
        p = self.pos
        for kind in range(15):
            self.copy(kind, p.d, p.cpeer).wait_send()


class FlowDeep(Flow):
    def start0(self):
        p = self.pos
        pltpu.make_async_remote_copy(
            src_ref=self.own, dst_ref=self.block(p.d), send_sem=self.ss(X0), recv_sem=self.rs(X0),
            device_id={"dp": p.xpeer, "tensor": p.xsib}, device_id_type=MESH).start()
        for kind, dev in ((R1, p.up), (L1, p.down), (C0, p.cpeer)):
            self.copy(kind, p.d, dev, own=True).start()


class FlowY(Flow):
    def half(self, kind, idx, dev, which):
        view = self.block(idx).at[pl.ds(which * 128, 128)]
        return pltpu.make_async_remote_copy(
            src_ref=view, dst_ref=view, send_sem=self.ss(kind), recv_sem=self.rs(kind),
            device_id={"dp": dev}, device_id_type=MESH)

    def start0(self):
        p = self.pos
        for kind, dev in ((R1, p.up), (L1, p.down), (X0, p.xpeer), (C0, p.cpeer)):
            self.copy(kind, p.d, dev, own=True).start()

    def across(self, kind, idx):
        self.forward(kind, idx, self.pos.xpeer)

    def stage1(self):
        p = self.pos
        self.got(R1)
        self.half(L3, p.down, p.up, 0).start()
        self.across(R2, p.down)
        self.forward(C0 + 2, p.down, p.cpeer)
        self.got(L1)
        self.half(15, p.up, p.down, 1).start()
        self.across(L2, p.up)
        self.forward(C0 + 3, p.up, p.cpeer)
        self.got(X0)
        self.forward(C0 + 1, p.xpeer, p.cpeer)

    def stage2(self):
        p = self.pos
        self.half(L3, p.far, p.up, 0).wait_recv()
        self.half(15, p.far, p.down, 1).wait_recv()
        self.across(R3, p.far)
        self.forward(C0 + 6, p.far, p.cpeer)
        self.got(R2)
        self.forward(C0 + 4, p.blocks[4], p.cpeer)
        self.got(L2)
        self.forward(C0 + 5, p.blocks[5], p.cpeer)

    def stage3(self):
        p = self.pos
        self.got(R3)
        self.forward(C0 + 7, p.blocks[7], p.cpeer)

    def drain(self):
        p = self.pos
        for kind in range(16):
            if kind in (L3, 15):
                self.half(kind, p.d, p.up, 0).wait_send()
            else:
                self.copy(kind, p.d, p.cpeer).wait_send()


class Ring:
    def __init__(self, pos, own, slots, long, add, ss, rs):
        self.pos, self.own, self.slots, self.long, self.add = pos, own, slots, long, add
        self.ss, self.rs = ss, rs

    def first(self, way):
        return 0 if way == self.long else 1

    def dest(self, way, s):
        return lax.rem(self.pos.z + (4 - s if way == 0 else 4 + s), NZ)

    def copy(self, way, s):
        slots = self.slots[way]
        src = self.own(self.dest(way, s)) if s == self.first(way) else slots.at[s - 1]
        k = 4 * way + s
        return pltpu.make_async_remote_copy(
            src_ref=src, dst_ref=slots.at[s], send_sem=self.ss.at[k], recv_sem=self.rs.at[k],
            device_id={"tensor": self.pos.zdown if way else self.pos.zup}, device_id_type=MESH)

    def step(self, s):
        for way in range(2):
            if s < self.first(way):
                continue
            if s > self.first(way):
                self.copy(way, s - 1).wait_recv()
                self.add(self.slots[way].at[s - 1], self.own(self.dest(way, s)))
            self.copy(way, s).start()

    def arrive(self):
        for way in range(2):
            self.copy(way, 3).wait_recv()

    def drain(self):
        for way in range(2):
            for s in range(self.first(way), 4):
                self.copy(way, s).wait_send()


def layer(gain, ogain, tid, code, cosr, sinr, dgain, fgain,
          hid_h, text_h, qkv_h, mix_h, din_h, tabs_h, dqkv, dmix_h, heads,
          loss,
          hid, text, hown, din, tabs, goal, wall, normed, acc, att, part, emb, er, el, eo, ei, pr, pe, po, pi, bs, br,
          cs, cr, xin, wq, wm, wh, hx, proj, datt, fin, sums, got,
          lsem, wss, wrs, ess, ers, pss, prs, bss, brs, xss, xrs, css, crs, hss, hrs, fss, frs, tss, trs):
    p = Places()
    d, t, z, xl = p.d, p.t, p.z, p.xl

    def block_of(f):
        return lambda i: wall.at[f, i]

    deep_block = lambda i: wq.at[:, pl.ds(pl.multiple_of(i * 64, 64), 64), :]
    own_lanes = pl.ds(pl.multiple_of(xl * 128, 128), 128)
    sib_lanes = pl.ds(pl.multiple_of((1 - xl) * 128, 128), 128)
    loads = [(qkv_h.at[0], wall.at[0, d]), (qkv_h.at[1], wall.at[1, d]), (qkv_h.at[2], wall.at[2, d]),
             (mix_h, wall.at[3, d]), (tabs_h, tabs), (hid_h, hid), (din_h, din.at[xl]), (dqkv, deep_block(d)),
             (dmix_h, wm), (heads, wh.at[:, :, own_lanes]), (text_h, text)]
    loads = [pltpu.make_async_copy(src, dst, lsem.at[n]) for n, (src, dst) in enumerate(loads)]
    for one in loads:
        one.start()

    def add_books(a, b):
        def one(n, carry):
            h, c = n // 4, lax.rem(n, 4)
            a[h, c] = a[h, c] + b[h, c]
            return carry

        lax.fori_loop(0, 8, one, 0)

    def add_rows(a, b):
        def one(n, carry):
            a[n] = (a[n].astype(F32) + b[n].astype(F32)).astype(BF16)
            return carry

        lax.fori_loop(0, 3, one, 0)

    def ering_of(n):
        books = pl.ds(4 * n, 4)
        return Ring(p, lambda i: emb.at[pl.ds(2 * i, 2), books], (er.at[n], el.at[n]), n, add_books, ess.at[n], ers.at[n])

    erings = [ering_of(n) for n in range(2)]

    def pring_of(n):
        rows = pl.ds(64 * n, 64)
        return Ring(p, lambda i: part.at[i, :, rows], (pr.at[n], pe.at[n]), n, add_rows, pss.at[n], prs.at[n])

    prings = [pring_of(n) for n in range(2)]

    barrier = pltpu.get_barrier_semaphore()
    for dev in (p.xpeer, p.up, p.down, p.cpeer):
        pl.semaphore_signal(barrier, inc=1, device_id={"dp": dev}, device_id_type=MESH)

    def greet(k, carry):
        pl.semaphore_signal(barrier, inc=1, device_id={"tensor": lax.rem(t + 2 * k, TP)}, device_id_type=MESH)
        return carry

    lax.fori_loop(1, NZ, greet, 0)
    pl.semaphore_signal(barrier, inc=1, device_id={"tensor": p.xsib}, device_id_type=MESH)
    pl.semaphore_signal(barrier, inc=1, device_id={"dp": p.xpeer, "tensor": p.xsib}, device_id_type=MESH)
    pl.semaphore_wait(barrier, 5 + NZ)

    def flow(f):
        kind = FlowY if f == 2 else Flow
        return kind(p, wall.at[f, d], block_of(f), lambda k: wss.at[f, k], lambda k: wrs.at[f, k])

    mixer = flow(3)
    deep = FlowDeep(p, dqkv, deep_block, lambda k: wss.at[4, k], lambda k: wrs.at[4, k])
    for n in range(3):
        loads[n].wait()
    for f in range(3):
        flow(f).start0()

    codev = code[...].astype(F32)
    pick = lax.broadcasted_iota(jnp.int32, codev.shape, 1)
    count = text.shape[0]
    whole = count // 128 * 128
    square_r = lax.broadcasted_iota(jnp.int32, (128, 128), 0)
    square_c = lax.broadcasted_iota(jnp.int32, (128, 128), 1)
    halves = [jnp.sum(jnp.where(square_r == square_c, jnp.broadcast_to(tid[h:h + 1].astype(F32), (128, 128)), 0.0),
                      axis=1, keepdims=True) for h in range(2)]
    text_want = jnp.concatenate(halves, axis=0) - (t * count).astype(F32)

    def named(want, start, width):
        lanes = lax.broadcasted_iota(jnp.int32, (FRAMES, width), 1).astype(F32) + start
        return (lanes == want).astype(BF16)

    loads[10].wait()
    found = dot(named(text_want, 0, whole), text[:whole])
    if count > whole:
        found = found + dot(named(text_want, whole, count - whole), text[whole:])
    emb[:, 0] = found.astype(BF16).reshape(TP, OWN, DD)
    loads[4].wait()

    def lookup(c, carry):
        want = jnp.sum(jnp.where(pick == c - 1, codev, 0.0), axis=1, keepdims=True) - (t * 128).astype(F32)
        emb[:, c] = dot(named(want, 0, 128), tabs[c - 1]).astype(BF16).reshape(TP, OWN, DD)
        return carry

    lax.fori_loop(1, 4, lookup, 0)
    erings[0].step(0)
    lax.fori_loop(4, CODEBOOKS, lookup, 0)
    erings[1].step(0)
    loads[5].wait()

    def norm_rows(n, carry):
        r = pl.ds(pl.multiple_of(n * 32, 32), 32)
        h = hid[r, :].astype(F32)
        scale = lax.rsqrt(jnp.mean(h * h, axis=-1, keepdims=True) + epsilon)
        normed[r, :] = (h * scale * gain[...]).astype(BF16)
        return carry

    lax.fori_loop(0, FRAMES // 32, norm_rows, 0)

    def side_rows(n, carry):
        frames = pl.ds(pl.multiple_of(n * 32 + xl * 16, 16), OWN)
        to = pl.ds(pl.multiple_of(n * 16, 16), OWN)
        hown[to, :] = hid[frames, pl.ds(pl.multiple_of(z * 512, 512), 512)]
        goal[to, :] = code[frames, :]
        return carry

    lax.fori_loop(0, NZ, side_rows, 0)
    def project(ns, first=False):
        for n in ns:
            for f in range(3):
                flow(f).core_in(n)
        y = p.blocks[ns[0]] // 4
        cols = normed[:, pl.ds(pl.multiple_of(y * 1024, 1024), 1024)]

        def one(i, carry):
            got_one = dot(cols, wall[i, pl.ds(4 * y, 4)].reshape(1024, 256))
            acc[i] = got_one if first else acc[i] + got_one
            return carry

        lax.fori_loop(0, 3, one, 0, unroll=3)

    flow(0).stage1()
    erings[0].step(1)
    flow(1).stage1()
    erings[1].step(1)
    flow(2).stage1()
    loads[3].wait()
    mixer.start0()
    project((0, 1), True)
    flow(0).stage2()
    erings[0].step(2)
    flow(1).stage2()
    flow(2).stage2()
    mixer.stage1()
    erings[1].step(2)
    project((2, 4))
    for f in range(3):
        flow(f).stage3()
    mixer.stage2()
    loads[7].wait()
    deep.start0()
    din_part = pl.ds(pl.multiple_of(128 * p.core, 128), 128)
    din_rest = pl.ds(pl.multiple_of(128 - 128 * p.core, 128), 128)
    din_x = pltpu.make_async_remote_copy(
        src_ref=din_h.at[din_part], dst_ref=din.at[xl, din_part], send_sem=hss.at[2], recv_sem=hrs.at[2],
        device_id={"tensor": p.xsib}, device_id_type=MESH)
    din_x.start()

    def din_core(some):
        view = din.at[1 - xl, some]
        return pltpu.make_async_remote_copy(
            src_ref=view, dst_ref=view, send_sem=hss.at[3], recv_sem=hrs.at[3],
            device_id={"dp": p.cpeer}, device_id_type=MESH)

    project((3, 5))
    erings[0].step(3)
    project((6, 7))

    order_q = lax.broadcasted_iota(jnp.int32, (FRAMES, FRAMES), 0)
    order_k = lax.broadcasted_iota(jnp.int32, (FRAMES, FRAMES), 1)
    causal = order_q >= order_k

    def rotate(v):
        half = HEAD_DIM // 2
        swapped = jnp.concatenate([v[:, half:], v[:, :half]], axis=1)
        return (v * cosr[...] + swapped * sinr[...]).astype(BF16)

    def attend(h, carry):
        cols = pl.ds(pl.multiple_of(h * HEAD_DIM, HEAD_DIM), HEAD_DIM)
        q = rotate(acc[0, :, cols])
        k = rotate(acc[1, :, cols])
        v = acc[2, :, cols].astype(BF16)
        scores = dot_t(q, k) * HEAD_DIM ** (-0.5)
        e = jnp.where(causal, jnp.exp(jnp.where(causal, scores, 0.0)), 0.0)
        w = (e / jnp.sum(e, axis=-1, keepdims=True)).astype(BF16)
        mixed_rows = dot(w, v).astype(BF16).reshape(NZ, 2, OWN, HEAD_DIM)
        for side in range(2):
            att[side * 128:side * 128 + 128, cols] = mixed_rows[:, side].reshape(128, HEAD_DIM)
        return carry

    lax.fori_loop(0, 2, attend, 0, unroll=2)
    erings[1].step(3)
    mixer.stage3()
    mixer.stage4()

    def cross(zz):
        return pltpu.make_async_remote_copy(
            src_ref=bs.at[zz], dst_ref=br.at[zz], send_sem=bss.at[zz], recv_sem=brs.at[zz],
            device_id={"tensor": p.xsib}, device_id_type=MESH)

    def near_far(n):
        step = (n + 1) // 2
        return lax.rem(z + 4 + jnp.where(lax.rem(n, 2) == 1, -step, step), NZ)

    def mixed(n, carry):
        zz = near_far(n)
        second = wall[3, 2 * zz + 1]
        bs[zz] = dot(att[pl.ds(pl.multiple_of(128 - 128 * xl, 128), 128), :], second).astype(BF16)
        cross(zz).start()
        part[zz, 2] = dot(att[pl.ds(pl.multiple_of(128 * xl, 128), 128), :], second).astype(BF16)
        one = dot(att[...], wall[3, 2 * zz]).astype(BF16)
        part[zz, 0] = one[:128]
        part[zz, 1] = one[128:]
        return carry

    lax.fori_loop(0, NZ, mixed, 0, unroll=2)

    def crossed(n, carry):
        zz = near_far(n)
        cross(zz).wait_recv()
        part[zz, 2] = (part[zz, 2].astype(F32) + br[zz].astype(F32)).astype(BF16)
        return carry

    crossed(0, 0)
    for n in range(2):
        prings[n].step(0)
    lax.fori_loop(1, 3, crossed, 0)
    for n in range(2):
        prings[n].step(1)
    din_x.wait_recv()
    din_core(din_part).start()
    lax.fori_loop(3, 5, crossed, 0)
    for n in range(2):
        prings[n].step(2)

    def swap(src, dst, k):
        return pltpu.make_async_remote_copy(
            src_ref=src, dst_ref=dst, send_sem=xss.at[k], recv_sem=xrs.at[k],
            device_id={"tensor": p.xsib}, device_id_type=MESH)

    lax.fori_loop(5, 7, crossed, 0)
    for n in range(2):
        prings[n].step(3)
    deep.stage1()
    for n in range(2):
        erings[n].arrive()
        mine = pl.ds(4 * n, 4)
        eo[mine] = emb[2 * z + 1 - xl, mine] + er[n, 3, 1 - xl] + el[n, 3, 1 - xl]
    swap(eo, ei, 0).start()
    for n in range(2):
        prings[n].arrive()

    crossed(7, 0)

    def total(h):
        sides = [pr[n, 3, h].astype(F32) + pe[n, 3, h].astype(F32) for n in range(2)]
        return part[z, h].astype(F32) + jnp.concatenate(sides, axis=0)

    po[...] = total(1 - xl).astype(BF16)
    swap(po, pi, 1).start()
    head_part = pl.ds(p.core * 4, 4)
    head_rest = pl.ds(4 - p.core * 4, 4)
    head_x = pltpu.make_async_remote_copy(
        src_ref=heads.at[head_part], dst_ref=hx.at[head_part], send_sem=hss.at[0],
        recv_sem=hrs.at[0], device_id={"tensor": p.xsib}, device_id_type=MESH)
    head_x.start()
    deep.stage2()
    loads[6].wait()
    din_core(din_rest).wait_recv()

    def scale_cols(b, summed):
        resid = summed + hown[:, b * 256:b * 256 + 256].astype(F32)
        gains = ogain[:, pl.ds(pl.multiple_of(z * 512 + b * 256, 256), 256)]
        return jnp.sum(resid * resid, axis=-1, keepdims=True), dot((resid * gains).astype(BF16), din[b])

    square, context = scale_cols(1, total(2))
    swap(po, pi, 1).wait_recv()
    square_b, context_b = scale_cols(0, total(xl) + pi[...].astype(F32))
    square = square + square_b
    cs[:, :, :DD] = (context + context_b).astype(BF16).reshape(NZ, OWN, DD)
    high = square.astype(BF16)
    low = (square - high.astype(F32)).astype(BF16)
    first = lax.broadcasted_iota(jnp.int32, (128, 128), 1) < 64
    both = jnp.where(first, high.astype(F32), low.astype(F32)).astype(BF16)
    cs[:, :, DD:] = both.reshape(NZ, OWN, 128)

    def share(k, sender):
        to = lax.rem(z + k, NZ)
        return pltpu.make_async_remote_copy(
            src_ref=cs.at[to], dst_ref=cr.at[sender], send_sem=css.at[k], recv_sem=crs.at[k],
            device_id={"tensor": 2 * to + xl}, device_id_type=MESH)

    def give(n, carry):
        share(lax.rem(near_far(n) - z + NZ, NZ), z).start()
        return carry

    lax.fori_loop(0, NZ - 1, give, 0)
    deep.stage3()
    cr[z] = cs[z]
    swap(eo, ei, 0).wait_recv()
    embeds = [emb[2 * z + xl, pl.ds(4 * n, 4)].astype(F32) + er[n, 3, xl].astype(F32) + el[n, 3, xl].astype(F32)
              + ei[pl.ds(4 * n, 4)].astype(F32) for n in range(2)]
    xin[...] = jnp.concatenate(embeds, axis=0).reshape(CODEBOOKS * OWN, DD)

    def take(k, carry):
        share(k, lax.rem(z + NZ - k, NZ)).wait_recv()
        return carry

    lax.fori_loop(1, NZ, take, 0)

    def gathered(n, carry):
        context, square = carry
        v = cr[n]
        hl = v[:, DD:].astype(F32)
        return context + v[:, :DD].astype(F32), square + hl[:, :1] + hl[:, 64:65]

    context, square = lax.fori_loop(0, NZ, gathered, (jnp.zeros((OWN, DD), F32), jnp.zeros((OWN, 1), F32)))
    context = context * lax.rsqrt(square / D + epsilon)

    def ring(n, way, s, block):
        view = fin.at[pl.ds(2 * n, 2), block]
        return pltpu.make_async_remote_copy(
            src_ref=view, dst_ref=view, send_sem=fss.at[n, 4 * way + s], recv_sem=frs.at[n, 4 * way + s],
            device_id={"tensor": p.zdown if way else p.zup}, device_id_type=MESH)

    rows = CODEBOOKS * OWN
    x = (context[None] + xin[...].reshape(CODEBOOKS, OWN, DD)).reshape(rows, DD)
    dn = (x * lax.rsqrt(jnp.mean(x * x, axis=-1, keepdims=True) + epsilon) * dgain[...]).astype(BF16)
    deep.stage4()

    def dproject(i, carry):
        proj[i] = dot(dn, wq[i]).astype(BF16)
        return carry

    lax.fori_loop(0, 3, dproject, 0, unroll=3)

    rq = lax.broadcasted_iota(jnp.int32, (rows, rows), 0)
    rk = lax.broadcasted_iota(jnp.int32, (rows, rows), 1)
    seen = (lax.rem(rq, OWN) == lax.rem(rk, OWN)) & (rq >= rk)
    low_half = lax.broadcasted_iota(jnp.int32, (rows, 128), 1) < DHEAD_DIM

    def dattend(j, carry):
        cols = pl.ds(pl.multiple_of(j * 128, 128), 128)
        q, k, v = proj[0, :, cols], proj[1, :, cols], proj[2, :, cols]
        parts = []
        for half in (low_half, jnp.logical_not(low_half)):
            scores = dot_t(jnp.where(half, q, jnp.zeros_like(q)), k) * DHEAD_DIM ** (-0.5)
            e = jnp.where(seen, jnp.exp(jnp.where(seen, scores, 0.0)), 0.0)
            w = (e / jnp.sum(e, axis=-1, keepdims=True)).astype(BF16)
            parts.append(dot(w, v))
        datt[:, cols] = jnp.where(low_half, parts[0], parts[1]).astype(BF16)
        return carry

    lax.fori_loop(0, DHEADS // 2, dattend, 0, unroll=4)
    loads[8].wait()
    out = x + dot(datt[...], wm[...])
    final = (out * lax.rsqrt(jnp.mean(out * out, axis=-1, keepdims=True) + epsilon) * fgain[...]).astype(BF16)
    fin[:, z] = final.reshape(CODEBOOKS, OWN, DD)

    for n in range(4):
        for way in range(2):
            ring(n, way, 0, z).start()

    head_x_in = pltpu.make_async_remote_copy(
        src_ref=hx.at[head_part], dst_ref=hx.at[head_part], send_sem=hss.at[1],
        recv_sem=hrs.at[0], device_id={"dp": p.cpeer}, device_id_type=MESH)
    head_c = pltpu.make_async_remote_copy(
        src_ref=hx.at[head_part], dst_ref=hx.at[head_part], send_sem=hss.at[1],
        recv_sem=hrs.at[1], device_id={"dp": p.cpeer}, device_id_type=MESH)
    head_c_in = pltpu.make_async_remote_copy(
        src_ref=hx.at[head_rest], dst_ref=hx.at[head_rest], send_sem=hss.at[1],
        recv_sem=hrs.at[1], device_id={"dp": p.cpeer}, device_id_type=MESH)
    placed = [pltpu.make_async_copy(hx.at[some], wh.at[some, :, sib_lanes], lsem.at[11 + n])
              for n, some in enumerate((head_part, head_rest))]

    for s in range(1, 4):
        for n in range(4):
            for way in range(2):
                block = lax.rem(z + (s if way else NZ - s), NZ)
                ring(n, way, s - 1, block).wait_recv()
                if s < 3 or way == n % 2:
                    ring(n, way, s, block).start()
        if s == 1:
            for one in (flow(0), flow(1), flow(2), mixer, deep, erings[0], erings[1], prings[0], prings[1]):
                one.drain()
            din_x.wait_send()
            din_core(din_part).wait_send()
            swap(eo, ei, 0).wait_send()
            swap(po, pi, 1).wait_send()

            def sent(k, carry):
                cross(k).wait_send()
                return carry

            def sent_far(k, carry):
                share(k, z).wait_send()
                return carry

            lax.fori_loop(0, NZ, sent, 0)
            lax.fori_loop(1, NZ, sent_far, 0)
        if s == 2:
            head_x_in.wait_recv()
            head_c.start()
            placed[0].start()
        if s == 3:
            head_c_in.wait_recv()
            placed[1].start()

    loads[9].wait()
    placed[0].wait()
    placed[1].wait()
    shared = OWN * NZ
    lanes = lax.broadcasted_iota(jnp.int32, (shared, 256), 1).astype(F32)
    spots = lax.broadcasted_iota(jnp.int32, (shared, 128), 1)
    goals = goal[...].astype(F32) - (z * 256).astype(F32)
    books = lax.broadcasted_iota(jnp.int32, goals.shape, 1)

    def book(c, total):
        logits = dot(fin[c].reshape(shared, DD), wh[c])
        e = jnp.sum(jnp.exp(logits), axis=-1, keepdims=True)
        want = jnp.sum(jnp.where(books == c, goals, 0.0), axis=1, keepdims=True)
        hit = jnp.sum(jnp.where(lanes == want, logits, 0.0), axis=-1, keepdims=True)
        total = jnp.where(spots == c, e, total)
        return jnp.where(spots == CODEBOOKS + c, hit, total)

    total_sums = jnp.zeros((shared, 128), F32)
    for h in range(2):
        for n in range(2 * h, 2 * h + 2):
            ring(n, n % 2, 3, lax.rem(z + 4, NZ)).wait_recv()
        total_sums = lax.fori_loop(4 * h, 4 * h + 4, book, total_sums, unroll=4)
    sums[...] = total_sums.reshape(NZ, OWN, 128)

    def reply(k, sender):
        to = lax.rem(z + k, NZ)
        return pltpu.make_async_remote_copy(
            src_ref=sums.at[to], dst_ref=got.at[sender], send_sem=tss.at[k], recv_sem=trs.at[k],
            device_id={"tensor": 2 * to + xl}, device_id_type=MESH)

    def start_reply(k, carry):
        reply(k, z).start()
        return carry

    def take_reply(k, carry):
        reply(k, lax.rem(z + NZ - k, NZ)).wait_recv()
        return carry

    lax.fori_loop(1, NZ, start_reply, 0)
    got[z] = sums[z]
    lax.fori_loop(1, NZ, take_reply, 0)
    both = got[0]
    for n in range(1, NZ):
        both = both + got[n]
    loss[...] = jnp.log(both[:, :CODEBOOKS]) - both[:, CODEBOOKS:2 * CODEBOOKS]

    head_x.wait_send()
    head_c.wait_send()

    def reply_sent(k, carry):
        reply(k, z).wait_send()
        return carry

    lax.fori_loop(1, NZ, reply_sent, 0)
    for n in range(4):
        for way in range(2):
            for s in range(4 if way == n % 2 else 3):
                ring(n, way, s, z).wait_send()


def shards(hidden_in, attn_gain, qkv_weight, mix_weight, out_gain, depth_in_weight, text_table, code_tables,
           depth_gain, depth_qkv, depth_mix, final_gain, heads_weight, text_ids, codes):
    half = HEAD_DIM // 2
    angles = np.arange(FRAMES)[:, None] * 10000.0 ** (-np.arange(half) / half)[None, :]
    cosv = np.concatenate([np.cos(angles)] * 2, axis=1).astype(np.float32)
    sinv = np.concatenate([-np.sin(angles), np.sin(angles)], axis=1).astype(np.float32)
    vmem = pl.BlockSpec(memory_space=pltpu.VMEM)
    anym = pl.BlockSpec(memory_space=pl.ANY)
    dma = pltpu.SemaphoreType.DMA
    b16 = lambda *shape: pltpu.VMEM(shape, BF16)
    f32 = lambda *shape: pltpu.VMEM(shape, F32)
    wide = DD + 128
    return pl.pallas_call(
        layer,
        out_shape=jax.ShapeDtypeStruct((OWN, CODEBOOKS), F32),
        in_specs=[vmem] * 8 + [anym] * 9,
        out_specs=vmem,
        scratch_shapes=[
            b16(FRAMES, D), b16(*text_table.shape), b16(128, 512), b16(2, 256, DD), b16(CODEBOOKS - 1, 128, DD),
            pltpu.VMEM((128, CODEBOOKS), jnp.int32),
            b16(4, DP, 256, 256), b16(FRAMES, D), f32(3, FRAMES, 256), b16(FRAMES, 256),
            b16(NZ, 3, 128, 256),
            b16(TP, CODEBOOKS, OWN, DD),
            b16(2, 4, 2, 4, OWN, DD), b16(2, 4, 2, 4, OWN, DD),
            b16(CODEBOOKS, OWN, DD), b16(CODEBOOKS, OWN, DD),
            b16(2, 4, 3, 64, 256), b16(2, 4, 3, 64, 256), b16(128, 256), b16(128, 256),
            b16(NZ, 128, 256), b16(NZ, 128, 256),
            b16(NZ, OWN, wide), b16(NZ, OWN, wide), f32(CODEBOOKS * OWN, DD),
            b16(3, DD, DD), b16(DD, DD), b16(CODEBOOKS, DD, 256), b16(CODEBOOKS, DD, 128),
            b16(3, CODEBOOKS * OWN, DD), b16(CODEBOOKS * OWN, DD),
            b16(CODEBOOKS, NZ, OWN, DD), f32(NZ, OWN, 128), f32(NZ, OWN, 128),
            dma((13,)),
            dma((5, 16)), dma((5, 16)),
            dma((2, 8)), dma((2, 8)),
            dma((2, 8)), dma((2, 8)),
            dma((NZ,)), dma((NZ,)),
            dma((2,)), dma((2,)),
            dma((NZ,)), dma((NZ,)),
            dma((4,)), dma((4,)),
            dma((4, 8)), dma((4, 8)),
            dma((NZ,)), dma((NZ,)),
        ],
        compiler_params=pltpu.CompilerParams(
            collective_id=0, has_side_effects=True, vmem_limit_bytes=60 * 2**20),
        name="layer",
    )(attn_gain[None], out_gain[None], text_ids.reshape(2, 128), codes, cosv, sinv, depth_gain[None],
      final_gain[None],
      hidden_in, text_table, qkv_weight, mix_weight, depth_in_weight, code_tables, depth_qkv, depth_mix, heads_weight)


def solution(mesh):
    in_specs = (
        P("dp", None),
        P(),
        P(None, "dp", "tensor"),
        P("tensor", "dp"),
        P(),
        P("tensor", None),
        P("tensor", None),
        P(None, "tensor", None),
        P(),
        P(None, "dp", None),
        P(),
        P(),
        P(None, None, "tensor"),
        P("dp"),
        P("dp", None),
    )
    out_specs = P(("dp", "tensor"), None)
    return jax.shard_map(shards, mesh=mesh, in_specs=in_specs, out_specs=out_specs, check_vma=False)
```

```python
import functools

import jax
import jax.numpy as jnp
import numpy as np
from jax import lax
from jax.experimental import pallas as pl
from jax.experimental.pallas import tpu as pltpu
from jax.sharding import PartitionSpec as P

D = 4096
HEAD_DIM = 128
FRAMES = 256
DD = 1024
DHEADS = 16
DHEAD_DIM = 64
CODEBOOKS = 8
DP = 16
TP = 16
NZ = 8
OWN = 16
F32 = jnp.float32
BF16 = jnp.bfloat16
MESH = pl.DeviceIdType.MESH

epsilon = 1e-05

X0, R1, L1, R2, L2, R3, L3, C0 = range(8)


def dot(a, b):
    return jnp.dot(a, b, preferred_element_type=F32)


def dot_t(a, b):
    return lax.dot_general(a, b, (((1,), (1,)), ((), ())), preferred_element_type=F32)


class Places:
    def __init__(self):
        d = lax.axis_index("dp")
        t = lax.axis_index("tensor")
        self.d, self.t = d, t
        self.core = lax.rem(d, 2)
        self.xh = lax.rem(d // 2, 2)
        self.xl = lax.rem(t, 2)
        self.z = t // 2
        self.up = lax.rem(d + 4, 16)
        self.down = lax.rem(d + 12, 16)
        self.far = lax.rem(d + 8, 16)
        self.xstep = 2 - 4 * self.xh
        self.xpeer = d + self.xstep
        self.cstep = 1 - 2 * self.core
        self.cpeer = d + self.cstep
        self.xsib = t + 1 - 2 * self.xl
        self.zup = lax.rem(t + 2, 16)
        self.zdown = lax.rem(t + 14, 16)
        self.blocks = [d, self.xpeer, self.down, self.up, self.down + self.xstep,
                       self.up + self.xstep, self.far, self.far + self.xstep]


class Flow:
    def __init__(self, pos, own, block, send_sem, recv_sem):
        self.pos, self.own, self.block = pos, own, block
        self.ss, self.rs = send_sem, recv_sem

    def copy(self, kind, idx, dev, own=False):
        src = self.own if own else self.block(idx)
        return pltpu.make_async_remote_copy(
            src_ref=src, dst_ref=self.block(idx), send_sem=self.ss(kind), recv_sem=self.rs(kind),
            device_id={"dp": dev}, device_id_type=MESH)

    def start0(self):
        p = self.pos
        for kind, dev in ((X0, p.xpeer), (R1, p.up), (L1, p.down), (C0, p.cpeer)):
            self.copy(kind, p.d, dev, own=True).start()

    def core_in(self, n):
        p = self.pos
        self.copy(C0 + n, p.blocks[n] + p.cstep, p.cpeer).wait_recv()

    def got(self, kind):
        p = self.pos
        self.copy(kind, p.blocks[kind + 1], p.cpeer).wait_recv()

    def forward(self, kind, idx, dev):
        self.copy(kind, idx, dev).start()

    def to_core(self, kind):
        p = self.pos
        self.forward(C0 + kind + 1, p.blocks[kind + 1], p.cpeer)

    def stage1(self):
        p = self.pos
        self.got(X0)
        self.forward(R2, p.xpeer, p.up)
        self.forward(L2, p.xpeer, p.down)
        self.to_core(X0)
        self.got(R1)
        self.forward(R3, p.down, p.up)
        self.to_core(R1)
        self.got(L1)
        self.to_core(L1)

    def stage2(self):
        p = self.pos
        self.got(R2)
        self.to_core(R2)
        self.got(L2)
        self.forward(L3, p.up + p.xstep, p.down)
        self.to_core(L2)

    def stage3(self):
        self.got(R3)
        self.to_core(R3)
        self.got(L3)
        self.to_core(L3)

    def stage4(self):
        p = self.pos
        for n in range(8):
            self.core_in(n)

    def drain(self):
        p = self.pos
        for kind in range(15):
            self.copy(kind, p.d, p.cpeer).wait_send()


class FlowDeep(Flow):
    def start_x(self):
        p = self.pos
        pltpu.make_async_remote_copy(
            src_ref=self.own, dst_ref=self.block(p.d), send_sem=self.ss(X0), recv_sem=self.rs(X0),
            device_id={"dp": p.xpeer, "tensor": p.xsib}, device_id_type=MESH).start()
        self.copy(C0, p.d, p.cpeer, own=True).start()

    def start_y(self):
        p = self.pos
        self.copy(R1, p.d, p.up, own=True).start()
        self.copy(L1, p.d, p.down, own=True).start()

    def pass_x(self):
        p = self.pos
        self.got(X0)
        self.forward(R2, p.xpeer, p.up)
        self.forward(L2, p.xpeer, p.down)
        self.to_core(X0)

    def stage1(self):
        p = self.pos
        self.got(R1)
        self.forward(R3, p.down, p.up)
        self.to_core(R1)
        self.got(L1)
        self.to_core(L1)


class FlowY(Flow):
    def half(self, kind, idx, dev, which):
        view = self.block(idx).at[pl.ds(which * 128, 128)]
        return pltpu.make_async_remote_copy(
            src_ref=view, dst_ref=view, send_sem=self.ss(kind), recv_sem=self.rs(kind),
            device_id={"dp": dev}, device_id_type=MESH)

    def start0(self):
        p = self.pos
        for kind, dev in ((R1, p.up), (L1, p.down), (X0, p.xpeer), (C0, p.cpeer)):
            self.copy(kind, p.d, dev, own=True).start()

    def across(self, kind, idx):
        self.forward(kind, idx, self.pos.xpeer)

    def stage1(self):
        p = self.pos
        self.got(R1)
        self.half(L3, p.down, p.up, 0).start()
        self.across(R2, p.down)
        self.forward(C0 + 2, p.down, p.cpeer)
        self.got(L1)
        self.half(15, p.up, p.down, 1).start()
        self.across(L2, p.up)
        self.forward(C0 + 3, p.up, p.cpeer)
        self.got(X0)
        self.forward(C0 + 1, p.xpeer, p.cpeer)

    def stage2(self):
        p = self.pos
        self.half(L3, p.far, p.up, 0).wait_recv()
        self.half(15, p.far, p.down, 1).wait_recv()
        self.across(R3, p.far)
        self.forward(C0 + 6, p.far, p.cpeer)
        self.got(R2)
        self.forward(C0 + 4, p.blocks[4], p.cpeer)
        self.got(L2)
        self.forward(C0 + 5, p.blocks[5], p.cpeer)

    def stage3(self):
        p = self.pos
        self.got(R3)
        self.forward(C0 + 7, p.blocks[7], p.cpeer)

    def drain(self):
        p = self.pos
        for kind in range(16):
            if kind in (L3, 15):
                self.half(kind, p.d, p.up, 0).wait_send()
            else:
                self.copy(kind, p.d, p.cpeer).wait_send()


class Ring:
    def __init__(self, pos, own, slots, long, add, ss, rs):
        self.pos, self.own, self.slots, self.long, self.add = pos, own, slots, long, add
        self.ss, self.rs = ss, rs

    def first(self, way):
        return 0 if way == self.long else 1

    def dest(self, way, s):
        return lax.rem(self.pos.z + (4 - s if way == 0 else 4 + s), NZ)

    def copy(self, way, s):
        slots = self.slots[way]
        src = self.own(self.dest(way, s)) if s == self.first(way) else slots.at[s - 1]
        k = 4 * way + s
        return pltpu.make_async_remote_copy(
            src_ref=src, dst_ref=slots.at[s], send_sem=self.ss.at[k], recv_sem=self.rs.at[k],
            device_id={"tensor": self.pos.zdown if way else self.pos.zup}, device_id_type=MESH)

    def step(self, s):
        for way in range(2):
            if s < self.first(way):
                continue
            if s > self.first(way):
                self.copy(way, s - 1).wait_recv()
                self.add(self.slots[way].at[s - 1], self.own(self.dest(way, s)))
            self.copy(way, s).start()

    def arrive(self):
        for way in range(2):
            self.copy(way, 3).wait_recv()

    def drain(self):
        for way in range(2):
            for s in range(self.first(way), 4):
                self.copy(way, s).wait_send()


def layer(gain, ogain, tid, code, cosr, sinr, dgain, fgain,
          hid_h, text_h, qkv_h, mix_h, din_h, tabs_h, dqkv, dmix_h, heads,
          loss,
          hid, text, hown, din, tabs, goal, wall, normed, acc, att, part, emb, er, el, eo, ei, pr, pe, po, pi, bs, br,
          cs, cr, xin, wq, wm, wh, hx, proj, datt, fin, sums, got,
          lsem, wss, wrs, ess, ers, pss, prs, bss, brs, xss, xrs, css, crs, hss, hrs, fss, frs, tss, trs):
    p = Places()
    d, t, z, xl = p.d, p.t, p.z, p.xl

    def block_of(f):
        return lambda i: wall.at[f, i]

    deep_block = lambda i: wq.at[:, pl.ds(pl.multiple_of(i * 64, 64), 64), :]
    own_lanes = pl.ds(pl.multiple_of(xl * 128, 128), 128)
    sib_lanes = pl.ds(pl.multiple_of((1 - xl) * 128, 128), 128)
    loads = [(qkv_h.at[0], wall.at[0, d]), (qkv_h.at[1], wall.at[1, d]), (qkv_h.at[2], wall.at[2, d]),
             (mix_h, wall.at[3, d]), (tabs_h, tabs), (hid_h, hid), (din_h, din.at[xl]), (dqkv, deep_block(d)),
             (dmix_h, wm), (heads, wh.at[:, :, own_lanes]), (text_h, text)]
    loads = [pltpu.make_async_copy(src, dst, lsem.at[n]) for n, (src, dst) in enumerate(loads)]
    for one in loads:
        one.start()

    def add_books(a, b):
        def one(n, carry):
            h, c = n // 4, lax.rem(n, 4)
            a[h, c] = a[h, c] + b[h, c]
            return carry

        lax.fori_loop(0, 8, one, 0)

    def add_rows(a, b):
        def one(n, carry):
            a[n] = (a[n].astype(F32) + b[n].astype(F32)).astype(BF16)
            return carry

        lax.fori_loop(0, 3, one, 0)

    def ering_of(n):
        books = pl.ds(4 * n, 4)
        return Ring(p, lambda i: emb.at[pl.ds(2 * i, 2), books], (er.at[n], el.at[n]), n, add_books, ess.at[n], ers.at[n])

    erings = [ering_of(n) for n in range(2)]

    def pring_of(n):
        rows = pl.ds(64 * n, 64)
        return Ring(p, lambda i: part.at[i, :, rows], (pr.at[n], pe.at[n]), n, add_rows, pss.at[n], prs.at[n])

    prings = [pring_of(n) for n in range(2)]

    barrier = pltpu.get_barrier_semaphore()
    for dev in (p.xpeer, p.up, p.down, p.cpeer):
        pl.semaphore_signal(barrier, inc=1, device_id={"dp": dev}, device_id_type=MESH)

    def greet(k, carry):
        pl.semaphore_signal(barrier, inc=1, device_id={"tensor": lax.rem(t + 2 * k, TP)}, device_id_type=MESH)
        return carry

    lax.fori_loop(1, NZ, greet, 0)
    pl.semaphore_signal(barrier, inc=1, device_id={"tensor": p.xsib}, device_id_type=MESH)
    pl.semaphore_signal(barrier, inc=1, device_id={"dp": p.xpeer, "tensor": p.xsib}, device_id_type=MESH)
    pl.semaphore_wait(barrier, 5 + NZ)

    def flow(f):
        kind = FlowY if f == 2 else Flow
        return kind(p, wall.at[f, d], block_of(f), lambda k: wss.at[f, k], lambda k: wrs.at[f, k])

    mixer = flow(3)
    deep = FlowDeep(p, dqkv, deep_block, lambda k: wss.at[4, k], lambda k: wrs.at[4, k])
    for n in range(3):
        loads[n].wait()
    for f in range(3):
        flow(f).start0()

    codev = code[...].astype(F32)
    pick = lax.broadcasted_iota(jnp.int32, codev.shape, 1)
    count = text.shape[0]
    whole = count // 128 * 128
    square_r = lax.broadcasted_iota(jnp.int32, (128, 128), 0)
    square_c = lax.broadcasted_iota(jnp.int32, (128, 128), 1)
    halves = [jnp.sum(jnp.where(square_r == square_c, jnp.broadcast_to(tid[h:h + 1].astype(F32), (128, 128)), 0.0),
                      axis=1, keepdims=True) for h in range(2)]
    text_want = jnp.concatenate(halves, axis=0) - (t * count).astype(F32)

    def named(want, start, width):
        lanes = lax.broadcasted_iota(jnp.int32, (FRAMES, width), 1).astype(F32) + start
        return (lanes == want).astype(BF16)

    loads[10].wait()
    found = dot(named(text_want, 0, whole), text[:whole])
    if count > whole:
        found = found + dot(named(text_want, whole, count - whole), text[whole:])
    emb[:, 0] = found.astype(BF16).reshape(TP, OWN, DD)
    loads[4].wait()

    def lookup(c, carry):
        want = jnp.sum(jnp.where(pick == c - 1, codev, 0.0), axis=1, keepdims=True) - (t * 128).astype(F32)
        emb[:, c] = dot(named(want, 0, 128), tabs[c - 1]).astype(BF16).reshape(TP, OWN, DD)
        return carry

    lax.fori_loop(1, 4, lookup, 0)
    erings[0].step(0)
    lax.fori_loop(4, CODEBOOKS, lookup, 0)
    erings[1].step(0)
    loads[5].wait()

    def norm_rows(n, carry):
        r = pl.ds(pl.multiple_of(n * 32, 32), 32)
        h = hid[r, :].astype(F32)
        scale = lax.rsqrt(jnp.mean(h * h, axis=-1, keepdims=True) + epsilon)
        normed[r, :] = (h * scale * gain[...]).astype(BF16)
        return carry

    lax.fori_loop(0, FRAMES // 32, norm_rows, 0)

    def side_rows(n, carry):
        frames = pl.ds(pl.multiple_of(n * 32 + xl * 16, 16), OWN)
        to = pl.ds(pl.multiple_of(n * 16, 16), OWN)
        hown[to, :] = hid[frames, pl.ds(pl.multiple_of(z * 512, 512), 512)]
        goal[to, :] = code[frames, :]
        return carry

    lax.fori_loop(0, NZ, side_rows, 0)
    def project(ns, first=False):
        for n in ns:
            for f in range(3):
                flow(f).core_in(n)
        y = p.blocks[ns[0]] // 4
        cols = normed[:, pl.ds(pl.multiple_of(y * 1024, 1024), 1024)]

        def one(i, carry):
            got_one = dot(cols, wall[i, pl.ds(4 * y, 4)].reshape(1024, 256))
            acc[i] = got_one if first else acc[i] + got_one
            return carry

        lax.fori_loop(0, 3, one, 0, unroll=3)

    flow(0).stage1()
    erings[0].step(1)
    flow(1).stage1()
    erings[1].step(1)
    flow(2).stage1()
    loads[3].wait()
    mixer.start0()
    project((0, 1), True)
    flow(0).stage2()
    erings[0].step(2)
    flow(1).stage2()
    flow(2).stage2()
    deep.start_x()
    mixer.stage1()
    erings[1].step(2)
    project((2, 4))
    for f in range(3):
        flow(f).stage3()
    mixer.stage2()
    loads[7].wait()
    deep.start_y()
    din_part = pl.ds(pl.multiple_of(128 * p.core, 128), 128)
    din_rest = pl.ds(pl.multiple_of(128 - 128 * p.core, 128), 128)
    din_x = pltpu.make_async_remote_copy(
        src_ref=din_h.at[din_part], dst_ref=din.at[xl, din_part], send_sem=hss.at[2], recv_sem=hrs.at[2],
        device_id={"tensor": p.xsib}, device_id_type=MESH)
    din_x.start()

    def din_core(some):
        view = din.at[1 - xl, some]
        return pltpu.make_async_remote_copy(
            src_ref=view, dst_ref=view, send_sem=hss.at[3], recv_sem=hrs.at[3],
            device_id={"dp": p.cpeer}, device_id_type=MESH)

    project((3, 5))
    erings[0].step(3)
    project((6, 7))

    order_q = lax.broadcasted_iota(jnp.int32, (FRAMES, FRAMES), 0)
    order_k = lax.broadcasted_iota(jnp.int32, (FRAMES, FRAMES), 1)
    causal = order_q >= order_k

    def rotate(v):
        half = HEAD_DIM // 2
        swapped = jnp.concatenate([v[:, half:], v[:, :half]], axis=1)
        return (v * cosr[...] + swapped * sinr[...]).astype(BF16)

    def attend(h, carry):
        cols = pl.ds(pl.multiple_of(h * HEAD_DIM, HEAD_DIM), HEAD_DIM)
        q = rotate(acc[0, :, cols])
        k = rotate(acc[1, :, cols])
        v = acc[2, :, cols].astype(BF16)
        scores = dot_t(q, k) * HEAD_DIM ** (-0.5)
        e = jnp.where(causal, jnp.exp(jnp.where(causal, scores, 0.0)), 0.0)
        w = (e / jnp.sum(e, axis=-1, keepdims=True)).astype(BF16)
        mixed_rows = dot(w, v).astype(BF16).reshape(NZ, 2, OWN, HEAD_DIM)
        for side in range(2):
            att[side * 128:side * 128 + 128, cols] = mixed_rows[:, side].reshape(128, HEAD_DIM)
        return carry

    lax.fori_loop(0, 2, attend, 0, unroll=2)
    deep.pass_x()
    erings[1].step(3)
    mixer.stage3()
    mixer.stage4()

    def cross(zz):
        return pltpu.make_async_remote_copy(
            src_ref=bs.at[zz], dst_ref=br.at[zz], send_sem=bss.at[zz], recv_sem=brs.at[zz],
            device_id={"tensor": p.xsib}, device_id_type=MESH)

    def near_far(n):
        step = (n + 1) // 2
        return lax.rem(z + 4 + jnp.where(lax.rem(n, 2) == 1, -step, step), NZ)

    def mixed(n, carry):
        zz = near_far(n)
        second = wall[3, 2 * zz + 1]
        bs[zz] = dot(att[pl.ds(pl.multiple_of(128 - 128 * xl, 128), 128), :], second).astype(BF16)
        cross(zz).start()
        part[zz, 2] = dot(att[pl.ds(pl.multiple_of(128 * xl, 128), 128), :], second).astype(BF16)
        one = dot(att[...], wall[3, 2 * zz]).astype(BF16)
        part[zz, 0] = one[:128]
        part[zz, 1] = one[128:]
        return carry

    lax.fori_loop(0, NZ, mixed, 0, unroll=2)

    def crossed(n, carry):
        zz = near_far(n)
        cross(zz).wait_recv()
        part[zz, 2] = (part[zz, 2].astype(F32) + br[zz].astype(F32)).astype(BF16)
        return carry

    crossed(0, 0)
    for n in range(2):
        prings[n].step(0)
    lax.fori_loop(1, 3, crossed, 0)
    for n in range(2):
        prings[n].step(1)
    deep.stage1()
    din_x.wait_recv()
    din_core(din_part).start()
    lax.fori_loop(3, 5, crossed, 0)
    for n in range(2):
        prings[n].step(2)

    def swap(src, dst, k):
        return pltpu.make_async_remote_copy(
            src_ref=src, dst_ref=dst, send_sem=xss.at[k], recv_sem=xrs.at[k],
            device_id={"tensor": p.xsib}, device_id_type=MESH)

    lax.fori_loop(5, 7, crossed, 0)
    for n in range(2):
        prings[n].step(3)
    deep.stage2()
    for n in range(2):
        erings[n].arrive()
        mine = pl.ds(4 * n, 4)
        eo[mine] = emb[2 * z + 1 - xl, mine] + er[n, 3, 1 - xl] + el[n, 3, 1 - xl]
    swap(eo, ei, 0).start()
    for n in range(2):
        prings[n].arrive()

    crossed(7, 0)

    def total(h):
        sides = [pr[n, 3, h].astype(F32) + pe[n, 3, h].astype(F32) for n in range(2)]
        return part[z, h].astype(F32) + jnp.concatenate(sides, axis=0)

    po[...] = total(1 - xl).astype(BF16)
    swap(po, pi, 1).start()
    head_part = pl.ds(p.core * 4, 4)
    head_rest = pl.ds(4 - p.core * 4, 4)
    head_x = pltpu.make_async_remote_copy(
        src_ref=heads.at[head_part], dst_ref=hx.at[head_part], send_sem=hss.at[0],
        recv_sem=hrs.at[0], device_id={"tensor": p.xsib}, device_id_type=MESH)
    head_x.start()
    loads[6].wait()
    din_core(din_rest).wait_recv()

    def scale_cols(b, summed):
        resid = summed + hown[:, b * 256:b * 256 + 256].astype(F32)
        gains = ogain[:, pl.ds(pl.multiple_of(z * 512 + b * 256, 256), 256)]
        return jnp.sum(resid * resid, axis=-1, keepdims=True), dot((resid * gains).astype(BF16), din[b])

    square, context = scale_cols(1, total(2))
    swap(po, pi, 1).wait_recv()
    square_b, context_b = scale_cols(0, total(xl) + pi[...].astype(F32))
    square = square + square_b
    cs[:, :, :DD] = (context + context_b).astype(BF16).reshape(NZ, OWN, DD)
    high = square.astype(BF16)
    low = (square - high.astype(F32)).astype(BF16)
    first = lax.broadcasted_iota(jnp.int32, (128, 128), 1) < 64
    both = jnp.where(first, high.astype(F32), low.astype(F32)).astype(BF16)
    cs[:, :, DD:] = both.reshape(NZ, OWN, 128)

    def share(k, sender):
        to = lax.rem(z + k, NZ)
        return pltpu.make_async_remote_copy(
            src_ref=cs.at[to], dst_ref=cr.at[sender], send_sem=css.at[k], recv_sem=crs.at[k],
            device_id={"tensor": 2 * to + xl}, device_id_type=MESH)

    def give(n, carry):
        share(lax.rem(near_far(n) - z + NZ, NZ), z).start()
        return carry

    lax.fori_loop(0, NZ - 1, give, 0)
    deep.stage3()
    cr[z] = cs[z]
    swap(eo, ei, 0).wait_recv()
    embeds = [emb[2 * z + xl, pl.ds(4 * n, 4)].astype(F32) + er[n, 3, xl].astype(F32) + el[n, 3, xl].astype(F32)
              + ei[pl.ds(4 * n, 4)].astype(F32) for n in range(2)]
    xin[...] = jnp.concatenate(embeds, axis=0).reshape(CODEBOOKS * OWN, DD)

    def take(k, carry):
        share(k, lax.rem(z + NZ - k, NZ)).wait_recv()
        return carry

    lax.fori_loop(1, NZ, take, 0)

    def gathered(n, carry):
        context, square = carry
        v = cr[n]
        hl = v[:, DD:].astype(F32)
        return context + v[:, :DD].astype(F32), square + hl[:, :1] + hl[:, 64:65]

    context, square = lax.fori_loop(0, NZ, gathered, (jnp.zeros((OWN, DD), F32), jnp.zeros((OWN, 1), F32)))
    context = context * lax.rsqrt(square / D + epsilon)

    def ring(n, way, s, block):
        view = fin.at[pl.ds(2 * n, 2), block]
        return pltpu.make_async_remote_copy(
            src_ref=view, dst_ref=view, send_sem=fss.at[n, 4 * way + s], recv_sem=frs.at[n, 4 * way + s],
            device_id={"tensor": p.zdown if way else p.zup}, device_id_type=MESH)

    rows = CODEBOOKS * OWN
    x = (context[None] + xin[...].reshape(CODEBOOKS, OWN, DD)).reshape(rows, DD)
    dn = (x * lax.rsqrt(jnp.mean(x * x, axis=-1, keepdims=True) + epsilon) * dgain[...]).astype(BF16)
    deep.stage4()

    def dproject(i, carry):
        proj[i] = dot(dn, wq[i]).astype(BF16)
        return carry

    lax.fori_loop(0, 3, dproject, 0, unroll=3)

    rq = lax.rem(lax.broadcasted_iota(jnp.int32, (2 * rows, rows), 0), rows)
    rk = lax.broadcasted_iota(jnp.int32, (2 * rows, rows), 1)
    seen = (lax.rem(rq, OWN) == lax.rem(rk, OWN)) & (rq >= rk)
    low_half = lax.broadcasted_iota(jnp.int32, (rows, 128), 1) < DHEAD_DIM

    def dattend(j, carry):
        cols = pl.ds(pl.multiple_of(j * 128, 128), 128)
        q, k, v = proj[0, :, cols], proj[1, :, cols], proj[2, :, cols]
        both = jnp.concatenate([jnp.where(low_half, q, jnp.zeros_like(q)), jnp.where(low_half, jnp.zeros_like(q), q)], axis=0)
        scores = dot_t(both, k) * DHEAD_DIM ** (-0.5)
        e = jnp.where(seen, jnp.exp(jnp.where(seen, scores, 0.0)), 0.0)
        w = (e / jnp.sum(e, axis=-1, keepdims=True)).astype(BF16)
        outs = dot(w, v)
        datt[:, cols] = jnp.where(low_half, outs[:rows], outs[rows:]).astype(BF16)
        return carry

    lax.fori_loop(0, DHEADS // 2, dattend, 0, unroll=8)
    loads[8].wait()
    out = x + dot(datt[...], wm[...])
    final = (out * lax.rsqrt(jnp.mean(out * out, axis=-1, keepdims=True) + epsilon) * fgain[...]).astype(BF16)
    fin[:, z] = final.reshape(CODEBOOKS, OWN, DD)

    for n in range(4):
        for way in range(2):
            ring(n, way, 0, z).start()

    head_x_in = pltpu.make_async_remote_copy(
        src_ref=hx.at[head_part], dst_ref=hx.at[head_part], send_sem=hss.at[1],
        recv_sem=hrs.at[0], device_id={"dp": p.cpeer}, device_id_type=MESH)
    head_c = pltpu.make_async_remote_copy(
        src_ref=hx.at[head_part], dst_ref=hx.at[head_part], send_sem=hss.at[1],
        recv_sem=hrs.at[1], device_id={"dp": p.cpeer}, device_id_type=MESH)
    head_c_in = pltpu.make_async_remote_copy(
        src_ref=hx.at[head_rest], dst_ref=hx.at[head_rest], send_sem=hss.at[1],
        recv_sem=hrs.at[1], device_id={"dp": p.cpeer}, device_id_type=MESH)
    placed = [pltpu.make_async_copy(hx.at[some], wh.at[some, :, sib_lanes], lsem.at[11 + n])
              for n, some in enumerate((head_part, head_rest))]

    for s in range(1, 4):
        for n in range(4):
            for way in range(2):
                block = lax.rem(z + (s if way else NZ - s), NZ)
                ring(n, way, s - 1, block).wait_recv()
                if s < 3 or way == n % 2:
                    ring(n, way, s, block).start()
        if s == 1:
            for one in (flow(0), flow(1), flow(2), mixer, deep, erings[0], erings[1], prings[0], prings[1]):
                one.drain()
            din_x.wait_send()
            din_core(din_part).wait_send()
            swap(eo, ei, 0).wait_send()
            swap(po, pi, 1).wait_send()

            def sent(k, carry):
                cross(k).wait_send()
                return carry

            def sent_far(k, carry):
                share(k, z).wait_send()
                return carry

            lax.fori_loop(0, NZ, sent, 0)
            lax.fori_loop(1, NZ, sent_far, 0)
        if s == 2:
            head_x_in.wait_recv()
            head_c.start()
            placed[0].start()
        if s == 3:
            head_c_in.wait_recv()
            placed[1].start()

    loads[9].wait()
    placed[0].wait()
    placed[1].wait()
    shared = OWN * NZ
    lanes = lax.broadcasted_iota(jnp.int32, (shared, 256), 1).astype(F32)
    spots = lax.broadcasted_iota(jnp.int32, (shared, 128), 1)
    goals = goal[...].astype(F32) - (z * 256).astype(F32)
    books = lax.broadcasted_iota(jnp.int32, goals.shape, 1)

    def book(c, total):
        logits = dot(fin[c].reshape(shared, DD), wh[c])
        e = jnp.sum(jnp.exp(logits), axis=-1, keepdims=True)
        want = jnp.sum(jnp.where(books == c, goals, 0.0), axis=1, keepdims=True)
        hit = jnp.sum(jnp.where(lanes == want, logits, 0.0), axis=-1, keepdims=True)
        total = jnp.where(spots == c, e, total)
        return jnp.where(spots == CODEBOOKS + c, hit, total)

    total_sums = jnp.zeros((shared, 128), F32)
    for h in range(2):
        for n in range(2 * h, 2 * h + 2):
            ring(n, n % 2, 3, lax.rem(z + 4, NZ)).wait_recv()
        total_sums = lax.fori_loop(4 * h, 4 * h + 4, book, total_sums, unroll=4)
    sums[...] = total_sums.reshape(NZ, OWN, 128)

    def reply(k, sender):
        to = lax.rem(z + k, NZ)
        return pltpu.make_async_remote_copy(
            src_ref=sums.at[to], dst_ref=got.at[sender], send_sem=tss.at[k], recv_sem=trs.at[k],
            device_id={"tensor": 2 * to + xl}, device_id_type=MESH)

    def start_reply(k, carry):
        reply(k, z).start()
        return carry

    def take_reply(k, carry):
        reply(k, lax.rem(z + NZ - k, NZ)).wait_recv()
        return carry

    lax.fori_loop(1, NZ, start_reply, 0)
    got[z] = sums[z]
    lax.fori_loop(1, NZ, take_reply, 0)
    both = got[0]
    for n in range(1, NZ):
        both = both + got[n]
    loss[...] = jnp.log(both[:, :CODEBOOKS]) - both[:, CODEBOOKS:2 * CODEBOOKS]

    head_x.wait_send()
    head_c.wait_send()

    def reply_sent(k, carry):
        reply(k, z).wait_send()
        return carry

    lax.fori_loop(1, NZ, reply_sent, 0)
    for n in range(4):
        for way in range(2):
            for s in range(4 if way == n % 2 else 3):
                ring(n, way, s, z).wait_send()


def shards(hidden_in, attn_gain, qkv_weight, mix_weight, out_gain, depth_in_weight, text_table, code_tables,
           depth_gain, depth_qkv, depth_mix, final_gain, heads_weight, text_ids, codes):
    half = HEAD_DIM // 2
    angles = np.arange(FRAMES)[:, None] * 10000.0 ** (-np.arange(half) / half)[None, :]
    cosv = np.concatenate([np.cos(angles)] * 2, axis=1).astype(np.float32)
    sinv = np.concatenate([-np.sin(angles), np.sin(angles)], axis=1).astype(np.float32)
    vmem = pl.BlockSpec(memory_space=pltpu.VMEM)
    anym = pl.BlockSpec(memory_space=pl.ANY)
    dma = pltpu.SemaphoreType.DMA
    b16 = lambda *shape: pltpu.VMEM(shape, BF16)
    f32 = lambda *shape: pltpu.VMEM(shape, F32)
    wide = DD + 128
    return pl.pallas_call(
        layer,
        out_shape=jax.ShapeDtypeStruct((OWN, CODEBOOKS), F32),
        in_specs=[vmem] * 8 + [anym] * 9,
        out_specs=vmem,
        scratch_shapes=[
            b16(FRAMES, D), b16(*text_table.shape), b16(128, 512), b16(2, 256, DD), b16(CODEBOOKS - 1, 128, DD),
            pltpu.VMEM((128, CODEBOOKS), jnp.int32),
            b16(4, DP, 256, 256), b16(FRAMES, D), f32(3, FRAMES, 256), b16(FRAMES, 256),
            b16(NZ, 3, 128, 256),
            b16(TP, CODEBOOKS, OWN, DD),
            b16(2, 4, 2, 4, OWN, DD), b16(2, 4, 2, 4, OWN, DD),
            b16(CODEBOOKS, OWN, DD), b16(CODEBOOKS, OWN, DD),
            b16(2, 4, 3, 64, 256), b16(2, 4, 3, 64, 256), b16(128, 256), b16(128, 256),
            b16(NZ, 128, 256), b16(NZ, 128, 256),
            b16(NZ, OWN, wide), b16(NZ, OWN, wide), f32(CODEBOOKS * OWN, DD),
            b16(3, DD, DD), b16(DD, DD), b16(CODEBOOKS, DD, 256), b16(CODEBOOKS, DD, 128),
            b16(3, CODEBOOKS * OWN, DD), b16(CODEBOOKS * OWN, DD),
            b16(CODEBOOKS, NZ, OWN, DD), f32(NZ, OWN, 128), f32(NZ, OWN, 128),
            dma((13,)),
            dma((5, 16)), dma((5, 16)),
            dma((2, 8)), dma((2, 8)),
            dma((2, 8)), dma((2, 8)),
            dma((NZ,)), dma((NZ,)),
            dma((2,)), dma((2,)),
            dma((NZ,)), dma((NZ,)),
            dma((4,)), dma((4,)),
            dma((4, 8)), dma((4, 8)),
            dma((NZ,)), dma((NZ,)),
        ],
        compiler_params=pltpu.CompilerParams(
            collective_id=0, has_side_effects=True, vmem_limit_bytes=60 * 2**20),
        name="layer",
    )(attn_gain[None], out_gain[None], text_ids.reshape(2, 128), codes, cosv, sinv, depth_gain[None],
      final_gain[None],
      hidden_in, text_table, qkv_weight, mix_weight, depth_in_weight, code_tables, depth_qkv, depth_mix, heads_weight)


def solution(mesh):
    in_specs = (
        P("dp", None),
        P(),
        P(None, "dp", "tensor"),
        P("tensor", "dp"),
        P(),
        P("tensor", None),
        P("tensor", None),
        P(None, "tensor", None),
        P(),
        P(None, "dp", None),
        P(),
        P(),
        P(None, None, "tensor"),
        P("dp"),
        P("dp", None),
    )
    out_specs = P(("dp", "tensor"), None)
    return jax.shard_map(shards, mesh=mesh, in_specs=in_specs, out_specs=out_specs, check_vma=False)
```

```python
import functools

import jax
import jax.numpy as jnp
import numpy as np
from jax import lax
from jax.experimental import pallas as pl
from jax.experimental.pallas import tpu as pltpu
from jax.sharding import PartitionSpec as P

D = 4096
HEAD_DIM = 128
FRAMES = 256
DD = 1024
DHEADS = 16
DHEAD_DIM = 64
CODEBOOKS = 8
DP = 16
TP = 16
NZ = 8
OWN = 16
F32 = jnp.float32
BF16 = jnp.bfloat16
MESH = pl.DeviceIdType.MESH

epsilon = 1e-05

X0, R1, L1, R2, L2, R3, L3, C0 = range(8)


def dot(a, b):
    return jnp.dot(a, b, preferred_element_type=F32)


def dot_t(a, b):
    return lax.dot_general(a, b, (((1,), (1,)), ((), ())), preferred_element_type=F32)


class Places:
    def __init__(self):
        d = lax.axis_index("dp")
        t = lax.axis_index("tensor")
        self.d, self.t = d, t
        self.core = lax.rem(d, 2)
        self.xh = lax.rem(d // 2, 2)
        self.xl = lax.rem(t, 2)
        self.z = t // 2
        self.up = lax.rem(d + 4, 16)
        self.down = lax.rem(d + 12, 16)
        self.far = lax.rem(d + 8, 16)
        self.xstep = 2 - 4 * self.xh
        self.xpeer = d + self.xstep
        self.cstep = 1 - 2 * self.core
        self.cpeer = d + self.cstep
        self.xsib = t + 1 - 2 * self.xl
        self.zup = lax.rem(t + 2, 16)
        self.zdown = lax.rem(t + 14, 16)
        self.blocks = [d, self.xpeer, self.down, self.up, self.down + self.xstep,
                       self.up + self.xstep, self.far, self.far + self.xstep]


class Flow:
    def __init__(self, pos, own, block, send_sem, recv_sem):
        self.pos, self.own, self.block = pos, own, block
        self.ss, self.rs = send_sem, recv_sem

    def copy(self, kind, idx, dev, own=False):
        src = self.own if own else self.block(idx)
        return pltpu.make_async_remote_copy(
            src_ref=src, dst_ref=self.block(idx), send_sem=self.ss(kind), recv_sem=self.rs(kind),
            device_id={"dp": dev}, device_id_type=MESH)

    def start0(self):
        p = self.pos
        for kind, dev in ((X0, p.xpeer), (R1, p.up), (L1, p.down), (C0, p.cpeer)):
            self.copy(kind, p.d, dev, own=True).start()

    def core_in(self, n):
        p = self.pos
        self.copy(C0 + n, p.blocks[n] + p.cstep, p.cpeer).wait_recv()

    def got(self, kind):
        p = self.pos
        self.copy(kind, p.blocks[kind + 1], p.cpeer).wait_recv()

    def forward(self, kind, idx, dev):
        self.copy(kind, idx, dev).start()

    def to_core(self, kind):
        p = self.pos
        self.forward(C0 + kind + 1, p.blocks[kind + 1], p.cpeer)

    def stage1(self):
        p = self.pos
        self.got(X0)
        self.forward(R2, p.xpeer, p.up)
        self.forward(L2, p.xpeer, p.down)
        self.to_core(X0)
        self.got(R1)
        self.forward(R3, p.down, p.up)
        self.to_core(R1)
        self.got(L1)
        self.to_core(L1)

    def stage2(self):
        p = self.pos
        self.got(R2)
        self.to_core(R2)
        self.got(L2)
        self.forward(L3, p.up + p.xstep, p.down)
        self.to_core(L2)

    def stage3(self):
        self.got(R3)
        self.to_core(R3)
        self.got(L3)
        self.to_core(L3)

    def stage4(self):
        p = self.pos
        for n in range(8):
            self.core_in(n)

    def drain(self):
        p = self.pos
        for kind in range(15):
            self.copy(kind, p.d, p.cpeer).wait_send()


class FlowDeep(Flow):
    def start_x(self):
        p = self.pos
        pltpu.make_async_remote_copy(
            src_ref=self.own, dst_ref=self.block(p.d), send_sem=self.ss(X0), recv_sem=self.rs(X0),
            device_id={"dp": p.xpeer, "tensor": p.xsib}, device_id_type=MESH).start()
        self.copy(C0, p.d, p.cpeer, own=True).start()

    def start_y(self):
        p = self.pos
        self.copy(R1, p.d, p.up, own=True).start()
        self.copy(L1, p.d, p.down, own=True).start()

    def pass_x(self):
        p = self.pos
        self.got(X0)
        self.forward(R2, p.xpeer, p.up)
        self.forward(L2, p.xpeer, p.down)
        self.to_core(X0)

    def stage1(self):
        p = self.pos
        self.got(R1)
        self.forward(R3, p.down, p.up)
        self.to_core(R1)
        self.got(L1)
        self.to_core(L1)


class FlowY(Flow):
    def half(self, kind, idx, dev, which):
        view = self.block(idx).at[pl.ds(which * 128, 128)]
        return pltpu.make_async_remote_copy(
            src_ref=view, dst_ref=view, send_sem=self.ss(kind), recv_sem=self.rs(kind),
            device_id={"dp": dev}, device_id_type=MESH)

    def start0(self):
        p = self.pos
        for kind, dev in ((R1, p.up), (L1, p.down), (X0, p.xpeer), (C0, p.cpeer)):
            self.copy(kind, p.d, dev, own=True).start()

    def across(self, kind, idx):
        self.forward(kind, idx, self.pos.xpeer)

    def stage1(self):
        p = self.pos
        self.got(R1)
        self.half(L3, p.down, p.up, 0).start()
        self.across(R2, p.down)
        self.forward(C0 + 2, p.down, p.cpeer)
        self.got(L1)
        self.half(15, p.up, p.down, 1).start()
        self.across(L2, p.up)
        self.forward(C0 + 3, p.up, p.cpeer)
        self.got(X0)
        self.forward(C0 + 1, p.xpeer, p.cpeer)

    def stage2(self):
        p = self.pos
        self.half(L3, p.far, p.up, 0).wait_recv()
        self.half(15, p.far, p.down, 1).wait_recv()
        self.across(R3, p.far)
        self.forward(C0 + 6, p.far, p.cpeer)
        self.got(R2)
        self.forward(C0 + 4, p.blocks[4], p.cpeer)
        self.got(L2)
        self.forward(C0 + 5, p.blocks[5], p.cpeer)

    def stage3(self):
        p = self.pos
        self.got(R3)
        self.forward(C0 + 7, p.blocks[7], p.cpeer)

    def drain(self):
        p = self.pos
        for kind in range(16):
            if kind in (L3, 15):
                self.half(kind, p.d, p.up, 0).wait_send()
            else:
                self.copy(kind, p.d, p.cpeer).wait_send()


class Ring:
    def __init__(self, pos, own, slots, long, add, ss, rs):
        self.pos, self.own, self.slots, self.long, self.add = pos, own, slots, long, add
        self.ss, self.rs = ss, rs

    def first(self, way):
        return 0 if way == self.long else 1

    def dest(self, way, s):
        return lax.rem(self.pos.z + (4 - s if way == 0 else 4 + s), NZ)

    def copy(self, way, s):
        slots = self.slots[way]
        src = self.own(self.dest(way, s)) if s == self.first(way) else slots.at[s - 1]
        k = 4 * way + s
        return pltpu.make_async_remote_copy(
            src_ref=src, dst_ref=slots.at[s], send_sem=self.ss.at[k], recv_sem=self.rs.at[k],
            device_id={"tensor": self.pos.zdown if way else self.pos.zup}, device_id_type=MESH)

    def step(self, s):
        for way in range(2):
            if s < self.first(way):
                continue
            if s > self.first(way):
                self.copy(way, s - 1).wait_recv()
                self.add(self.slots[way].at[s - 1], self.own(self.dest(way, s)))
            self.copy(way, s).start()

    def arrive(self):
        for way in range(2):
            self.copy(way, 3).wait_recv()

    def drain(self):
        for way in range(2):
            for s in range(self.first(way), 4):
                self.copy(way, s).wait_send()


def layer(gain, ogain, tid, code_t, cosr, sinr, dgain, fgain,
          hid_h, text_h, qkv_h, mix_h, din_h, tabs_h, dqkv, dmix_h, heads,
          loss,
          hid, text, hown, din, tabs, goal, code, wall, normed, acc, att, part, emb, er, el, eo, ei, pr, pe, po, pi, bs, br,
          cs, cr, xin, wq, wm, wh, hx, proj, datt, fin, sums, got,
          lsem, wss, wrs, ess, ers, pss, prs, bss, brs, xss, xrs, css, crs, hss, hrs, fss, frs, tss, trs):
    p = Places()
    d, t, z, xl = p.d, p.t, p.z, p.xl

    def block_of(f):
        return lambda i: wall.at[f, i]

    deep_block = lambda i: wq.at[:, pl.ds(pl.multiple_of(i * 64, 64), 64), :]
    own_lanes = pl.ds(pl.multiple_of(xl * 128, 128), 128)
    sib_lanes = pl.ds(pl.multiple_of((1 - xl) * 128, 128), 128)
    loads = [(qkv_h.at[0], wall.at[0, d]), (qkv_h.at[1], wall.at[1, d]), (qkv_h.at[2], wall.at[2, d]),
             (mix_h, wall.at[3, d]), (tabs_h, tabs), (hid_h, hid), (din_h, din.at[xl]), (dqkv, deep_block(d)),
             (dmix_h, wm), (heads, wh.at[:, :, own_lanes]), (text_h, text)]
    loads = [pltpu.make_async_copy(src, dst, lsem.at[n]) for n, (src, dst) in enumerate(loads)]
    for one in loads:
        one.start()

    def add_books(a, b):
        def one(n, carry):
            h, c = n // 4, lax.rem(n, 4)
            a[h, c] = a[h, c] + b[h, c]
            return carry

        lax.fori_loop(0, 8, one, 0)

    def add_rows(a, b):
        def one(n, carry):
            a[n] = (a[n].astype(F32) + b[n].astype(F32)).astype(BF16)
            return carry

        lax.fori_loop(0, 3, one, 0)

    def ering_of(n):
        books = pl.ds(4 * n, 4)
        return Ring(p, lambda i: emb.at[pl.ds(2 * i, 2), books], (er.at[n], el.at[n]), n, add_books, ess.at[n], ers.at[n])

    erings = [ering_of(n) for n in range(2)]

    def pring_of(n):
        rows = pl.ds(64 * n, 64)
        return Ring(p, lambda i: part.at[i, :, rows], (pr.at[n], pe.at[n]), n, add_rows, pss.at[n], prs.at[n])

    prings = [pring_of(n) for n in range(2)]

    barrier = pltpu.get_barrier_semaphore()
    for dev in (p.xpeer, p.up, p.down, p.cpeer):
        pl.semaphore_signal(barrier, inc=1, device_id={"dp": dev}, device_id_type=MESH)

    def greet(k, carry):
        pl.semaphore_signal(barrier, inc=1, device_id={"tensor": lax.rem(t + 2 * k, TP)}, device_id_type=MESH)
        return carry

    lax.fori_loop(1, NZ, greet, 0)
    pl.semaphore_signal(barrier, inc=1, device_id={"tensor": p.xsib}, device_id_type=MESH)
    pl.semaphore_signal(barrier, inc=1, device_id={"dp": p.xpeer, "tensor": p.xsib}, device_id_type=MESH)
    pl.semaphore_wait(barrier, 5 + NZ)

    def flow(f):
        kind = FlowY if f == 2 else Flow
        return kind(p, wall.at[f, d], block_of(f), lambda k: wss.at[f, k], lambda k: wrs.at[f, k])

    mixer = flow(3)
    deep = FlowDeep(p, dqkv, deep_block, lambda k: wss.at[4, k], lambda k: wrs.at[4, k])
    for n in range(3):
        loads[n].wait()
    for f in range(3):
        flow(f).start0()

    codev = code_t[...].astype(F32).T
    code[...] = codev
    pick = lax.broadcasted_iota(jnp.int32, codev.shape, 1)
    count = text.shape[0]
    whole = count // 128 * 128
    square_r = lax.broadcasted_iota(jnp.int32, (128, 128), 0)
    square_c = lax.broadcasted_iota(jnp.int32, (128, 128), 1)
    halves = [jnp.sum(jnp.where(square_r == square_c, jnp.broadcast_to(tid[h:h + 1].astype(F32), (128, 128)), 0.0),
                      axis=1, keepdims=True) for h in range(2)]
    text_want = jnp.concatenate(halves, axis=0) - (t * count).astype(F32)

    def named(want, start, width):
        lanes = lax.broadcasted_iota(jnp.int32, (FRAMES, width), 1).astype(F32) + start
        return (lanes == want).astype(BF16)

    loads[10].wait()
    found = dot(named(text_want, 0, whole), text[:whole])
    if count > whole:
        found = found + dot(named(text_want, whole, count - whole), text[whole:])
    emb[:, 0] = found.astype(BF16).reshape(TP, OWN, DD)
    loads[4].wait()

    def lookup(c, carry):
        want = jnp.sum(jnp.where(pick == c - 1, codev, 0.0), axis=1, keepdims=True) - (t * 128).astype(F32)
        emb[:, c] = dot(named(want, 0, 128), tabs[c - 1]).astype(BF16).reshape(TP, OWN, DD)
        return carry

    lax.fori_loop(1, 4, lookup, 0)
    erings[0].step(0)
    lax.fori_loop(4, CODEBOOKS, lookup, 0)
    erings[1].step(0)
    loads[5].wait()

    def norm_rows(n, carry):
        r = pl.ds(pl.multiple_of(n * 32, 32), 32)
        h = hid[r, :].astype(F32)
        scale = lax.rsqrt(jnp.mean(h * h, axis=-1, keepdims=True) + epsilon)
        normed[r, :] = (h * scale * gain[...]).astype(BF16)
        return carry

    lax.fori_loop(0, FRAMES // 32, norm_rows, 0)

    def side_rows(n, carry):
        frames = pl.ds(pl.multiple_of(n * 32 + xl * 16, 16), OWN)
        to = pl.ds(pl.multiple_of(n * 16, 16), OWN)
        hown[to, :] = hid[frames, pl.ds(pl.multiple_of(z * 512, 512), 512)]
        goal[to, :] = code[frames, :]
        return carry

    lax.fori_loop(0, NZ, side_rows, 0)
    def project(ns, first=False):
        for n in ns:
            for f in range(3):
                flow(f).core_in(n)
        y = p.blocks[ns[0]] // 4
        cols = normed[:, pl.ds(pl.multiple_of(y * 1024, 1024), 1024)]

        def one(i, carry):
            got_one = dot(cols, wall[i, pl.ds(4 * y, 4)].reshape(1024, 256))
            acc[i] = got_one if first else acc[i] + got_one
            return carry

        lax.fori_loop(0, 3, one, 0, unroll=3)

    flow(0).stage1()
    erings[0].step(1)
    flow(1).stage1()
    erings[1].step(1)
    flow(2).stage1()
    loads[3].wait()
    mixer.start0()
    project((0, 1), True)
    flow(0).stage2()
    erings[0].step(2)
    flow(1).stage2()
    flow(2).stage2()
    deep.start_x()
    mixer.stage1()
    erings[1].step(2)
    project((2, 4))
    for f in range(3):
        flow(f).stage3()
    mixer.stage2()
    loads[7].wait()
    deep.start_y()
    din_part = pl.ds(pl.multiple_of(128 * p.core, 128), 128)
    din_rest = pl.ds(pl.multiple_of(128 - 128 * p.core, 128), 128)
    din_x = pltpu.make_async_remote_copy(
        src_ref=din_h.at[din_part], dst_ref=din.at[xl, din_part], send_sem=hss.at[2], recv_sem=hrs.at[2],
        device_id={"tensor": p.xsib}, device_id_type=MESH)
    din_x.start()

    def din_core(some):
        view = din.at[1 - xl, some]
        return pltpu.make_async_remote_copy(
            src_ref=view, dst_ref=view, send_sem=hss.at[3], recv_sem=hrs.at[3],
            device_id={"dp": p.cpeer}, device_id_type=MESH)

    project((3, 5))
    erings[0].step(3)
    project((6, 7))

    order_q = lax.broadcasted_iota(jnp.int32, (FRAMES, FRAMES), 0)
    order_k = lax.broadcasted_iota(jnp.int32, (FRAMES, FRAMES), 1)
    causal = order_q >= order_k

    def rotate(v):
        half = HEAD_DIM // 2
        swapped = jnp.concatenate([v[:, half:], v[:, :half]], axis=1)
        return (v * cosr[...] + swapped * sinr[...]).astype(BF16)

    def attend(h, carry):
        cols = pl.ds(pl.multiple_of(h * HEAD_DIM, HEAD_DIM), HEAD_DIM)
        q = rotate(acc[0, :, cols])
        k = rotate(acc[1, :, cols])
        v = acc[2, :, cols].astype(BF16)
        scores = dot_t(q, k) * HEAD_DIM ** (-0.5)
        e = jnp.where(causal, jnp.exp(jnp.where(causal, scores, 0.0)), 0.0)
        w = (e / jnp.sum(e, axis=-1, keepdims=True)).astype(BF16)
        mixed_rows = dot(w, v).astype(BF16).reshape(NZ, 2, OWN, HEAD_DIM)
        for side in range(2):
            att[side * 128:side * 128 + 128, cols] = mixed_rows[:, side].reshape(128, HEAD_DIM)
        return carry

    lax.fori_loop(0, 2, attend, 0, unroll=2)
    erings[1].step(3)
    mixer.stage3()
    deep.pass_x()
    mixer.stage4()

    def cross(zz):
        return pltpu.make_async_remote_copy(
            src_ref=bs.at[zz], dst_ref=br.at[zz], send_sem=bss.at[zz], recv_sem=brs.at[zz],
            device_id={"tensor": p.xsib}, device_id_type=MESH)

    def near_far(n):
        step = (n + 1) // 2
        return lax.rem(z + 4 + jnp.where(lax.rem(n, 2) == 1, -step, step), NZ)

    def mixed(n, carry):
        zz = near_far(n)
        second = wall[3, 2 * zz + 1]
        bs[zz] = dot(att[pl.ds(pl.multiple_of(128 - 128 * xl, 128), 128), :], second).astype(BF16)
        cross(zz).start()
        part[zz, 2] = dot(att[pl.ds(pl.multiple_of(128 * xl, 128), 128), :], second).astype(BF16)
        one = dot(att[...], wall[3, 2 * zz]).astype(BF16)
        part[zz, 0] = one[:128]
        part[zz, 1] = one[128:]
        return carry

    lax.fori_loop(0, NZ, mixed, 0, unroll=2)

    def crossed(n, carry):
        zz = near_far(n)
        cross(zz).wait_recv()
        part[zz, 2] = (part[zz, 2].astype(F32) + br[zz].astype(F32)).astype(BF16)
        return carry

    crossed(0, 0)
    for n in range(2):
        prings[n].step(0)
    lax.fori_loop(1, 3, crossed, 0)
    for n in range(2):
        prings[n].step(1)
    deep.stage1()
    din_x.wait_recv()
    din_core(din_part).start()
    lax.fori_loop(3, 5, crossed, 0)
    for n in range(2):
        prings[n].step(2)

    def swap(src, dst, k):
        return pltpu.make_async_remote_copy(
            src_ref=src, dst_ref=dst, send_sem=xss.at[k], recv_sem=xrs.at[k],
            device_id={"tensor": p.xsib}, device_id_type=MESH)

    lax.fori_loop(5, 7, crossed, 0)
    for n in range(2):
        prings[n].step(3)
    deep.stage2()
    for n in range(2):
        erings[n].arrive()
        mine = pl.ds(4 * n, 4)
        eo[mine] = emb[2 * z + 1 - xl, mine] + er[n, 3, 1 - xl] + el[n, 3, 1 - xl]
    swap(eo, ei, 0).start()
    for n in range(2):
        prings[n].arrive()

    crossed(7, 0)

    def total(h):
        sides = [pr[n, 3, h].astype(F32) + pe[n, 3, h].astype(F32) for n in range(2)]
        return part[z, h].astype(F32) + jnp.concatenate(sides, axis=0)

    po[...] = total(1 - xl).astype(BF16)
    swap(po, pi, 1).start()
    head_part = pl.ds(p.core * 4, 4)
    head_rest = pl.ds(4 - p.core * 4, 4)
    head_x = pltpu.make_async_remote_copy(
        src_ref=heads.at[head_part], dst_ref=hx.at[head_part], send_sem=hss.at[0],
        recv_sem=hrs.at[0], device_id={"tensor": p.xsib}, device_id_type=MESH)
    head_x.start()
    loads[6].wait()
    din_core(din_rest).wait_recv()

    def scale_cols(b, summed):
        resid = summed + hown[:, b * 256:b * 256 + 256].astype(F32)
        gains = ogain[:, pl.ds(pl.multiple_of(z * 512 + b * 256, 256), 256)]
        return jnp.sum(resid * resid, axis=-1, keepdims=True), dot((resid * gains).astype(BF16), din[b])

    square, context = scale_cols(1, total(2))
    swap(po, pi, 1).wait_recv()
    square_b, context_b = scale_cols(0, total(xl) + pi[...].astype(F32))
    square = square + square_b
    cs[:, :, :DD] = (context + context_b).astype(BF16).reshape(NZ, OWN, DD)
    high = square.astype(BF16)
    low = (square - high.astype(F32)).astype(BF16)
    first = lax.broadcasted_iota(jnp.int32, (128, 128), 1) < 64
    both = jnp.where(first, high.astype(F32), low.astype(F32)).astype(BF16)
    cs[:, :, DD:] = both.reshape(NZ, OWN, 128)

    def share(k, sender):
        to = lax.rem(z + k, NZ)
        return pltpu.make_async_remote_copy(
            src_ref=cs.at[to], dst_ref=cr.at[sender], send_sem=css.at[k], recv_sem=crs.at[k],
            device_id={"tensor": 2 * to + xl}, device_id_type=MESH)

    def give(n, carry):
        share(lax.rem(near_far(n) - z + NZ, NZ), z).start()
        return carry

    lax.fori_loop(0, NZ - 1, give, 0)
    deep.stage3()
    cr[z] = cs[z]
    swap(eo, ei, 0).wait_recv()
    embeds = [emb[2 * z + xl, pl.ds(4 * n, 4)].astype(F32) + er[n, 3, xl].astype(F32) + el[n, 3, xl].astype(F32)
              + ei[pl.ds(4 * n, 4)].astype(F32) for n in range(2)]
    xin[...] = jnp.concatenate(embeds, axis=0).reshape(CODEBOOKS * OWN, DD)

    def take(k, carry):
        share(k, lax.rem(z + NZ - k, NZ)).wait_recv()
        return carry

    lax.fori_loop(1, NZ, take, 0)

    def gathered(n, carry):
        context, square = carry
        v = cr[n]
        hl = v[:, DD:].astype(F32)
        return context + v[:, :DD].astype(F32), square + hl[:, :1] + hl[:, 64:65]

    context, square = lax.fori_loop(0, NZ, gathered, (jnp.zeros((OWN, DD), F32), jnp.zeros((OWN, 1), F32)))
    context = context * lax.rsqrt(square / D + epsilon)

    def ring(n, way, s, block):
        view = fin.at[pl.ds(2 * n, 2), block]
        return pltpu.make_async_remote_copy(
            src_ref=view, dst_ref=view, send_sem=fss.at[n, 4 * way + s], recv_sem=frs.at[n, 4 * way + s],
            device_id={"tensor": p.zdown if way else p.zup}, device_id_type=MESH)

    rows = CODEBOOKS * OWN
    x = (context[None] + xin[...].reshape(CODEBOOKS, OWN, DD)).reshape(rows, DD)
    dn = (x * lax.rsqrt(jnp.mean(x * x, axis=-1, keepdims=True) + epsilon) * dgain[...]).astype(BF16)
    deep.stage4()

    def dproject(i, carry):
        proj[i] = dot(dn, wq[i]).astype(BF16)
        return carry

    lax.fori_loop(0, 3, dproject, 0, unroll=3)

    rq = lax.rem(lax.broadcasted_iota(jnp.int32, (2 * rows, rows), 0), rows)
    rk = lax.broadcasted_iota(jnp.int32, (2 * rows, rows), 1)
    seen = (lax.rem(rq, OWN) == lax.rem(rk, OWN)) & (rq >= rk)
    low_half = lax.broadcasted_iota(jnp.int32, (rows, 128), 1) < DHEAD_DIM

    def dattend(j, carry):
        cols = pl.ds(pl.multiple_of(j * 128, 128), 128)
        q, k, v = proj[0, :, cols], proj[1, :, cols], proj[2, :, cols]
        both = jnp.concatenate([jnp.where(low_half, q, jnp.zeros_like(q)), jnp.where(low_half, jnp.zeros_like(q), q)], axis=0)
        scores = dot_t(both, k) * DHEAD_DIM ** (-0.5)
        e = jnp.where(seen, jnp.exp(jnp.where(seen, scores, 0.0)), 0.0)
        w = (e / jnp.sum(e, axis=-1, keepdims=True)).astype(BF16)
        outs = dot(w, v)
        datt[:, cols] = jnp.where(low_half, outs[:rows], outs[rows:]).astype(BF16)
        return carry

    lax.fori_loop(0, DHEADS // 2, dattend, 0, unroll=8)
    loads[8].wait()
    out = x + dot(datt[...], wm[...])
    final = (out * lax.rsqrt(jnp.mean(out * out, axis=-1, keepdims=True) + epsilon) * fgain[...]).astype(BF16)
    fin[:, z] = final.reshape(CODEBOOKS, OWN, DD)

    for n in range(4):
        for way in range(2):
            ring(n, way, 0, z).start()

    head_x_in = pltpu.make_async_remote_copy(
        src_ref=hx.at[head_part], dst_ref=hx.at[head_part], send_sem=hss.at[1],
        recv_sem=hrs.at[0], device_id={"dp": p.cpeer}, device_id_type=MESH)
    head_c = pltpu.make_async_remote_copy(
        src_ref=hx.at[head_part], dst_ref=hx.at[head_part], send_sem=hss.at[1],
        recv_sem=hrs.at[1], device_id={"dp": p.cpeer}, device_id_type=MESH)
    head_c_in = pltpu.make_async_remote_copy(
        src_ref=hx.at[head_rest], dst_ref=hx.at[head_rest], send_sem=hss.at[1],
        recv_sem=hrs.at[1], device_id={"dp": p.cpeer}, device_id_type=MESH)
    placed = [pltpu.make_async_copy(hx.at[some], wh.at[some, :, sib_lanes], lsem.at[11 + n])
              for n, some in enumerate((head_part, head_rest))]

    for s in range(1, 4):
        for n in range(4):
            for way in range(2):
                block = lax.rem(z + (s if way else NZ - s), NZ)
                ring(n, way, s - 1, block).wait_recv()
                if s < 3 or way == n % 2:
                    ring(n, way, s, block).start()
        if s == 1:
            for one in (flow(0), flow(1), flow(2), mixer, deep, erings[0], erings[1], prings[0], prings[1]):
                one.drain()
            din_x.wait_send()
            din_core(din_part).wait_send()
            swap(eo, ei, 0).wait_send()
            swap(po, pi, 1).wait_send()

            def sent(k, carry):
                cross(k).wait_send()
                return carry

            def sent_far(k, carry):
                share(k, z).wait_send()
                return carry

            lax.fori_loop(0, NZ, sent, 0)
            lax.fori_loop(1, NZ, sent_far, 0)
        if s == 2:
            head_x_in.wait_recv()
            head_c.start()
            placed[0].start()
        if s == 3:
            head_c_in.wait_recv()
            placed[1].start()

    loads[9].wait()
    placed[0].wait()
    placed[1].wait()
    shared = OWN * NZ
    lanes = lax.broadcasted_iota(jnp.int32, (shared, 256), 1).astype(F32)
    spots = lax.broadcasted_iota(jnp.int32, (shared, 128), 1)
    goals = goal[...] - (z * 256).astype(F32)
    books = lax.broadcasted_iota(jnp.int32, goals.shape, 1)

    def book(c, total):
        logits = dot(fin[c].reshape(shared, DD), wh[c])
        e = jnp.sum(jnp.exp(logits), axis=-1, keepdims=True)
        want = jnp.sum(jnp.where(books == c, goals, 0.0), axis=1, keepdims=True)
        hit = jnp.sum(jnp.where(lanes == want, logits, 0.0), axis=-1, keepdims=True)
        total = jnp.where(spots == c, e, total)
        return jnp.where(spots == CODEBOOKS + c, hit, total)

    total_sums = jnp.zeros((shared, 128), F32)
    for h in range(2):
        for n in range(2 * h, 2 * h + 2):
            ring(n, n % 2, 3, lax.rem(z + 4, NZ)).wait_recv()
        total_sums = lax.fori_loop(4 * h, 4 * h + 4, book, total_sums, unroll=4)
    sums[...] = total_sums.reshape(NZ, OWN, 128)

    def reply(k, sender):
        to = lax.rem(z + k, NZ)
        return pltpu.make_async_remote_copy(
            src_ref=sums.at[to], dst_ref=got.at[sender], send_sem=tss.at[k], recv_sem=trs.at[k],
            device_id={"tensor": 2 * to + xl}, device_id_type=MESH)

    def start_reply(k, carry):
        reply(k, z).start()
        return carry

    def take_reply(k, carry):
        reply(k, lax.rem(z + NZ - k, NZ)).wait_recv()
        return carry

    lax.fori_loop(1, NZ, start_reply, 0)
    got[z] = sums[z]
    lax.fori_loop(1, NZ, take_reply, 0)
    both = got[0]
    for n in range(1, NZ):
        both = both + got[n]
    loss[...] = jnp.log(both[:, :CODEBOOKS]) - both[:, CODEBOOKS:2 * CODEBOOKS]

    head_x.wait_send()
    head_c.wait_send()

    def reply_sent(k, carry):
        reply(k, z).wait_send()
        return carry

    lax.fori_loop(1, NZ, reply_sent, 0)
    for n in range(4):
        for way in range(2):
            for s in range(4 if way == n % 2 else 3):
                ring(n, way, s, z).wait_send()


def shards(hidden_in, attn_gain, qkv_weight, mix_weight, out_gain, depth_in_weight, text_table, code_tables,
           depth_gain, depth_qkv, depth_mix, final_gain, heads_weight, text_ids, codes):
    half = HEAD_DIM // 2
    angles = np.arange(FRAMES)[:, None] * 10000.0 ** (-np.arange(half) / half)[None, :]
    cosv = np.concatenate([np.cos(angles)] * 2, axis=1).astype(np.float32)
    sinv = np.concatenate([-np.sin(angles), np.sin(angles)], axis=1).astype(np.float32)
    vmem = pl.BlockSpec(memory_space=pltpu.VMEM)
    anym = pl.BlockSpec(memory_space=pl.ANY)
    dma = pltpu.SemaphoreType.DMA
    b16 = lambda *shape: pltpu.VMEM(shape, BF16)
    f32 = lambda *shape: pltpu.VMEM(shape, F32)
    wide = DD + 128
    return pl.pallas_call(
        layer,
        out_shape=jax.ShapeDtypeStruct((OWN, CODEBOOKS), F32),
        in_specs=[vmem] * 8 + [anym] * 9,
        out_specs=vmem,
        scratch_shapes=[
            b16(FRAMES, D), b16(*text_table.shape), b16(128, 512), b16(2, 256, DD), b16(CODEBOOKS - 1, 128, DD),
            f32(128, CODEBOOKS), f32(FRAMES, CODEBOOKS),
            b16(4, DP, 256, 256), b16(FRAMES, D), f32(3, FRAMES, 256), b16(FRAMES, 256),
            b16(NZ, 3, 128, 256),
            b16(TP, CODEBOOKS, OWN, DD),
            b16(2, 4, 2, 4, OWN, DD), b16(2, 4, 2, 4, OWN, DD),
            b16(CODEBOOKS, OWN, DD), b16(CODEBOOKS, OWN, DD),
            b16(2, 4, 3, 64, 256), b16(2, 4, 3, 64, 256), b16(128, 256), b16(128, 256),
            b16(NZ, 128, 256), b16(NZ, 128, 256),
            b16(NZ, OWN, wide), b16(NZ, OWN, wide), f32(CODEBOOKS * OWN, DD),
            b16(3, DD, DD), b16(DD, DD), b16(CODEBOOKS, DD, 256), b16(CODEBOOKS, DD, 128),
            b16(3, CODEBOOKS * OWN, DD), b16(CODEBOOKS * OWN, DD),
            b16(CODEBOOKS, NZ, OWN, DD), f32(NZ, OWN, 128), f32(NZ, OWN, 128),
            dma((13,)),
            dma((5, 16)), dma((5, 16)),
            dma((2, 8)), dma((2, 8)),
            dma((2, 8)), dma((2, 8)),
            dma((NZ,)), dma((NZ,)),
            dma((2,)), dma((2,)),
            dma((NZ,)), dma((NZ,)),
            dma((4,)), dma((4,)),
            dma((4, 8)), dma((4, 8)),
            dma((NZ,)), dma((NZ,)),
        ],
        compiler_params=pltpu.CompilerParams(
            collective_id=0, has_side_effects=True, vmem_limit_bytes=60 * 2**20),
        name="layer",
    )(attn_gain[None], out_gain[None], text_ids.reshape(2, 128), codes.T, cosv, sinv, depth_gain[None],
      final_gain[None],
      hidden_in, text_table, qkv_weight, mix_weight, depth_in_weight, code_tables, depth_qkv, depth_mix, heads_weight)


def solution(mesh):
    in_specs = (
        P("dp", None),
        P(),
        P(None, "dp", "tensor"),
        P("tensor", "dp"),
        P(),
        P("tensor", None),
        P("tensor", None),
        P(None, "tensor", None),
        P(),
        P(None, "dp", None),
        P(),
        P(),
        P(None, None, "tensor"),
        P("dp"),
        P("dp", None),
    )
    out_specs = P(("dp", "tensor"), None)
    return jax.shard_map(shards, mesh=mesh, in_specs=in_specs, out_specs=out_specs, check_vma=False)
```

```python
import functools

import jax
import jax.numpy as jnp
import numpy as np
from jax import lax
from jax.experimental import pallas as pl
from jax.experimental.pallas import tpu as pltpu
from jax.sharding import PartitionSpec as P

D = 4096
HEAD_DIM = 128
FRAMES = 256
DD = 1024
DHEADS = 16
DHEAD_DIM = 64
CODEBOOKS = 8
DP = 16
TP = 16
NZ = 8
OWN = 16
F32 = jnp.float32
BF16 = jnp.bfloat16
MESH = pl.DeviceIdType.MESH

epsilon = 1e-05

X0, R1, L1, R2, L2, R3, L3, C0 = range(8)


def dot(a, b):
    return jnp.dot(a, b, preferred_element_type=F32)


def dot_t(a, b):
    return lax.dot_general(a, b, (((1,), (1,)), ((), ())), preferred_element_type=F32)


class Places:
    def __init__(self):
        d = lax.axis_index("dp")
        t = lax.axis_index("tensor")
        self.d, self.t = d, t
        self.core = lax.rem(d, 2)
        self.xh = lax.rem(d // 2, 2)
        self.xl = lax.rem(t, 2)
        self.z = t // 2
        self.up = lax.rem(d + 4, 16)
        self.down = lax.rem(d + 12, 16)
        self.far = lax.rem(d + 8, 16)
        self.xstep = 2 - 4 * self.xh
        self.xpeer = d + self.xstep
        self.cstep = 1 - 2 * self.core
        self.cpeer = d + self.cstep
        self.xsib = t + 1 - 2 * self.xl
        self.zup = lax.rem(t + 2, 16)
        self.zdown = lax.rem(t + 14, 16)
        self.blocks = [d, self.xpeer, self.down, self.up, self.down + self.xstep,
                       self.up + self.xstep, self.far, self.far + self.xstep]


class Flow:
    def __init__(self, pos, own, block, send_sem, recv_sem):
        self.pos, self.own, self.block = pos, own, block
        self.ss, self.rs = send_sem, recv_sem

    def copy(self, kind, idx, dev, own=False):
        src = self.own if own else self.block(idx)
        return pltpu.make_async_remote_copy(
            src_ref=src, dst_ref=self.block(idx), send_sem=self.ss(kind), recv_sem=self.rs(kind),
            device_id={"dp": dev}, device_id_type=MESH)

    def start0(self):
        p = self.pos
        for kind, dev in ((X0, p.xpeer), (R1, p.up), (L1, p.down), (C0, p.cpeer)):
            self.copy(kind, p.d, dev, own=True).start()

    def core_in(self, n):
        p = self.pos
        self.copy(C0 + n, p.blocks[n] + p.cstep, p.cpeer).wait_recv()

    def got(self, kind):
        p = self.pos
        self.copy(kind, p.blocks[kind + 1], p.cpeer).wait_recv()

    def forward(self, kind, idx, dev):
        self.copy(kind, idx, dev).start()

    def to_core(self, kind):
        p = self.pos
        self.forward(C0 + kind + 1, p.blocks[kind + 1], p.cpeer)

    def stage1(self):
        p = self.pos
        self.got(X0)
        self.forward(R2, p.xpeer, p.up)
        self.forward(L2, p.xpeer, p.down)
        self.to_core(X0)
        self.got(R1)
        self.forward(R3, p.down, p.up)
        self.to_core(R1)
        self.got(L1)
        self.to_core(L1)

    def stage2(self):
        p = self.pos
        self.got(R2)
        self.to_core(R2)
        self.got(L2)
        self.forward(L3, p.up + p.xstep, p.down)
        self.to_core(L2)

    def stage3(self):
        self.got(R3)
        self.to_core(R3)
        self.got(L3)
        self.to_core(L3)

    def stage4(self):
        p = self.pos
        for n in range(8):
            self.core_in(n)

    def drain(self):
        p = self.pos
        for kind in range(15):
            self.copy(kind, p.d, p.cpeer).wait_send()


class FlowDeep(Flow):
    def start_x(self):
        p = self.pos
        pltpu.make_async_remote_copy(
            src_ref=self.own, dst_ref=self.block(p.d), send_sem=self.ss(X0), recv_sem=self.rs(X0),
            device_id={"dp": p.xpeer, "tensor": p.xsib}, device_id_type=MESH).start()
        self.copy(C0, p.d, p.cpeer, own=True).start()

    def start_y(self):
        p = self.pos
        self.copy(R1, p.d, p.up, own=True).start()
        self.copy(L1, p.d, p.down, own=True).start()

    def pass_x(self):
        p = self.pos
        self.got(X0)
        self.forward(R2, p.xpeer, p.up)
        self.forward(L2, p.xpeer, p.down)
        self.to_core(X0)

    def stage1(self):
        p = self.pos
        self.got(R1)
        self.forward(R3, p.down, p.up)
        self.to_core(R1)
        self.got(L1)
        self.to_core(L1)


class FlowY(Flow):
    def half(self, kind, idx, dev, which):
        view = self.block(idx).at[pl.ds(which * 128, 128)]
        return pltpu.make_async_remote_copy(
            src_ref=view, dst_ref=view, send_sem=self.ss(kind), recv_sem=self.rs(kind),
            device_id={"dp": dev}, device_id_type=MESH)

    def start0(self):
        p = self.pos
        for kind, dev in ((R1, p.up), (L1, p.down), (X0, p.xpeer), (C0, p.cpeer)):
            self.copy(kind, p.d, dev, own=True).start()

    def across(self, kind, idx):
        self.forward(kind, idx, self.pos.xpeer)

    def stage1(self):
        p = self.pos
        self.got(R1)
        self.half(L3, p.down, p.up, 0).start()
        self.across(R2, p.down)
        self.forward(C0 + 2, p.down, p.cpeer)
        self.got(L1)
        self.half(15, p.up, p.down, 1).start()
        self.across(L2, p.up)
        self.forward(C0 + 3, p.up, p.cpeer)
        self.got(X0)
        self.forward(C0 + 1, p.xpeer, p.cpeer)

    def stage2(self):
        p = self.pos
        self.half(L3, p.far, p.up, 0).wait_recv()
        self.half(15, p.far, p.down, 1).wait_recv()
        self.across(R3, p.far)
        self.forward(C0 + 6, p.far, p.cpeer)
        self.got(R2)
        self.forward(C0 + 4, p.blocks[4], p.cpeer)
        self.got(L2)
        self.forward(C0 + 5, p.blocks[5], p.cpeer)

    def stage3(self):
        p = self.pos
        self.got(R3)
        self.forward(C0 + 7, p.blocks[7], p.cpeer)

    def drain(self):
        p = self.pos
        for kind in range(16):
            if kind in (L3, 15):
                self.half(kind, p.d, p.up, 0).wait_send()
            else:
                self.copy(kind, p.d, p.cpeer).wait_send()


class Ring:
    def __init__(self, pos, own, slots, long, add, ss, rs):
        self.pos, self.own, self.slots, self.long, self.add = pos, own, slots, long, add
        self.ss, self.rs = ss, rs

    def first(self, way):
        return 0 if way == self.long else 1

    def dest(self, way, s):
        return lax.rem(self.pos.z + (4 - s if way == 0 else 4 + s), NZ)

    def copy(self, way, s):
        slots = self.slots[way]
        src = self.own(self.dest(way, s)) if s == self.first(way) else slots.at[s - 1]
        k = 4 * way + s
        return pltpu.make_async_remote_copy(
            src_ref=src, dst_ref=slots.at[s], send_sem=self.ss.at[k], recv_sem=self.rs.at[k],
            device_id={"tensor": self.pos.zdown if way else self.pos.zup}, device_id_type=MESH)

    def step(self, s):
        for way in range(2):
            if s < self.first(way):
                continue
            if s > self.first(way):
                self.copy(way, s - 1).wait_recv()
                self.add(self.slots[way].at[s - 1], self.own(self.dest(way, s)))
            self.copy(way, s).start()

    def arrive(self):
        for way in range(2):
            self.copy(way, 3).wait_recv()

    def drain(self):
        for way in range(2):
            for s in range(self.first(way), 4):
                self.copy(way, s).wait_send()


def layer(gain, ogain, tid, code_t, cosr, sinr, dgain, fgain,
          hid_h, text_h, qkv_h, mix_h, din_h, tabs_h, dqkv, dmix_h, heads,
          loss,
          hid, text, hown, din, tabs, goal, code, wall, normed, acc, att, part, emb, er, el, eo, ei, pr, pe, po, pi, bs, br,
          cs, cr, xin, wq, wm, wh, hx, proj, datt, fin, sums, got,
          lsem, wss, wrs, ess, ers, pss, prs, bss, brs, xss, xrs, css, crs, hss, hrs, fss, frs, tss, trs):
    p = Places()
    d, t, z, xl = p.d, p.t, p.z, p.xl

    def block_of(f):
        return lambda i: wall.at[f, i]

    deep_block = lambda i: wq.at[:, pl.ds(pl.multiple_of(i * 64, 64), 64), :]
    own_lanes = pl.ds(pl.multiple_of(xl * 128, 128), 128)
    sib_lanes = pl.ds(pl.multiple_of((1 - xl) * 128, 128), 128)
    loads = [(qkv_h.at[0], wall.at[0, d]), (qkv_h.at[1], wall.at[1, d]), (qkv_h.at[2], wall.at[2, d]),
             (mix_h, wall.at[3, d]), (tabs_h, tabs), (hid_h, hid), (din_h, din.at[xl]), (dqkv, deep_block(d)),
             (dmix_h, wm), (heads, wh.at[:, :, own_lanes]), (text_h, text)]
    loads = [pltpu.make_async_copy(src, dst, lsem.at[n]) for n, (src, dst) in enumerate(loads)]
    for one in loads:
        one.start()

    def add_books(a, b):
        def one(n, carry):
            h, c = n // 4, lax.rem(n, 4)
            a[h, c] = a[h, c] + b[h, c]
            return carry

        lax.fori_loop(0, 8, one, 0)

    def add_rows(a, b):
        def one(n, carry):
            a[n] = (a[n].astype(F32) + b[n].astype(F32)).astype(BF16)
            return carry

        lax.fori_loop(0, 3, one, 0)

    def ering_of(n):
        books = pl.ds(4 * n, 4)
        return Ring(p, lambda i: emb.at[pl.ds(2 * i, 2), books], (er.at[n], el.at[n]), n, add_books, ess.at[n], ers.at[n])

    erings = [ering_of(n) for n in range(2)]

    def pring_of(n):
        rows = pl.ds(64 * n, 64)
        return Ring(p, lambda i: part.at[i, :, rows], (pr.at[n], pe.at[n]), n, add_rows, pss.at[n], prs.at[n])

    prings = [pring_of(n) for n in range(2)]

    barrier = pltpu.get_barrier_semaphore()
    for dev in (p.xpeer, p.up, p.down, p.cpeer):
        pl.semaphore_signal(barrier, inc=1, device_id={"dp": dev}, device_id_type=MESH)

    def greet(k, carry):
        pl.semaphore_signal(barrier, inc=1, device_id={"tensor": lax.rem(t + 2 * k, TP)}, device_id_type=MESH)
        return carry

    lax.fori_loop(1, NZ, greet, 0)
    pl.semaphore_signal(barrier, inc=1, device_id={"tensor": p.xsib}, device_id_type=MESH)
    pl.semaphore_signal(barrier, inc=1, device_id={"dp": p.xpeer, "tensor": p.xsib}, device_id_type=MESH)
    pl.semaphore_wait(barrier, 5 + NZ)

    def flow(f):
        kind = FlowY if f == 2 else Flow
        return kind(p, wall.at[f, d], block_of(f), lambda k: wss.at[f, k], lambda k: wrs.at[f, k])

    mixer = flow(3)
    deep = FlowDeep(p, dqkv, deep_block, lambda k: wss.at[4, k], lambda k: wrs.at[4, k])
    for n in range(3):
        loads[n].wait()
    for f in range(3):
        flow(f).start0()

    codev = code_t[...].astype(F32).T
    code[...] = codev
    pick = lax.broadcasted_iota(jnp.int32, codev.shape, 1)
    count = text.shape[0]
    whole = count // 128 * 128
    square_r = lax.broadcasted_iota(jnp.int32, (128, 128), 0)
    square_c = lax.broadcasted_iota(jnp.int32, (128, 128), 1)
    halves = [jnp.sum(jnp.where(square_r == square_c, jnp.broadcast_to(tid[h:h + 1].astype(F32), (128, 128)), 0.0),
                      axis=1, keepdims=True) for h in range(2)]
    text_want = jnp.concatenate(halves, axis=0) - (t * count).astype(F32)

    def named(want, start, width):
        lanes = lax.broadcasted_iota(jnp.int32, (FRAMES, width), 1).astype(F32) + start
        return (lanes == want).astype(BF16)

    loads[10].wait()
    found = dot(named(text_want, 0, whole), text[:whole])
    if count > whole:
        found = found + dot(named(text_want, whole, count - whole), text[whole:])
    emb[:, 0] = found.astype(BF16).reshape(TP, OWN, DD)
    loads[4].wait()

    def lookup(c, carry):
        want = jnp.sum(jnp.where(pick == c - 1, codev, 0.0), axis=1, keepdims=True) - (t * 128).astype(F32)
        emb[:, c] = dot(named(want, 0, 128), tabs[c - 1]).astype(BF16).reshape(TP, OWN, DD)
        return carry

    lax.fori_loop(1, 4, lookup, 0)
    erings[0].step(0)
    lax.fori_loop(4, CODEBOOKS, lookup, 0)
    erings[1].step(0)
    loads[5].wait()

    def norm_rows(n, carry):
        r = pl.ds(pl.multiple_of(n * 32, 32), 32)
        h = hid[r, :].astype(F32)
        scale = lax.rsqrt(jnp.mean(h * h, axis=-1, keepdims=True) + epsilon)
        normed[r, :] = (h * scale * gain[...]).astype(BF16)
        return carry

    lax.fori_loop(0, FRAMES // 32, norm_rows, 0)

    def side_rows(n, carry):
        frames = pl.ds(pl.multiple_of(n * 32 + xl * 16, 16), OWN)
        to = pl.ds(pl.multiple_of(n * 16, 16), OWN)
        hown[to, :] = hid[frames, pl.ds(pl.multiple_of(z * 512, 512), 512)]
        goal[to, :] = code[frames, :]
        return carry

    lax.fori_loop(0, NZ, side_rows, 0)
    def project(ns, first=False):
        for n in ns:
            for f in range(3):
                flow(f).core_in(n)
        y = p.blocks[ns[0]] // 4
        cols = normed[:, pl.ds(pl.multiple_of(y * 1024, 1024), 1024)]

        def one(i, carry):
            got_one = dot(cols, wall[i, pl.ds(4 * y, 4)].reshape(1024, 256))
            acc[i] = got_one if first else acc[i] + got_one
            return carry

        lax.fori_loop(0, 3, one, 0, unroll=3)

    flow(0).stage1()
    erings[0].step(1)
    flow(1).stage1()
    erings[1].step(1)
    flow(2).stage1()
    loads[3].wait()
    mixer.start0()
    project((0, 1), True)
    flow(0).stage2()
    erings[0].step(2)
    flow(1).stage2()
    flow(2).stage2()
    deep.start_x()
    mixer.stage1()
    erings[1].step(2)
    project((2, 4))
    for f in range(3):
        flow(f).stage3()
    mixer.stage2()
    loads[7].wait()
    deep.start_y()
    din_part = pl.ds(pl.multiple_of(128 * p.core, 128), 128)
    din_rest = pl.ds(pl.multiple_of(128 - 128 * p.core, 128), 128)
    din_x = pltpu.make_async_remote_copy(
        src_ref=din_h.at[din_part], dst_ref=din.at[xl, din_part], send_sem=hss.at[2], recv_sem=hrs.at[2],
        device_id={"tensor": p.xsib}, device_id_type=MESH)
    din_x.start()

    def din_core(some):
        view = din.at[1 - xl, some]
        return pltpu.make_async_remote_copy(
            src_ref=view, dst_ref=view, send_sem=hss.at[3], recv_sem=hrs.at[3],
            device_id={"dp": p.cpeer}, device_id_type=MESH)

    project((3, 5))
    erings[0].step(3)
    project((6, 7))

    order_q = lax.broadcasted_iota(jnp.int32, (FRAMES, FRAMES), 0)
    order_k = lax.broadcasted_iota(jnp.int32, (FRAMES, FRAMES), 1)
    causal = order_q >= order_k

    def rotate(v):
        half = HEAD_DIM // 2
        swapped = jnp.concatenate([v[:, half:], v[:, :half]], axis=1)
        return (v * cosr[...] + swapped * sinr[...]).astype(BF16)

    def attend(h, carry):
        cols = pl.ds(pl.multiple_of(h * HEAD_DIM, HEAD_DIM), HEAD_DIM)
        q = rotate(acc[0, :, cols])
        k = rotate(acc[1, :, cols])
        v = acc[2, :, cols].astype(BF16)
        scores = dot_t(q, k) * HEAD_DIM ** (-0.5)
        e = jnp.where(causal, jnp.exp(jnp.where(causal, scores, 0.0)), 0.0)
        w = (e / jnp.sum(e, axis=-1, keepdims=True)).astype(BF16)
        mixed_rows = dot(w, v).astype(BF16).reshape(NZ, 2, OWN, HEAD_DIM)
        for side in range(2):
            att[side * 128:side * 128 + 128, cols] = mixed_rows[:, side].reshape(128, HEAD_DIM)
        return carry

    lax.fori_loop(0, 2, attend, 0, unroll=2)
    erings[1].step(3)
    mixer.stage3()
    deep.pass_x()
    mixer.stage4()

    def cross(zz):
        return pltpu.make_async_remote_copy(
            src_ref=bs.at[zz], dst_ref=br.at[zz], send_sem=bss.at[zz], recv_sem=brs.at[zz],
            device_id={"tensor": p.xsib}, device_id_type=MESH)

    def near_far(n):
        step = (n + 1) // 2
        return lax.rem(z + 4 + jnp.where(lax.rem(n, 2) == 1, -step, step), NZ)

    def mixed(n, carry):
        zz = near_far(n)
        second = wall[3, 2 * zz + 1]
        bs[zz] = dot(att[pl.ds(pl.multiple_of(128 - 128 * xl, 128), 128), :], second).astype(BF16)
        cross(zz).start()
        part[zz, 2] = dot(att[pl.ds(pl.multiple_of(128 * xl, 128), 128), :], second).astype(BF16)
        one = dot(att[...], wall[3, 2 * zz]).astype(BF16)
        part[zz, 0] = one[:128]
        part[zz, 1] = one[128:]
        return carry

    lax.fori_loop(0, NZ, mixed, 0, unroll=2)

    def crossed(n, carry):
        zz = near_far(n)
        cross(zz).wait_recv()
        part[zz, 2] = (part[zz, 2].astype(F32) + br[zz].astype(F32)).astype(BF16)
        return carry

    crossed(0, 0)
    for n in range(2):
        prings[n].step(0)
    lax.fori_loop(1, 3, crossed, 0, unroll=2)
    for n in range(2):
        prings[n].step(1)
    deep.stage1()
    din_x.wait_recv()
    din_core(din_part).start()
    lax.fori_loop(3, 5, crossed, 0, unroll=2)
    for n in range(2):
        prings[n].step(2)

    def swap(src, dst, k):
        return pltpu.make_async_remote_copy(
            src_ref=src, dst_ref=dst, send_sem=xss.at[k], recv_sem=xrs.at[k],
            device_id={"tensor": p.xsib}, device_id_type=MESH)

    lax.fori_loop(5, 7, crossed, 0, unroll=2)
    for n in range(2):
        prings[n].step(3)
    deep.stage2()
    for n in range(2):
        erings[n].arrive()
        mine = pl.ds(4 * n, 4)
        eo[mine] = emb[2 * z + 1 - xl, mine] + er[n, 3, 1 - xl] + el[n, 3, 1 - xl]
    swap(eo, ei, 0).start()
    for n in range(2):
        prings[n].arrive()

    crossed(7, 0)

    def total(h):
        sides = [pr[n, 3, h].astype(F32) + pe[n, 3, h].astype(F32) for n in range(2)]
        return part[z, h].astype(F32) + jnp.concatenate(sides, axis=0)

    po[...] = total(1 - xl).astype(BF16)
    swap(po, pi, 1).start()
    head_part = pl.ds(p.core * 4, 4)
    head_rest = pl.ds(4 - p.core * 4, 4)
    head_x = pltpu.make_async_remote_copy(
        src_ref=heads.at[head_part], dst_ref=hx.at[head_part], send_sem=hss.at[0],
        recv_sem=hrs.at[0], device_id={"tensor": p.xsib}, device_id_type=MESH)
    head_x.start()
    loads[6].wait()
    din_core(din_rest).wait_recv()

    def scale_cols(b, summed):
        resid = summed + hown[:, b * 256:b * 256 + 256].astype(F32)
        gains = ogain[:, pl.ds(pl.multiple_of(z * 512 + b * 256, 256), 256)]
        return jnp.sum(resid * resid, axis=-1, keepdims=True), dot((resid * gains).astype(BF16), din[b])

    square, context = scale_cols(1, total(2))
    swap(po, pi, 1).wait_recv()
    square_b, context_b = scale_cols(0, total(xl) + pi[...].astype(F32))
    square = square + square_b
    cs[:, :, :DD] = (context + context_b).astype(BF16).reshape(NZ, OWN, DD)
    high = square.astype(BF16)
    low = (square - high.astype(F32)).astype(BF16)
    first = lax.broadcasted_iota(jnp.int32, (128, 128), 1) < 64
    both = jnp.where(first, high.astype(F32), low.astype(F32)).astype(BF16)
    cs[:, :, DD:] = both.reshape(NZ, OWN, 128)

    def share(k, sender):
        to = lax.rem(z + k, NZ)
        return pltpu.make_async_remote_copy(
            src_ref=cs.at[to], dst_ref=cr.at[sender], send_sem=css.at[k], recv_sem=crs.at[k],
            device_id={"tensor": 2 * to + xl}, device_id_type=MESH)

    def give(n, carry):
        share(lax.rem(near_far(n) - z + NZ, NZ), z).start()
        return carry

    lax.fori_loop(0, NZ - 1, give, 0)
    deep.stage3()
    cr[z] = cs[z]
    swap(eo, ei, 0).wait_recv()
    embeds = [emb[2 * z + xl, pl.ds(4 * n, 4)].astype(F32) + er[n, 3, xl].astype(F32) + el[n, 3, xl].astype(F32)
              + ei[pl.ds(4 * n, 4)].astype(F32) for n in range(2)]
    xin[...] = jnp.concatenate(embeds, axis=0).reshape(CODEBOOKS * OWN, DD)

    def take(k, carry):
        share(k, lax.rem(z + NZ - k, NZ)).wait_recv()
        return carry

    lax.fori_loop(1, NZ, take, 0)

    def gathered(n, carry):
        context, square = carry
        v = cr[n]
        hl = v[:, DD:].astype(F32)
        return context + v[:, :DD].astype(F32), square + hl[:, :1] + hl[:, 64:65]

    context, square = lax.fori_loop(0, NZ, gathered, (jnp.zeros((OWN, DD), F32), jnp.zeros((OWN, 1), F32)), unroll=8)
    context = context * lax.rsqrt(square / D + epsilon)

    def ring(n, way, s, block):
        view = fin.at[pl.ds(2 * n, 2), block]
        return pltpu.make_async_remote_copy(
            src_ref=view, dst_ref=view, send_sem=fss.at[n, 4 * way + s], recv_sem=frs.at[n, 4 * way + s],
            device_id={"tensor": p.zdown if way else p.zup}, device_id_type=MESH)

    rows = CODEBOOKS * OWN
    x = (context[None] + xin[...].reshape(CODEBOOKS, OWN, DD)).reshape(rows, DD)
    dn = (x * lax.rsqrt(jnp.mean(x * x, axis=-1, keepdims=True) + epsilon) * dgain[...]).astype(BF16)
    deep.stage4()

    def dproject(i, carry):
        proj[i] = dot(dn, wq[i]).astype(BF16)
        return carry

    lax.fori_loop(0, 3, dproject, 0, unroll=3)

    rq = lax.rem(lax.broadcasted_iota(jnp.int32, (2 * rows, rows), 0), rows)
    rk = lax.broadcasted_iota(jnp.int32, (2 * rows, rows), 1)
    seen = (lax.rem(rq, OWN) == lax.rem(rk, OWN)) & (rq >= rk)
    low_half = lax.broadcasted_iota(jnp.int32, (rows, 128), 1) < DHEAD_DIM

    def dattend(j, carry):
        cols = pl.ds(pl.multiple_of(j * 128, 128), 128)
        q, k, v = proj[0, :, cols], proj[1, :, cols], proj[2, :, cols]
        both = jnp.concatenate([jnp.where(low_half, q, jnp.zeros_like(q)), jnp.where(low_half, jnp.zeros_like(q), q)], axis=0)
        scores = dot_t(both, k) * DHEAD_DIM ** (-0.5)
        e = jnp.where(seen, jnp.exp(jnp.where(seen, scores, 0.0)), 0.0)
        w = (e / jnp.sum(e, axis=-1, keepdims=True)).astype(BF16)
        outs = dot(w, v)
        datt[:, cols] = jnp.where(low_half, outs[:rows], outs[rows:]).astype(BF16)
        return carry

    lax.fori_loop(0, DHEADS // 2, dattend, 0, unroll=8)
    loads[8].wait()
    out = x + dot(datt[...], wm[...])
    final = (out * lax.rsqrt(jnp.mean(out * out, axis=-1, keepdims=True) + epsilon) * fgain[...]).astype(BF16)
    fin[:, z] = final.reshape(CODEBOOKS, OWN, DD)

    for n in range(4):
        for way in range(2):
            ring(n, way, 0, z).start()

    head_x_in = pltpu.make_async_remote_copy(
        src_ref=hx.at[head_part], dst_ref=hx.at[head_part], send_sem=hss.at[1],
        recv_sem=hrs.at[0], device_id={"dp": p.cpeer}, device_id_type=MESH)
    head_c = pltpu.make_async_remote_copy(
        src_ref=hx.at[head_part], dst_ref=hx.at[head_part], send_sem=hss.at[1],
        recv_sem=hrs.at[1], device_id={"dp": p.cpeer}, device_id_type=MESH)
    head_c_in = pltpu.make_async_remote_copy(
        src_ref=hx.at[head_rest], dst_ref=hx.at[head_rest], send_sem=hss.at[1],
        recv_sem=hrs.at[1], device_id={"dp": p.cpeer}, device_id_type=MESH)
    placed = [pltpu.make_async_copy(hx.at[some], wh.at[some, :, sib_lanes], lsem.at[11 + n])
              for n, some in enumerate((head_part, head_rest))]

    for s in range(1, 4):
        for n in range(4):
            for way in range(2):
                block = lax.rem(z + (s if way else NZ - s), NZ)
                ring(n, way, s - 1, block).wait_recv()
                if s < 3 or way == n % 2:
                    ring(n, way, s, block).start()
        if s == 1:
            for one in (flow(0), flow(1), flow(2), mixer, deep, erings[0], erings[1], prings[0], prings[1]):
                one.drain()
            din_x.wait_send()
            din_core(din_part).wait_send()
            swap(eo, ei, 0).wait_send()
            swap(po, pi, 1).wait_send()

            def sent(k, carry):
                cross(k).wait_send()
                return carry

            def sent_far(k, carry):
                share(k, z).wait_send()
                return carry

            lax.fori_loop(0, NZ, sent, 0)
            lax.fori_loop(1, NZ, sent_far, 0)
        if s == 2:
            head_x_in.wait_recv()
            head_c.start()
            placed[0].start()
        if s == 3:
            head_c_in.wait_recv()
            placed[1].start()

    loads[9].wait()
    placed[0].wait()
    placed[1].wait()
    shared = OWN * NZ
    lanes = lax.broadcasted_iota(jnp.int32, (shared, 256), 1).astype(F32)
    spots = lax.broadcasted_iota(jnp.int32, (shared, 128), 1)
    goals = goal[...] - (z * 256).astype(F32)
    books = lax.broadcasted_iota(jnp.int32, goals.shape, 1)

    def book(c, total):
        logits = dot(fin[c].reshape(shared, DD), wh[c])
        e = jnp.sum(jnp.exp(logits), axis=-1, keepdims=True)
        want = jnp.sum(jnp.where(books == c, goals, 0.0), axis=1, keepdims=True)
        hit = jnp.sum(jnp.where(lanes == want, logits, 0.0), axis=-1, keepdims=True)
        total = jnp.where(spots == c, e, total)
        return jnp.where(spots == CODEBOOKS + c, hit, total)

    total_sums = jnp.zeros((shared, 128), F32)
    for h in range(2):
        for n in range(2 * h, 2 * h + 2):
            ring(n, n % 2, 3, lax.rem(z + 4, NZ)).wait_recv()
        total_sums = lax.fori_loop(4 * h, 4 * h + 4, book, total_sums, unroll=4)
    sums[...] = total_sums.reshape(NZ, OWN, 128)

    def reply(k, sender):
        to = lax.rem(z + k, NZ)
        return pltpu.make_async_remote_copy(
            src_ref=sums.at[to], dst_ref=got.at[sender], send_sem=tss.at[k], recv_sem=trs.at[k],
            device_id={"tensor": 2 * to + xl}, device_id_type=MESH)

    def start_reply(k, carry):
        reply(k, z).start()
        return carry

    def take_reply(k, carry):
        reply(k, lax.rem(z + NZ - k, NZ)).wait_recv()
        return carry

    lax.fori_loop(1, NZ, start_reply, 0)
    got[z] = sums[z]
    lax.fori_loop(1, NZ, take_reply, 0)
    both = got[0]
    for n in range(1, NZ):
        both = both + got[n]
    loss[...] = jnp.log(both[:, :CODEBOOKS]) - both[:, CODEBOOKS:2 * CODEBOOKS]

    head_x.wait_send()
    head_c.wait_send()

    def reply_sent(k, carry):
        reply(k, z).wait_send()
        return carry

    lax.fori_loop(1, NZ, reply_sent, 0)
    for n in range(4):
        for way in range(2):
            for s in range(4 if way == n % 2 else 3):
                ring(n, way, s, z).wait_send()


def shards(hidden_in, attn_gain, qkv_weight, mix_weight, out_gain, depth_in_weight, text_table, code_tables,
           depth_gain, depth_qkv, depth_mix, final_gain, heads_weight, text_ids, codes):
    half = HEAD_DIM // 2
    angles = np.arange(FRAMES)[:, None] * 10000.0 ** (-np.arange(half) / half)[None, :]
    cosv = np.concatenate([np.cos(angles)] * 2, axis=1).astype(np.float32)
    sinv = np.concatenate([-np.sin(angles), np.sin(angles)], axis=1).astype(np.float32)
    vmem = pl.BlockSpec(memory_space=pltpu.VMEM)
    anym = pl.BlockSpec(memory_space=pl.ANY)
    dma = pltpu.SemaphoreType.DMA
    b16 = lambda *shape: pltpu.VMEM(shape, BF16)
    f32 = lambda *shape: pltpu.VMEM(shape, F32)
    wide = DD + 128
    return pl.pallas_call(
        layer,
        out_shape=jax.ShapeDtypeStruct((OWN, CODEBOOKS), F32),
        in_specs=[vmem] * 8 + [anym] * 9,
        out_specs=vmem,
        scratch_shapes=[
            b16(FRAMES, D), b16(*text_table.shape), b16(128, 512), b16(2, 256, DD), b16(CODEBOOKS - 1, 128, DD),
            f32(128, CODEBOOKS), f32(FRAMES, CODEBOOKS),
            b16(4, DP, 256, 256), b16(FRAMES, D), f32(3, FRAMES, 256), b16(FRAMES, 256),
            b16(NZ, 3, 128, 256),
            b16(TP, CODEBOOKS, OWN, DD),
            b16(2, 4, 2, 4, OWN, DD), b16(2, 4, 2, 4, OWN, DD),
            b16(CODEBOOKS, OWN, DD), b16(CODEBOOKS, OWN, DD),
            b16(2, 4, 3, 64, 256), b16(2, 4, 3, 64, 256), b16(128, 256), b16(128, 256),
            b16(NZ, 128, 256), b16(NZ, 128, 256),
            b16(NZ, OWN, wide), b16(NZ, OWN, wide), f32(CODEBOOKS * OWN, DD),
            b16(3, DD, DD), b16(DD, DD), b16(CODEBOOKS, DD, 256), b16(CODEBOOKS, DD, 128),
            b16(3, CODEBOOKS * OWN, DD), b16(CODEBOOKS * OWN, DD),
            b16(CODEBOOKS, NZ, OWN, DD), f32(NZ, OWN, 128), f32(NZ, OWN, 128),
            dma((13,)),
            dma((5, 16)), dma((5, 16)),
            dma((2, 8)), dma((2, 8)),
            dma((2, 8)), dma((2, 8)),
            dma((NZ,)), dma((NZ,)),
            dma((2,)), dma((2,)),
            dma((NZ,)), dma((NZ,)),
            dma((4,)), dma((4,)),
            dma((4, 8)), dma((4, 8)),
            dma((NZ,)), dma((NZ,)),
        ],
        compiler_params=pltpu.CompilerParams(
            collective_id=0, has_side_effects=True, vmem_limit_bytes=60 * 2**20),
        name="layer",
    )(attn_gain[None], out_gain[None], text_ids.reshape(2, 128), codes.T, cosv, sinv, depth_gain[None],
      final_gain[None],
      hidden_in, text_table, qkv_weight, mix_weight, depth_in_weight, code_tables, depth_qkv, depth_mix, heads_weight)


def solution(mesh):
    in_specs = (
        P("dp", None),
        P(),
        P(None, "dp", "tensor"),
        P("tensor", "dp"),
        P(),
        P("tensor", None),
        P("tensor", None),
        P(None, "tensor", None),
        P(),
        P(None, "dp", None),
        P(),
        P(),
        P(None, None, "tensor"),
        P("dp"),
        P("dp", None),
    )
    out_specs = P(("dp", "tensor"), None)
    return jax.shard_map(shards, mesh=mesh, in_specs=in_specs, out_specs=out_specs, check_vma=False)
```
